256 devices in a mesh: ord: 8 (over y, core), lat: 16 (over x, z_lo), lev: 2 (over z_hi).
Axes of the slice: x: 4, y: 4, z: 8 (z_hi: 2, z_lo: 4; z = z_hi * 4 + z_lo), core: 2. Of those that a mesh axis runs over, the one named last changes fastest.
Arguments:
- spectral_state: float32 [720, 720, 16, 7, 2], P('ord', 'lat', 'lev'), may hold values from -6 to 6
- legendre: bfloat16 [720, 720, 720], P('ord', 'lat'), may hold values from -0.21875 to 0.21875
- quad_weight: float32 [720], P('lat'), may hold values from 0.5 to 2
- weight_in: bfloat16 [112, 256], replicated, may hold values from -0.5 to 0.5
- bias_in: float32 [256], replicated, may hold values from -3 to 3
- weight_hidden: bfloat16 [4, 256, 256], replicated, may hold values from -0.375 to 0.375
- weight_out: bfloat16 [256, 112], replicated, may hold values from -0.375 to 0.375
Outputs:
- new_state: float32 [720, 720, 16, 7, 2], P('ord', 'lat', 'lev')
The draws below stay inside these ranges and needn't reach their ends.
All inputs are finite; a program needn't handle non-finite values.
Results may differ from the reference program's by a relative error of at most 0.017.
Values may be sent and summed in bfloat16 or wider, within the bound.
No kernel may reach another device: no remote copies, remote signals or barrier semaphores. Data moves between devices by JAX's collectives and lax.ppermute only.
A program may use at most 128 MiB of HBM per device.

```python
import math
import jax
import jax.numpy as jnp
from jax import lax

L = 720
NLAT = 720
NLON = 1440
FIELDS = 7
LEVELS = 16
HID = 256
LAYERS = 4
N_LAT = 16


def block_scale(key, dims, cuts, low, top_value):
    gain = 1.0
    for axis_at, blocks in cuts:
        heights = jax.random.uniform(jax.random.fold_in(jax.random.fold_in(key, 6), axis_at), (blocks,), jnp.float32, low / len(cuts), top_value / len(cuts))
        gain = gain * jnp.repeat(jnp.exp(heights), dims[axis_at] // blocks).reshape((-1,) + (1,) * (len(dims) - 1 - axis_at))
    return gain


def normal_values(rng, dims, spread, most, cuts=(), held_as=jnp.bfloat16):
    result = spread * jax.random.normal(rng, dims, jnp.float32)
    if cuts:
        result = result * block_scale(rng, dims, cuts, -0.22, 0.18)
    return jnp.clip(result, -most, most).astype(held_as)


def setup_inputs(seed: int = 0) -> dict:
    key_of = jax.random.split(jax.random.key(seed), 8)
    spectral_state = normal_values(key_of[0], (L, L, LEVELS, FIELDS, 2), 1.0, 6.0, ((0, 8), (1, 16), (2, 2)), jnp.float32)
    legendre = normal_values(key_of[1], (L, L, NLAT), L ** -0.5, 0.21875, ((0, 8), (1, 16)))
    quad_weight = jnp.clip(jnp.exp(math.log(2.0) - 1.3862944 * jax.random.uniform(key_of[2], (NLAT,), jnp.float32) ** block_scale(key_of[2], (NLAT,), ((0, 16),), -0.2, 0.2)), 0.5, 2.0)
    weight_in = normal_values(key_of[3], (LEVELS * FIELDS, HID), (LEVELS * FIELDS) ** -0.5, 0.5)
    bias_in = normal_values(key_of[4], (HID,), 0.5, 3.0, (), jnp.float32)
    weight_hidden = normal_values(key_of[5], (LAYERS, HID, HID), HID ** -0.5, 0.375)
    weight_out = normal_values(key_of[6], (HID, LEVELS * FIELDS), HID ** -0.5, 0.375)
    return {"spectral_state": spectral_state, "legendre": legendre, "quad_weight": quad_weight, "weight_in": weight_in, "bias_in": bias_in, "weight_hidden": weight_hidden, "weight_out": weight_out}


time_step = 1.0
hyper_rate = 2.0

def fourier_lookup(order_ids, lon_ids):
    phase_index = order_ids[:, None] * lon_ids[None, :] % NLON
    angles = 2.0 * math.pi / NLON * phase_index.astype(jnp.float32)
    return jnp.stack([jnp.cos(angles), -jnp.sin(angles)], axis=1).astype(jnp.bfloat16)

def column_network(features, weight_in, bias_in, weight_hidden, weight_out):
    hidden = jax.nn.silu(jnp.dot(features, weight_in, preferred_element_type=jnp.float32) + bias_in).astype(jnp.bfloat16)
    for layer_index in range(weight_hidden.shape[0]):
        update = jax.nn.silu(jnp.dot(hidden, weight_hidden[layer_index], preferred_element_type=jnp.float32))
        hidden = (hidden.astype(jnp.float32) + update).astype(jnp.bfloat16)
    return jnp.dot(hidden, weight_out, preferred_element_type=jnp.float32).astype(jnp.bfloat16)

def reference(spectral_state, legendre, quad_weight, weight_in, bias_in, weight_hidden, weight_out):
    feature_count = LEVELS * FIELDS
    channel_count = 2 * feature_count
    block_size = L // N_LAT
    order_ids = lax.iota(jnp.int32, L)
    keep_mask = (order_ids[None, :] >= order_ids[:, None]).astype(jnp.float32)
    coefficients = (spectral_state * keep_mask[:, :, None, None, None]).reshape(L, L, channel_count).astype(jnp.bfloat16)

    def inverse_order(operands):
        lookup_rows, block_rows = operands
        lookup_blocks = lookup_rows.reshape(N_LAT, block_size, NLAT).astype(jnp.float32)
        coef_blocks = block_rows.reshape(N_LAT, block_size, channel_count).astype(jnp.float32)
        partial_value = jnp.einsum('blj,blc->bjc', lookup_blocks, coef_blocks).astype(jnp.bfloat16)
        return lax.optimization_barrier(jnp.sum(partial_value.astype(jnp.float32), axis=0)).astype(jnp.bfloat16)
    fourier = lax.map(inverse_order, (legendre, coefficients)).reshape(L, NLAT, feature_count, 2)
    lookup = fourier_lookup(order_ids, lax.iota(jnp.int32, NLON))
    transform_scale = math.sqrt(2.0 / NLON)
    raw_grid = jnp.einsum('mjrp,mpx->xjr', fourier.astype(jnp.float32), lookup.astype(jnp.float32))
    grid_values = (transform_scale * raw_grid).astype(jnp.bfloat16)

    def column_block(features):
        return column_network(features, weight_in, bias_in, weight_hidden, weight_out)
    tendency = lax.map(column_block, grid_values)
    spectral_sums = jnp.einsum('xjr,mpx->mjrp', tendency.astype(jnp.float32), lookup.astype(jnp.float32))
    weighted = (transform_scale * quad_weight[None, :, None, None] * spectral_sums).astype(jnp.bfloat16)
    weighted = weighted.reshape(L, NLAT, channel_count)

    def forward_order(operands):
        lookup_rows, block_rows = operands
        return jnp.dot(lookup_rows, block_rows, preferred_element_type=jnp.float32)
    forcing = lax.map(forward_order, (legendre, weighted)).reshape(spectral_state.shape)
    degree_ratio = (order_ids * (order_ids + 1)).astype(jnp.float32) / ((L - 1) * L)
    damping = 1.0 / (1.0 + hyper_rate * degree_ratio * degree_ratio)
    updated = keep_mask[:, :, None, None, None] * (spectral_state + time_step * forcing) * damping[None, :, None, None, None]
    return updated
```

```python
import functools
import math

import jax
import jax.numpy as jnp
from jax import lax
from jax.experimental import pallas as pl
from jax.experimental.pallas import tpu as pltpu
from jax.sharding import PartitionSpec as P

L = 720
NLON = 1440
OWN = 3

time_step = 1.0
hyper_rate = 2.0
transform_scale = math.sqrt(2.0 / NLON)


def lookup_of(order_ids, valid):
    phase_index = order_ids[:, None] * lax.iota(jnp.int32, NLON)[None, :] % NLON
    angles = 2.0 * math.pi / NLON * phase_index.astype(jnp.float32)
    keep = valid[:, None]
    return jnp.stack(
        [jnp.where(keep, jnp.cos(angles), 0.0), jnp.where(keep, -jnp.sin(angles), 0.0)]
    ).astype(jnp.bfloat16)


def silu(v):
    return 0.5 * v * (1.0 + jnp.tanh(0.5 * v))


def column_kernel(
    weight_ref, fourier_ref, to_grid_ref, to_orders_ref, w_in_ref, bias_ref, w_hid_ref, w_out_ref,
    out_ref, tendency_ref, *, x_rows, m_rows,
):
    dot = functools.partial(jnp.dot, preferred_element_type=jnp.float32)

    def grid_rows(step, carry):
        rows = pl.ds(pl.multiple_of(step * x_rows, x_rows), x_rows)
        raw = dot(to_grid_ref[0, rows, :], fourier_ref[0, 0]) + dot(
            to_grid_ref[1, rows, :], fourier_ref[0, 1]
        )
        features = (transform_scale * raw).astype(jnp.bfloat16)
        hidden = silu(dot(features, w_in_ref[...]) + bias_ref[...]).astype(jnp.bfloat16)
        for layer in range(w_hid_ref.shape[0]):
            update = silu(dot(hidden, w_hid_ref[layer]))
            hidden = (hidden.astype(jnp.float32) + update).astype(jnp.bfloat16)
        tendency_ref[rows, :] = dot(hidden, w_out_ref[...]).astype(jnp.bfloat16)
        return carry

    lax.fori_loop(0, NLON // x_rows, grid_rows, 0)
    weight = weight_ref[pl.program_id(0)] * transform_scale

    def order_rows(step, carry):
        rows = pl.ds(pl.multiple_of(step * m_rows, m_rows), m_rows)
        for part in range(2):
            sums = dot(to_orders_ref[part, rows, :], tendency_ref[...])
            out_ref[0, part, rows, :] = (weight * sums).astype(jnp.bfloat16)
        return carry

    lax.fori_loop(0, out_ref.shape[2] // m_rows, order_rows, 0)


def columns(weights, fourier, to_grid, to_orders, w_in, bias, w_hid, w_out):
    lats, parts, orders, rows = fourier.shape
    whole = lambda a: pl.BlockSpec(a.shape, lambda i: (0,) * a.ndim)
    mine = pl.BlockSpec((1, parts, orders, rows), lambda i: (i, 0, 0, 0))
    return pl.pallas_call(
        functools.partial(column_kernel, x_rows=288, m_rows=256),
        grid=(lats,),
        in_specs=[pl.BlockSpec(memory_space=pltpu.SMEM), mine]
        + [whole(a) for a in (to_grid, to_orders, w_in, bias, w_hid, w_out)],
        out_specs=mine,
        out_shape=jax.ShapeDtypeStruct(fourier.shape, jnp.bfloat16),
        scratch_shapes=[pltpu.VMEM((NLON, rows), jnp.bfloat16)],
        compiler_params=pltpu.CompilerParams(vmem_limit_bytes=48 * 2**20),
        name="columns",
    )(weights, fourier, to_grid, to_orders, w_in, bias, w_hid, w_out)


def on_device(spectral_state, legendre, quad_weight, weight_in, bias_in, weight_hidden, weight_out):
    ord_size, lat_size, lev_size = (lax.axis_size(a) for a in ("ord", "lat", "lev"))
    ord_at, lat_at, lev_at = (lax.axis_index(a) for a in ("ord", "lat", "lev"))
    order_local, degree_local = spectral_state.shape[:2]
    lat_local = quad_weight.shape[0]
    row_local = spectral_state.shape[2] * spectral_state.shape[3]
    channels = 2 * row_local
    slots = lat_size * OWN
    shift = order_local - slots
    everyone = ("lat", "ord", "lev")

    order_ids = ord_at * order_local + lax.iota(jnp.int32, order_local)
    degree_ids = lat_at * degree_local + lax.iota(jnp.int32, degree_local)
    keep_mask = (degree_ids[None, :] >= order_ids[:, None]).astype(jnp.float32)

    coefficients = (spectral_state * keep_mask[:, :, None, None, None]).astype(jnp.bfloat16)
    coefficients = coefficients.reshape(order_local, degree_local, row_local, 2)
    coefficients = coefficients.swapaxes(2, 3).reshape(order_local, degree_local, channels)
    sent = jnp.concatenate([coefficients[:slots], coefficients[shift:]])
    sent = sent.reshape(lev_size * lat_size, OWN, degree_local, channels)
    coefficients = lax.all_to_all(sent, ("lev", "lat"), 0, 0, tiled=True)
    coefficients = coefficients.reshape(lev_size, lat_size, OWN, degree_local, 2, row_local)
    table = lax.dynamic_slice_in_dim(legendre, lev_at * shift, slots, 0)
    table = table.reshape(lat_size, OWN, degree_local, -1)
    table = lax.all_to_all(table, "lat", 0, 0, tiled=True)

    fourier = jnp.einsum(
        "smlj,vsmlpr->jmpvr", table, coefficients, preferred_element_type=jnp.float32
    ).astype(jnp.bfloat16)
    fourier = fourier.reshape(lat_size, lat_local, OWN, 2, lev_size * row_local)
    lat_slots = ord_size * lev_size * OWN
    fourier = jnp.pad(fourier, ((0, 0), (0, lat_slots - lat_local), (0, 0), (0, 0), (0, 0)))
    fourier = fourier.reshape(-1, OWN, OWN, 2, lev_size * row_local)
    fourier = lax.all_to_all(fourier, everyone, 0, 0, tiled=True)

    slot = lax.iota(jnp.int32, lat_size * ord_size * lev_size * OWN)
    slot_own = slot % OWN
    slot_lev = slot // OWN % lev_size
    slot_ord = slot // (OWN * lev_size) % ord_size
    slot_lat = slot // (OWN * lev_size * ord_size)
    within = slot_lev * shift + slot_lat * OWN + slot_own
    valid = (within >= order_local // 2) == (slot_lev == 1)
    to_orders = lookup_of(slot_ord * order_local + within, valid)
    to_grid = to_orders.swapaxes(1, 2)
    fourier = fourier.transpose(1, 3, 0, 2, 4).reshape(OWN, 2, -1, lev_size * row_local)
    first = (ord_at * lev_size + lev_at) * OWN
    weights = lax.dynamic_slice_in_dim(jnp.pad(quad_weight, (0, lat_slots - lat_local)), first, OWN)
    weighted = columns(
        weights, fourier, to_grid, to_orders, weight_in, bias_in[None, :], weight_hidden, weight_out
    )
    weighted = weighted.reshape(OWN, 2, -1, OWN, lev_size * row_local).transpose(2, 0, 3, 1, 4)

    weighted = lax.all_to_all(weighted, everyone, 0, 0, tiled=True)
    weighted = weighted.reshape(lat_size, lat_slots, OWN, 2, lev_size, row_local)[:, :lat_local]
    weighted = weighted.reshape(-1, OWN, 2, lev_size, row_local)
    forcing = jnp.einsum(
        "smlj,jmpvr->vsmlpr", table, weighted, preferred_element_type=jnp.float32
    ).astype(jnp.bfloat16)
    forcing = forcing.reshape(lev_size * lat_size, OWN, degree_local, channels)
    forcing = lax.all_to_all(forcing, ("lev", "lat"), 0, 0, tiled=True)
    forcing = forcing.reshape(lev_size, slots, degree_local, 2, row_local)
    half = order_local // 2
    forcing = jnp.concatenate([forcing[0, :half], forcing[1, half - shift :]])
    forcing = forcing.swapaxes(2, 3).astype(jnp.float32)

    degree_ratio = (degree_ids * (degree_ids + 1)).astype(jnp.float32) / ((L - 1) * L)
    damping = 1.0 / (1.0 + hyper_rate * degree_ratio * degree_ratio)
    return (
        keep_mask[:, :, None, None, None]
        * (spectral_state + time_step * forcing.reshape(spectral_state.shape))
        * damping[None, :, None, None, None]
    )


def solution(mesh):
    return jax.shard_map(
        on_device,
        mesh=mesh,
        in_specs=(
            P("ord", "lat", "lev", None, None),
            P("ord", "lat", None),
            P("lat"),
            P(),
            P(),
            P(),
            P(),
        ),
        out_specs=P("ord", "lat", "lev", None, None),
        check_vma=False,
    )
```

```python
import functools
import math

import jax
import jax.numpy as jnp
import numpy as np
from jax import lax
from jax.experimental import pallas as pl
from jax.experimental.pallas import tpu as pltpu
from jax.sharding import PartitionSpec as P

L = 720
NLON = 1440
OWN = 3
LANES = 128
SPARE = 14

time_step = 1.0
hyper_rate = 2.0
transform_scale = math.sqrt(2.0 / NLON)

f32, bf16 = jnp.float32, jnp.bfloat16
dot = functools.partial(jnp.dot, preferred_element_type=jnp.float32)


def lookup_of(order_ids, valid):
    phase_index = order_ids[:, None] * lax.iota(jnp.int32, NLON)[None, :] % NLON
    angles = 2.0 * math.pi / NLON * phase_index.astype(f32)
    keep = valid[:, None]
    return jnp.stack(
        [jnp.where(keep, jnp.cos(angles), 0.0), jnp.where(keep, -jnp.sin(angles), 0.0)]
    ).astype(bf16)


def silu(v):
    return 0.5 * v * (1.0 + jnp.tanh(0.5 * v))


def lane_maps(levs, row_local):
    maps = np.zeros((levs, 2 * LANES, 2 * row_local), np.float32)
    for lev in range(levs):
        for row in range(row_local):
            for part in range(2):
                maps[lev, part * LANES + lev * row_local + row, 2 * row + part] = 1.0
    return jnp.asarray(maps, bf16)


def pack_rows(slab_of, out_ref, scr_ref, peers, width):
    lane = lax.broadcasted_iota(jnp.int32, (peers, LANES), 1)
    spare = (lane >= width) & (lane < width + SPARE)
    for part in range(2):
        last = slab_of(part, 2, 2)
        for k in range(8):
            moved = pltpu.roll(last, (width - SPARE * k) % LANES, 1)
            scr_ref[part, pl.ds(k, peers, 8), :] = jnp.where(
                spare, moved, slab_of(part, k // OWN, k % OWN)
            )
        out_ref[:, part * LANES : (part + 1) * LANES] = scr_ref[part].astype(bf16)


def unpack_rows(in_ref, scr_ref, put_slab, peers, width):
    lane = lax.broadcasted_iota(jnp.int32, (peers, LANES), 1)
    for part in range(2):
        scr_ref[part] = in_ref[:, part * LANES : (part + 1) * LANES].astype(f32)
        last = jnp.zeros((peers, LANES), f32)
        for k in range(8):
            slab = scr_ref[part, pl.ds(k, peers, 8), :]
            put_slab(part, k // OWN, k % OWN, slab)
            moved = pltpu.roll(slab, (SPARE * k - width) % LANES, 1)
            last = jnp.where((lane >= SPARE * k) & (lane < SPARE * (k + 1)), moved, last)
        put_slab(part, 2, 2, last)


def prep_kernel(at_ref, state_ref, out_ref, scr_ref, *, degrees):
    orders = state_ref.shape[2]
    slots = out_ref.shape[1]
    step = pl.program_id(0) * 8
    order = lax.broadcasted_iota(jnp.int32, state_ref.shape[1:], 1) + at_ref[0]
    for i in range(8):
        degree = step + i
        keep = (degree + at_ref[1] >= order) & (degree < degrees)
        scr_ref[pl.ds(i, orders, 8), :] = jnp.where(keep, state_ref[i], 0.0).T
    rows = scr_ref[...].astype(bf16).reshape(orders, 8, -1)
    out_ref[0] = rows[:slots]
    out_ref[1] = rows[orders - slots :]


def prep(at, state, slots):
    degrees, channels, orders = state.shape
    padded = -(-degrees // 8) * 8
    return pl.pallas_call(
        functools.partial(prep_kernel, degrees=degrees),
        grid=(padded // 8,),
        in_specs=[
            pl.BlockSpec(memory_space=pltpu.SMEM),
            pl.BlockSpec((8, channels, orders), lambda i: (i, 0, 0)),
        ],
        out_specs=pl.BlockSpec((2, slots, 8, channels), lambda i: (0, 0, i, 0)),
        out_shape=jax.ShapeDtypeStruct((2, slots, padded, channels), bf16),
        scratch_shapes=[pltpu.VMEM((orders * 8, channels), f32)],
        cost_estimate=pl.CostEstimate(flops=10**6, bytes_accessed=4 * 10**6, transcendentals=0),
        name="prep",
    )(at, state)


def table_kernel(at_ref, in_ref, out_ref):
    out_ref[...] = jnp.zeros_like(out_ref)
    out_ref[:, : in_ref.shape[1], : in_ref.shape[2]] = in_ref[...]


def table_part(block_at, legendre, slots):
    _, degrees, lats = legendre.shape
    padded, lanes = -(-degrees // 8) * 8, -(-lats // LANES) * LANES
    return pl.pallas_call(
        table_kernel,
        grid_spec=pltpu.PrefetchScalarGridSpec(
            num_scalar_prefetch=1,
            grid=(slots // OWN,),
            in_specs=[pl.BlockSpec((OWN, degrees, lats), lambda i, at: (at[0] + i, 0, 0))],
            out_specs=pl.BlockSpec((OWN, padded, lanes), lambda i, at: (i, 0, 0)),
        ),
        out_shape=jax.ShapeDtypeStruct((slots, padded, lanes), bf16),
        name="table",
    )(block_at, legendre)


def inverse_kernel(
    table_ref, coef_ref, maps_ref, out_ref, sums_ref, scr_ref, *, lats, lat_local, lat_slots, width
):
    m = pl.program_id(0)
    degrees = table_ref.shape[0] * table_ref.shape[1]
    table = table_ref[...].reshape(degrees, -1)
    swapped = sum(
        lax.dot_general(
            maps_ref[v],
            coef_ref[v].reshape(degrees, -1),
            (((1,), (1,)), ((), ())),
            preferred_element_type=f32,
        )
        for v in range(maps_ref.shape[0])
    ).astype(bf16)
    sums = dot(swapped, table).T
    for part in range(2):
        lanes = slice(part * LANES, (part + 1) * LANES)
        for lat in range(lats):
            sums_ref[m, part, lat * lat_slots : lat * lat_slots + lat_local, :] = sums[
                lat * lat_local : (lat + 1) * lat_local, lanes
            ]
            sums_ref[m, part, lat * lat_slots + lat_local : (lat + 1) * lat_slots, :] = jnp.zeros(
                (lat_slots - lat_local, LANES), f32
            )

    @pl.when(m == OWN - 1)
    def _():
        peers = out_ref.shape[0] // 8
        slab_of = lambda part, i, m: sums_ref[m, part, pl.ds(i, peers, OWN), :]
        pack_rows(slab_of, out_ref, scr_ref, peers, width)


def inverse(table, coef, maps, peers, lat_local, lat_slots, width):
    lats, _, padded, lanes = table.shape
    levs, channels = coef.shape[0], coef.shape[-1]
    return pl.pallas_call(
        functools.partial(
            inverse_kernel, lats=lats, lat_local=lat_local, lat_slots=lat_slots, width=width
        ),
        grid=(OWN,),
        in_specs=[
            pl.BlockSpec((lats, None, padded, lanes), lambda m: (0, m, 0, 0)),
            pl.BlockSpec((levs, lats, None, padded, channels), lambda m: (0, 0, m, 0, 0)),
            pl.BlockSpec(maps.shape, lambda m: (0, 0, 0)),
        ],
        out_specs=pl.BlockSpec((peers * 8, 2 * LANES), lambda m: (0, 0)),
        out_shape=jax.ShapeDtypeStruct((peers * 8, 2 * LANES), bf16),
        scratch_shapes=[
            pltpu.VMEM((OWN, 2, lats * lat_slots, LANES), f32),
            pltpu.VMEM((2, peers * 8, LANES), f32),
        ],
        compiler_params=pltpu.CompilerParams(vmem_limit_bytes=40 * 2**20),
        name="inverse",
    )(table, coef, maps)


def column_kernel(
    weight_ref, in_ref, to_grid_ref, to_orders_ref, w_in_ref, bias_ref, w_hid_ref, w_out_ref,
    out_ref, fourier_ref, tendency_ref, sums_ref, scr_ref, *, x_rows, width,
):
    peers = in_ref.shape[0] // 8

    def put(part, i, m, slab):
        fourier_ref[part, m * peers : (m + 1) * peers, i * LANES : (i + 1) * LANES] = slab.astype(
            bf16
        )

    unpack_rows(in_ref, scr_ref, put, peers, width)

    def grid_rows(step, carry):
        rows = pl.ds(pl.multiple_of(step * x_rows, x_rows), x_rows)
        raw = dot(to_grid_ref[0, rows, :], fourier_ref[0]) + dot(
            to_grid_ref[1, rows, :], fourier_ref[1]
        )
        features = (transform_scale * raw).astype(bf16)
        for i in range(OWN):
            lanes = slice(i * LANES, (i + 1) * LANES)
            hidden = silu(dot(features[:, lanes], w_in_ref[...]) + bias_ref[...]).astype(bf16)
            for layer in range(w_hid_ref.shape[0]):
                update = silu(dot(hidden, w_hid_ref[layer]))
                hidden = (hidden.astype(f32) + update).astype(bf16)
            tendency_ref[rows, lanes] = dot(hidden, w_out_ref[...]).astype(bf16)
        return carry

    lax.fori_loop(0, NLON // x_rows, grid_rows, 0)

    for part in range(2):

        def order_rows(m, carry):
            rows = pl.ds(pl.multiple_of(m * peers, peers), peers)
            sums = dot(to_orders_ref[part, rows, :], tendency_ref[...])
            for i in range(OWN):
                weight = weight_ref[i] * transform_scale
                sums_ref[part, i, m] = weight * sums[:, i * LANES : (i + 1) * LANES]
            return carry

        lax.fori_loop(0, OWN, order_rows, 0)

    slab_of = lambda part, i, m: sums_ref[part, i, m]
    pack_rows(slab_of, out_ref, scr_ref, peers, width)


def columns(weights, fourier, to_grid, to_orders, w_in, bias, w_hid, w_out, width):
    peers = fourier.shape[0] // 8
    vmem = pl.BlockSpec(memory_space=pltpu.VMEM)
    return pl.pallas_call(
        functools.partial(column_kernel, x_rows=240, width=width),
        in_specs=[pl.BlockSpec(memory_space=pltpu.SMEM)] + [vmem] * 7,
        out_specs=vmem,
        out_shape=jax.ShapeDtypeStruct(fourier.shape, bf16),
        scratch_shapes=[
            pltpu.VMEM((2, OWN * peers, OWN * LANES), bf16),
            pltpu.VMEM((NLON, OWN * LANES), bf16),
            pltpu.VMEM((2, OWN, OWN, peers, LANES), f32),
            pltpu.VMEM((2, peers * 8, LANES), f32),
        ],
        compiler_params=pltpu.CompilerParams(vmem_limit_bytes=48 * 2**20),
        name="columns",
    )(weights, fourier, to_grid, to_orders, w_in, bias, w_hid, w_out)


def forward_kernel(
    in_ref, table_ref, maps_ref, out_ref, sums_ref, scr_ref, *, lats, lat_local, lat_slots, width
):
    m = pl.program_id(0)
    peers = in_ref.shape[0] // 8

    @pl.when(m == 0)
    def _():
        def put(part, i, m, slab):
            sums_ref[m, part, pl.ds(i, peers, OWN), :] = slab

        unpack_rows(in_ref, scr_ref, put, peers, width)

    lanes = table_ref.shape[-1]
    weighted = jnp.concatenate(
        [
            jnp.concatenate(
                [
                    sums_ref[m, part, lat * lat_slots : lat * lat_slots + lat_local, :]
                    for lat in range(lats)
                ]
                + [jnp.zeros((lanes - lats * lat_local, LANES), f32)]
            )
            for part in range(2)
        ],
        axis=1,
    ).astype(bf16)
    degrees = table_ref.shape[0] * table_ref.shape[1]
    forcing = dot(table_ref[...].reshape(degrees, lanes), weighted).astype(bf16)
    for v in range(maps_ref.shape[0]):
        moved = dot(forcing, maps_ref[v]).astype(bf16)
        out_ref[v] = moved.reshape(out_ref.shape[1:])


def forward(weighted, table, maps, peers, lat_local, lat_slots, width):
    lats, _, padded, lanes = table.shape
    levs, _, channels = maps.shape
    return pl.pallas_call(
        functools.partial(
            forward_kernel, lats=lats, lat_local=lat_local, lat_slots=lat_slots, width=width
        ),
        grid=(OWN,),
        in_specs=[
            pl.BlockSpec(weighted.shape, lambda m: (0, 0)),
            pl.BlockSpec((lats, None, padded, lanes), lambda m: (0, m, 0, 0)),
            pl.BlockSpec(maps.shape, lambda m: (0, 0, 0)),
        ],
        out_specs=pl.BlockSpec((levs, lats, None, padded, channels), lambda m: (0, 0, m, 0, 0)),
        out_shape=jax.ShapeDtypeStruct((levs, lats, OWN, padded, channels), bf16),
        scratch_shapes=[
            pltpu.VMEM((OWN, 2, lats * lat_slots, LANES), f32),
            pltpu.VMEM((2, peers * 8, LANES), f32),
        ],
        compiler_params=pltpu.CompilerParams(vmem_limit_bytes=40 * 2**20),
        name="forward",
    )(weighted, table, maps)


def update_kernel(at_ref, state_ref, forcing_ref, out_ref, scr_ref):
    _, channels, orders = state_ref.shape
    half, slots = orders // 2, forcing_ref.shape[1]
    first = forcing_ref[0, :half].astype(f32)
    second = forcing_ref[1, slots - half :].astype(f32)
    scr_ref[: half * 8, :] = first.reshape(half * 8, channels)
    scr_ref[half * 8 :, :] = second.reshape(half * 8, channels)
    order = lax.broadcasted_iota(jnp.int32, (channels, orders), 1) + at_ref[0]
    for i in range(8):
        degree = jnp.full((channels, orders), pl.program_id(0) * 8 + i + at_ref[1], jnp.int32)
        ratio = (degree * (degree + 1)).astype(f32) / ((L - 1) * L)
        damping = 1.0 / (1.0 + hyper_rate * ratio * ratio)
        forcing = scr_ref[pl.ds(i, orders, 8), :].T
        new = (state_ref[i] + time_step * forcing) * damping
        out_ref[i] = jnp.where(degree >= order, new, 0.0)


def update(at, state, forcing):
    degrees, channels, orders = state.shape
    _, slots, padded, _ = forcing.shape
    block = pl.BlockSpec((8, channels, orders), lambda i: (i, 0, 0))
    return pl.pallas_call(
        update_kernel,
        grid=(padded // 8,),
        in_specs=[
            pl.BlockSpec(memory_space=pltpu.SMEM),
            block,
            pl.BlockSpec((2, slots, 8, channels), lambda i: (0, 0, i, 0)),
        ],
        out_specs=block,
        out_shape=jax.ShapeDtypeStruct(state.shape, f32),
        scratch_shapes=[pltpu.VMEM((orders * 8, channels), f32)],
        name="update",
    )(at, state, forcing)


def on_device(spectral_state, legendre, quad_weight, weight_in, bias_in, weight_hidden, weight_out):
    ord_size, lat_size, lev_size = (lax.axis_size(a) for a in ("ord", "lat", "lev"))
    ord_at, lat_at, lev_at = (lax.axis_index(a) for a in ("ord", "lat", "lev"))
    order_local, degree_local = spectral_state.shape[:2]
    lat_local = quad_weight.shape[0]
    row_local = spectral_state.shape[2] * spectral_state.shape[3]
    channels = 2 * row_local
    width = lev_size * row_local
    slots = lat_size * OWN
    shift = order_local - slots
    peers = ord_size * lat_size * lev_size
    lat_slots = ord_size * lev_size * OWN
    everyone = ("lat", "ord", "lev")
    at = jnp.stack([ord_at * order_local, lat_at * degree_local]).astype(jnp.int32)
    maps = lane_maps(lev_size, row_local)
    state = spectral_state.transpose(1, 2, 3, 4, 0).reshape(degree_local, channels, order_local)

    table = table_part((lev_at * (shift // OWN))[None], legendre, slots)
    table = table.reshape(lat_size, OWN, *table.shape[1:])
    table = lax.all_to_all(table, "lat", 0, 0, tiled=True)
    coefficients = prep(at, state, slots)
    coefficients = coefficients.reshape(lev_size * lat_size, OWN, -1, channels)
    coefficients, table = lax.optimization_barrier((coefficients, table))
    coefficients = lax.all_to_all(coefficients, ("lev", "lat"), 0, 0, tiled=True)
    coefficients = coefficients.reshape(lev_size, lat_size, OWN, -1, channels)

    slot = lax.iota(jnp.int32, OWN * peers)
    slot_lev = slot % lev_size
    slot_ord = slot // lev_size % ord_size
    slot_lat = slot // (lev_size * ord_size) % lat_size
    within = slot_lev * shift + slot_lat * OWN + slot // peers
    valid = (within >= order_local // 2) == (slot_lev == 1)
    to_orders = lookup_of(slot_ord * order_local + within, valid)
    to_grid = to_orders.swapaxes(1, 2)

    fourier = inverse(table, coefficients, maps, peers, lat_local, lat_slots, width)
    fourier = lax.all_to_all(fourier.reshape(peers, 8, -1), everyone, 0, 0, tiled=True)
    first = (ord_at * lev_size + lev_at) * OWN
    weights = lax.dynamic_slice_in_dim(jnp.pad(quad_weight, (0, lat_slots - lat_local)), first, OWN)
    weighted = columns(
        weights,
        fourier.reshape(peers * 8, -1),
        to_grid,
        to_orders,
        jnp.pad(weight_in, ((0, LANES - width), (0, 0))),
        bias_in[None, :],
        weight_hidden,
        jnp.pad(weight_out, ((0, 0), (0, LANES - width))),
        width,
    )

    weighted = lax.all_to_all(weighted.reshape(peers, 8, -1), everyone, 0, 0, tiled=True)
    forcing = forward(
        weighted.reshape(peers * 8, -1), table, maps, peers, lat_local, lat_slots, width
    )
    forcing = forcing.reshape(lev_size * lat_size, OWN, -1, channels)
    forcing = lax.all_to_all(forcing, ("lev", "lat"), 0, 0, tiled=True)
    forcing = forcing.reshape(lev_size, slots, -1, channels)
    updated = update(at, state, forcing)
    updated = updated.reshape(degree_local, *spectral_state.shape[2:], order_local)
    return updated.transpose(4, 0, 1, 2, 3)


def solution(mesh):
    return jax.shard_map(
        on_device,
        mesh=mesh,
        in_specs=(
            P("ord", "lat", "lev", None, None),
            P("ord", "lat", None),
            P("lat"),
            P(),
            P(),
            P(),
            P(),
        ),
        out_specs=P("ord", "lat", "lev", None, None),
        check_vma=False,
    )
```

```python
import functools
import math

import jax
import jax.numpy as jnp
import numpy as np
from jax import lax
from jax.experimental import pallas as pl
from jax.experimental.pallas import tpu as pltpu
from jax.sharding import PartitionSpec as P

L = 720
NLON = 1440
OWN = 3
LANES = 128
LAT_X, Z_LOW, Z_RING = 4, 4, 8
HALF = 384
SPARE = 14

time_step = 1.0
hyper_rate = 2.0
transform_scale = math.sqrt(2.0 / NLON)

f32, bf16 = jnp.float32, jnp.bfloat16
dot = functools.partial(jnp.dot, preferred_element_type=jnp.float32)


def first_group(x):
    return (22 * x + 1) // 3


def lookup_of(order_ids, valid):
    phase_index = order_ids[None, :] * lax.iota(jnp.int32, NLON)[:, None] % NLON
    angles = 2.0 * math.pi / NLON * phase_index.astype(f32)
    keep = valid[None, :]
    return jnp.stack(
        [jnp.where(keep, jnp.cos(angles), 0.0), jnp.where(keep, -jnp.sin(angles), 0.0)]
    ).astype(bf16)


def silu(v):
    return 0.5 * v * (1.0 + jnp.tanh(0.5 * v))


def lane_maps(levs, row_local):
    maps = np.zeros((levs, 2 * LANES, 2 * row_local), np.float32)
    for lev in range(levs):
        for row in range(row_local):
            for part in range(2):
                maps[lev, part * LANES + lev * row_local + row, 2 * row + part] = 1.0
    return jnp.asarray(maps, bf16)


def pack_rows(slab_of, out_ref, scr_ref, peers, width):
    lane = lax.broadcasted_iota(jnp.int32, (peers, LANES), 1)
    spare = (lane >= width) & (lane < width + SPARE)
    for part in range(2):
        last = slab_of(part, 2, 2)
        for k in range(8):
            moved = pltpu.roll(last, (width - SPARE * k) % LANES, 1)
            scr_ref[part, pl.ds(k, peers, 8), :] = jnp.where(
                spare, moved, slab_of(part, k // OWN, k % OWN)
            )
        out_ref[:, part * LANES : (part + 1) * LANES] = scr_ref[part].astype(bf16)


def unpack_rows(in_ref, scr_ref, put_slab, peers, width):
    lane = lax.broadcasted_iota(jnp.int32, (peers, LANES), 1)
    for part in range(2):
        scr_ref[part] = in_ref[:, part * LANES : (part + 1) * LANES].astype(f32)
        last = jnp.zeros((peers, LANES), f32)
        for k in range(8):
            slab = scr_ref[part, pl.ds(k, peers, 8), :]
            put_slab(part, k // OWN, k % OWN, slab)
            moved = pltpu.roll(slab, (SPARE * k - width) % LANES, 1)
            last = jnp.where((lane >= SPARE * k) & (lane < SPARE * (k + 1)), moved, last)
        put_slab(part, 2, 2, last)


def prep_kernel(at_ref, state_ref, out_ref, scr_ref, *, degrees):
    orders = state_ref.shape[2]
    group = out_ref.shape[1]
    step = pl.program_id(0) * 8
    order = lax.broadcasted_iota(jnp.int32, state_ref.shape[1:], 1) + at_ref[0]
    for i in range(8):
        degree = step + i
        keep = (degree + at_ref[1] >= order) & (degree < degrees)
        scr_ref[pl.ds(i, orders, 8), :] = jnp.where(keep, state_ref[i], 0.0).T
    rows = scr_ref[...].astype(bf16).reshape(orders, 8, -1)
    for x in range(LAT_X):
        first = OWN * first_group(x)
        out_ref[x] = rows[first : first + group]


def prep(at, state):
    group = OWN * Z_RING
    degrees, channels, orders = state.shape
    padded = -(-degrees // 8) * 8
    return pl.pallas_call(
        functools.partial(prep_kernel, degrees=degrees),
        grid=(padded // 8,),
        in_specs=[
            pl.BlockSpec(memory_space=pltpu.SMEM),
            pl.BlockSpec((8, channels, orders), lambda i: (i, 0, 0)),
        ],
        out_specs=pl.BlockSpec((LAT_X, group, 8, channels), lambda i: (0, 0, i, 0)),
        out_shape=jax.ShapeDtypeStruct((LAT_X, group, padded, channels), bf16),
        scratch_shapes=[pltpu.VMEM((orders * 8, channels), f32)],
        cost_estimate=pl.CostEstimate(flops=10**6, bytes_accessed=4 * 10**6, transcendentals=0),
        name="prep",
    )(at, state)


def pack_kernel(own_ref, in_ref, a_ref, *b_refs):
    degrees, lats = in_ref.shape[1:]
    half, rows = a_ref.shape[-1], a_ref.shape[-2]
    split = rows // 2
    a_ref[...] = jnp.zeros_like(a_ref)
    for ref in b_refs:
        ref[...] = jnp.zeros_like(ref)
    for k in range(3):
        mine = in_ref[pl.ds(own_ref[k], OWN)]
        a_ref[0, k, :, :degrees, :] = mine[:, :, :half]
        b_refs[k][0, :, :degrees, : lats - half] = mine[:, :, half:]
    mine = in_ref[pl.ds(own_ref[3], OWN)]
    a_ref[0, 3, :, :split, :] = mine[:, :split, :half]
    b_refs[3][0, :, :, : lats - half] = mine[:, :split, half:]
    mine = in_ref[pl.ds(own_ref[4], OWN)]
    a_ref[0, 3, :, split:degrees, :] = mine[:, split:, :half]
    b_refs[4][0, :, : degrees - split, : lats - half] = mine[:, split:, half:]


def pack_table(own, legendre, half, rows):
    _, degrees, lats = legendre.shape
    group = OWN * Z_RING
    b_shape = lambda r: jax.ShapeDtypeStruct((LAT_X, OWN, r, half), bf16)
    b_spec = lambda r: pl.BlockSpec((1, OWN, r, half), lambda x: (x, 0, 0, 0))
    b_rows = (rows, rows, rows, rows // 2, rows // 2)
    return pl.pallas_call(
        pack_kernel,
        grid=(LAT_X,),
        in_specs=[
            pl.BlockSpec(memory_space=pltpu.SMEM),
            pl.BlockSpec(
                (pl.Element(group), pl.Element(degrees), pl.Element(lats)),
                lambda x: (OWN * first_group(x), 0, 0),
            ),
        ],
        out_specs=[pl.BlockSpec((1, 4, OWN, rows, half), lambda x: (x, 0, 0, 0, 0))]
        + [b_spec(r) for r in b_rows],
        out_shape=[jax.ShapeDtypeStruct((LAT_X, 4, OWN, rows, half), bf16)]
        + [b_shape(r) for r in b_rows],
        compiler_params=pltpu.CompilerParams(vmem_limit_bytes=24 * 2**20),
        name="pack_table",
    )(own, legendre)


def inverse_kernel(
    class_ref, a_own_ref, a_left_ref, a_right_ref, a_low_ref, a_high_ref, b_ref, coef_ref, maps_ref,
    out_ref, table_ref, sums_ref, scr_ref, *, lats, lat_local, lat_slots, width,
):
    m = pl.program_id(0)
    rows, half = b_ref.shape[-2:]
    place = LAT_X * rows
    far = jnp.concatenate([a_low_ref[...], a_high_ref[...]], axis=1)
    for k, piece in enumerate((a_own_ref[:, 0], a_left_ref[...], a_right_ref[...], far)):
        table_ref[0, k * place : (k + 1) * place, :half] = piece.reshape(place, half)
        table_ref[0, k * place : (k + 1) * place, half:] = b_ref[:, k].reshape(place, half)
    swapped = 0.0
    for v in range(maps_ref.shape[0]):
        coef = jnp.concatenate(
            [coef_ref[x * Z_LOW + class_ref[k], v] for k in range(4) for x in range(LAT_X)]
        )
        swapped += lax.dot_general(
            maps_ref[v], coef, (((1,), (1,)), ((), ())), preferred_element_type=f32
        )
    sums = dot(swapped.astype(bf16), table_ref[0]).T
    for part in range(2):
        lanes = slice(part * LANES, (part + 1) * LANES)
        for lat in range(lats):
            sums_ref[m, part, lat * lat_slots : lat * lat_slots + lat_local, :] = sums[
                lat * lat_local : (lat + 1) * lat_local, lanes
            ]
            sums_ref[m, part, lat * lat_slots + lat_local : (lat + 1) * lat_slots, :] = jnp.zeros(
                (lat_slots - lat_local, LANES), f32
            )

    @pl.when(m == OWN - 1)
    def _():
        peers = out_ref.shape[0] // 8
        slab_of = lambda part, i, m: sums_ref[m, part, pl.ds(i, peers, OWN), :]
        pack_rows(slab_of, out_ref, scr_ref, peers, width)


def inverse(classes, a_own, a_near, a_far, b_all, coef, maps, peers, lat_local, lat_slots, width):
    rows, half = b_all.shape[-2:]
    lats, levs, _, _, channels = coef.shape
    size = 4 * LAT_X * rows
    near = pl.BlockSpec((LAT_X, None, rows, half), lambda m: (0, m, 0, 0))
    far = pl.BlockSpec((LAT_X, None, rows // 2, half), lambda m: (0, m, 0, 0))
    return pl.pallas_call(
        functools.partial(
            inverse_kernel, lats=lats, lat_local=lat_local, lat_slots=lat_slots, width=width
        ),
        grid=(OWN,),
        in_specs=[
            pl.BlockSpec(memory_space=pltpu.SMEM),
            pl.BlockSpec((LAT_X, 1, None, rows, half), lambda m: (0, 0, m, 0, 0)),
            near,
            near,
            far,
            far,
            pl.BlockSpec((LAT_X, 4, None, rows, half), lambda m: (0, 0, m, 0, 0)),
            pl.BlockSpec((lats, levs, None, rows, channels), lambda m: (0, 0, m, 0, 0)),
            pl.BlockSpec(maps.shape, lambda m: (0, 0, 0)),
        ],
        out_specs=[
            pl.BlockSpec((peers * 8, 2 * LANES), lambda m: (0, 0)),
            pl.BlockSpec((1, size, 2 * half), lambda m: (m, 0, 0)),
        ],
        out_shape=[
            jax.ShapeDtypeStruct((peers * 8, 2 * LANES), bf16),
            jax.ShapeDtypeStruct((OWN, size, 2 * half), bf16),
        ],
        scratch_shapes=[
            pltpu.VMEM((OWN, 2, lats * lat_slots, LANES), f32),
            pltpu.VMEM((2, peers * 8, LANES), f32),
        ],
        compiler_params=pltpu.CompilerParams(vmem_limit_bytes=40 * 2**20),
        name="inverse",
    )(classes, a_own, *a_near, *a_far, b_all, coef, maps)


def column_kernel(
    weight_ref, in_ref, to_grid_ref, w_in_ref, bias_ref, w_hid_ref, w_out_ref,
    out_ref, fourier_ref, tendency_ref, sums_ref, scr_ref, *, x_rows, width,
):
    peers = in_ref.shape[0] // 8

    def put(part, i, m, slab):
        fourier_ref[part, m * peers : (m + 1) * peers, i * LANES : (i + 1) * LANES] = slab.astype(
            bf16
        )

    unpack_rows(in_ref, scr_ref, put, peers, width)

    def grid_rows(step, carry):
        rows = pl.ds(pl.multiple_of(step * x_rows, x_rows), x_rows)
        raw = dot(to_grid_ref[0, rows, :], fourier_ref[0]) + dot(
            to_grid_ref[1, rows, :], fourier_ref[1]
        )
        features = (transform_scale * raw).astype(bf16)
        for i in range(OWN):
            lanes = slice(i * LANES, (i + 1) * LANES)
            hidden = silu(dot(features[:, lanes], w_in_ref[...]) + bias_ref[...]).astype(bf16)
            for layer in range(w_hid_ref.shape[0]):
                update = silu(dot(hidden, w_hid_ref[layer]))
                hidden = (hidden.astype(f32) + update).astype(bf16)
            tendency_ref[rows, lanes] = dot(hidden, w_out_ref[...]).astype(bf16)
        return carry

    lax.fori_loop(0, NLON // x_rows, grid_rows, 0)

    for part in range(2):
        sums = lax.dot_general(
            tendency_ref[...],
            to_grid_ref[part],
            (((0,), (0,)), ((), ())),
            preferred_element_type=f32,
        )
        for i in range(OWN):
            weight = weight_ref[i] * transform_scale
            for m in range(OWN):
                block = sums[i * LANES : (i + 1) * LANES, m * peers : (m + 1) * peers]
                sums_ref[part, i, m] = weight * block.T

    slab_of = lambda part, i, m: sums_ref[part, i, m]
    pack_rows(slab_of, out_ref, scr_ref, peers, width)


def columns(weights, fourier, to_grid, w_in, bias, w_hid, w_out, width):
    peers = fourier.shape[0] // 8
    vmem = pl.BlockSpec(memory_space=pltpu.VMEM)
    return pl.pallas_call(
        functools.partial(column_kernel, x_rows=240, width=width),
        in_specs=[pl.BlockSpec(memory_space=pltpu.SMEM)] + [vmem] * 6,
        out_specs=vmem,
        out_shape=jax.ShapeDtypeStruct(fourier.shape, bf16),
        scratch_shapes=[
            pltpu.VMEM((2, OWN * peers, OWN * LANES), bf16),
            pltpu.VMEM((NLON, OWN * LANES), bf16),
            pltpu.VMEM((2, OWN, OWN, peers, LANES), f32),
            pltpu.VMEM((2, peers * 8, LANES), f32),
        ],
        compiler_params=pltpu.CompilerParams(vmem_limit_bytes=48 * 2**20),
        name="columns",
    )(weights, fourier, to_grid, w_in, bias, w_hid, w_out)


def forward_kernel(
    class_ref, in_ref, table_ref, maps_ref, out_ref, sums_ref, scr_ref,
    *, lats, lat_local, lat_slots, width,
):
    m = pl.program_id(0)
    peers = in_ref.shape[0] // 8

    @pl.when(m == 0)
    def _():
        def put(part, i, m, slab):
            sums_ref[m, part, pl.ds(i, peers, OWN), :] = slab

        unpack_rows(in_ref, scr_ref, put, peers, width)

    lanes = table_ref.shape[-1]
    weighted = jnp.concatenate(
        [
            jnp.concatenate(
                [
                    sums_ref[m, part, lat * lat_slots : lat * lat_slots + lat_local, :]
                    for lat in range(lats)
                ]
                + [jnp.zeros((lanes - lats * lat_local, LANES), f32)]
            )
            for part in range(2)
        ],
        axis=1,
    ).astype(bf16)
    forcing = dot(table_ref[0], weighted).astype(bf16)
    rows = out_ref.shape[2]
    for v in range(maps_ref.shape[0]):
        moved = dot(forcing, maps_ref[v]).astype(bf16)
        for k in range(4):
            for x in range(LAT_X):
                at = (k * LAT_X + x) * rows
                out_ref[x * Z_LOW + class_ref[k], v] = moved[at : at + rows]


def forward(classes, weighted, table, maps, peers, lats, rows, lat_local, lat_slots, width):
    levs, _, channels = maps.shape
    return pl.pallas_call(
        functools.partial(
            forward_kernel, lats=lats, lat_local=lat_local, lat_slots=lat_slots, width=width
        ),
        grid=(OWN,),
        in_specs=[
            pl.BlockSpec(memory_space=pltpu.SMEM),
            pl.BlockSpec(weighted.shape, lambda m: (0, 0)),
            pl.BlockSpec((1, *table.shape[1:]), lambda m: (m, 0, 0)),
            pl.BlockSpec(maps.shape, lambda m: (0, 0, 0)),
        ],
        out_specs=pl.BlockSpec((lats, levs, None, rows, channels), lambda m: (0, 0, m, 0, 0)),
        out_shape=jax.ShapeDtypeStruct((lats, levs, OWN, rows, channels), bf16),
        scratch_shapes=[
            pltpu.VMEM((OWN, 2, lats * lat_slots, LANES), f32),
            pltpu.VMEM((2, peers * 8, LANES), f32),
        ],
        compiler_params=pltpu.CompilerParams(vmem_limit_bytes=40 * 2**20),
        name="forward",
    )(classes, weighted, table, maps)


def update_kernel(at_ref, state_ref, forcing_ref, out_ref, scr_ref):
    _, channels, orders = state_ref.shape
    for x in range(LAT_X):
        skip = OWN * (first_group(x - 1) + Z_RING - first_group(x)) if x else 0
        first = (OWN * first_group(x) + skip) * 8
        mine = forcing_ref[x, skip:].astype(f32)
        scr_ref[first : first + mine.shape[0] * 8, :] = mine.reshape(-1, channels)
    order = lax.broadcasted_iota(jnp.int32, (channels, orders), 1) + at_ref[0]
    for i in range(8):
        degree = jnp.full((channels, orders), pl.program_id(0) * 8 + i + at_ref[1], jnp.int32)
        ratio = (degree * (degree + 1)).astype(f32) / ((L - 1) * L)
        damping = 1.0 / (1.0 + hyper_rate * ratio * ratio)
        forcing = scr_ref[pl.ds(i, orders, 8), :].T
        new = (state_ref[i] + time_step * forcing) * damping
        out_ref[i] = jnp.where(degree >= order, new, 0.0)


def update(at, state, forcing):
    degrees, channels, orders = state.shape
    _, group, padded, _ = forcing.shape
    block = pl.BlockSpec((8, channels, orders), lambda i: (i, 0, 0))
    return pl.pallas_call(
        update_kernel,
        grid=(padded // 8,),
        in_specs=[
            pl.BlockSpec(memory_space=pltpu.SMEM),
            block,
            pl.BlockSpec((LAT_X, group, 8, channels), lambda i: (0, 0, i, 0)),
        ],
        out_specs=block,
        out_shape=jax.ShapeDtypeStruct(state.shape, f32),
        scratch_shapes=[pltpu.VMEM((orders * 8, channels), f32)],
        name="update",
    )(at, state, forcing)


def along_z(value, step):
    pairs = []
    flat = lambda x, z: x * Z_RING + 2 * (z % Z_LOW) + z // Z_LOW
    for x in range(LAT_X):
        pairs += [(flat(x, z), flat(x, (z + step) % Z_RING)) for z in range(Z_RING)]
    return lax.ppermute(value, ("lat", "lev"), pairs)


def along_x(value):
    groups = [[x * Z_LOW + z for x in range(LAT_X)] for z in range(Z_LOW)]
    return lax.all_to_all(value, "lat", 0, 0, axis_index_groups=groups, tiled=True)


def on_device(spectral_state, legendre, quad_weight, weight_in, bias_in, weight_hidden, weight_out):
    ord_size, lat_size, lev_size = (lax.axis_size(a) for a in ("ord", "lat", "lev"))
    ord_at, lat_at, lev_at = (lax.axis_index(a) for a in ("ord", "lat", "lev"))
    order_local, degree_local = spectral_state.shape[:2]
    lat_local = quad_weight.shape[0]
    row_local = spectral_state.shape[2] * spectral_state.shape[3]
    channels = 2 * row_local
    width = lev_size * row_local
    rows = -(-degree_local // 16) * 16
    peers = ord_size * lat_size * lev_size
    lat_slots = ord_size * lev_size * OWN
    everyone = ("lat", "ord", "lev")
    at = jnp.stack([ord_at * order_local, lat_at * degree_local]).astype(jnp.int32)
    maps = lane_maps(lev_size, row_local)
    state = spectral_state.transpose(1, 2, 3, 4, 0).reshape(degree_local, channels, order_local)

    z_at = lev_at * Z_LOW + lat_at % Z_LOW
    ring = (z_at + jnp.array([0, 1, -1, 2, -2], jnp.int32)) % Z_RING
    own = OWN * (2 * (ring % Z_LOW) + ring // Z_LOW)
    a_all, b_own, *b_rest = pack_table(own, legendre, HALF, rows)
    b_left, b_right, b_low, b_high = (along_z(v, k) for v, k in zip(b_rest, (1, -1, 2, -2)))
    a_all = along_x(a_all)
    a_near = [along_z(a_all[:, 1], 1), along_z(a_all[:, 2], -1)]
    a_far = [along_z(a_all[:, 3, :, : rows // 2], 2), along_z(a_all[:, 3, :, rows // 2 :], -2)]
    b_far = jnp.concatenate([b_low, b_high], axis=2)
    b_all = along_x(jnp.stack([b_own, b_left, b_right, b_far], axis=1))

    slot = lax.iota(jnp.int32, OWN * peers)
    slot_lev = slot % lev_size
    slot_ord = slot // lev_size % ord_size
    slot_lat = slot // (lev_size * ord_size) % lat_size
    slot_x, slot_w = slot_lat // Z_LOW, 2 * (slot_lat % Z_LOW) + slot_lev
    valid = (slot_x % 2 == 0) | (slot_w > 0)
    order_ids = slot_ord * order_local + OWN * (first_group(slot_x) + slot_w) + slot // peers
    to_grid = lookup_of(order_ids, valid)
    coefficients = prep(at, state)
    coefficients, b_all, to_grid = lax.optimization_barrier((coefficients, b_all, to_grid))

    coefficients = coefficients.reshape(lat_size * lev_size, OWN, rows, channels)
    coefficients = lax.all_to_all(coefficients, ("lat", "lev"), 0, 0, tiled=True)
    coefficients = coefficients.reshape(lat_size, lev_size, OWN, rows, channels)
    classes = (z_at + jnp.array([0, -1, 1, 2], jnp.int32)) % Z_LOW
    fourier, table = inverse(
        classes, a_all, a_near, a_far, b_all, coefficients, maps, peers, lat_local, lat_slots, width
    )

    fourier = lax.all_to_all(fourier.reshape(peers, 8, -1), everyone, 0, 0, tiled=True)
    first = (ord_at * lev_size + lev_at) * OWN
    weights = lax.dynamic_slice_in_dim(jnp.pad(quad_weight, (0, lat_slots - lat_local)), first, OWN)
    weighted = columns(
        weights,
        fourier.reshape(peers * 8, -1),
        to_grid,
        jnp.pad(weight_in, ((0, LANES - width), (0, 0))),
        bias_in[None, :],
        weight_hidden,
        jnp.pad(weight_out, ((0, 0), (0, LANES - width))),
        width,
    )

    weighted = lax.all_to_all(weighted.reshape(peers, 8, -1), everyone, 0, 0, tiled=True)
    weighted = weighted.reshape(peers * 8, -1)
    forcing = forward(
        classes, weighted, table, maps, peers, lat_size, rows, lat_local, lat_slots, width
    )
    forcing = forcing.reshape(lat_size * lev_size, OWN, rows, channels)
    forcing = lax.all_to_all(forcing, ("lat", "lev"), 0, 0, tiled=True)
    forcing = forcing.reshape(LAT_X, OWN * Z_RING, rows, channels)
    updated = update(at, state, forcing)
    updated = updated.reshape(degree_local, *spectral_state.shape[2:], order_local)
    return updated.transpose(4, 0, 1, 2, 3)


def solution(mesh):
    return jax.shard_map(
        on_device,
        mesh=mesh,
        in_specs=(
            P("ord", "lat", "lev", None, None),
            P("ord", "lat", None),
            P("lat"),
            P(),
            P(),
            P(),
            P(),
        ),
        out_specs=P("ord", "lat", "lev", None, None),
        check_vma=False,
    )
```

```python
import functools
import math

import jax
import jax.numpy as jnp
import numpy as np
from jax import lax
from jax.experimental import pallas as pl
from jax.experimental.pallas import tpu as pltpu
from jax.sharding import PartitionSpec as P

L = 720
NLON = 1440
OWN = 3
LANES = 128
LAT_X, Z_LOW, Z_RING = 4, 4, 8
HALF = 384
SPARE = 14

time_step = 1.0
hyper_rate = 2.0
transform_scale = math.sqrt(2.0 / NLON)

f32, bf16 = jnp.float32, jnp.bfloat16
dot = functools.partial(jnp.dot, preferred_element_type=jnp.float32)


def first_group(x):
    return (22 * x + 1) // 3


def lookup_of(order_ids, valid):
    phase_index = order_ids[None, :] * lax.iota(jnp.int32, NLON)[:, None] % NLON
    angles = 2.0 * math.pi / NLON * phase_index.astype(f32)
    keep = valid[None, :]
    return jnp.stack(
        [jnp.where(keep, jnp.cos(angles), 0.0), jnp.where(keep, -jnp.sin(angles), 0.0)]
    ).astype(bf16)


def silu(v):
    return 0.5 * v * (1.0 + jnp.tanh(0.5 * v))


def lane_maps(levs, row_local):
    maps = np.zeros((levs, 2 * LANES, 2 * row_local), np.float32)
    for lev in range(levs):
        for row in range(row_local):
            for part in range(2):
                maps[lev, part * LANES + lev * row_local + row, 2 * row + part] = 1.0
    return jnp.asarray(maps, bf16)


def pack_rows(slab_of, out_ref, scr_ref, peers, width):
    lane = lax.broadcasted_iota(jnp.int32, (peers, LANES), 1)
    spare = (lane >= width) & (lane < width + SPARE)
    for part in range(2):
        last = slab_of(part, 2, 2)
        for k in range(8):
            moved = pltpu.roll(last, (width - SPARE * k) % LANES, 1)
            scr_ref[part, pl.ds(k, peers, 8), :] = jnp.where(
                spare, moved, slab_of(part, k // OWN, k % OWN)
            )
        out_ref[:, part * LANES : (part + 1) * LANES] = scr_ref[part].astype(bf16)


def unpack_rows(in_ref, scr_ref, put_slab, peers, width):
    lane = lax.broadcasted_iota(jnp.int32, (peers, LANES), 1)
    for part in range(2):
        scr_ref[part] = in_ref[:, part * LANES : (part + 1) * LANES].astype(f32)
        last = jnp.zeros((peers, LANES), f32)
        for k in range(8):
            slab = scr_ref[part, pl.ds(k, peers, 8), :]
            put_slab(part, k // OWN, k % OWN, slab)
            moved = pltpu.roll(slab, (SPARE * k - width) % LANES, 1)
            last = jnp.where((lane >= SPARE * k) & (lane < SPARE * (k + 1)), moved, last)
        put_slab(part, 2, 2, last)


def prep_kernel(at_ref, state_ref, out_ref, scr_ref, *, degrees):
    orders = state_ref.shape[2]
    group = out_ref.shape[1]
    step = pl.program_id(0) * 8
    order = lax.broadcasted_iota(jnp.int32, state_ref.shape[1:], 1) + at_ref[0]
    for i in range(8):
        degree = step + i
        keep = (degree + at_ref[1] >= order) & (degree < degrees)
        scr_ref[pl.ds(i, orders, 8), :] = jnp.where(keep, state_ref[i], 0.0).T
    rows = scr_ref[...].astype(bf16).reshape(orders, 8, -1)
    for x in range(LAT_X):
        first = OWN * first_group(x)
        out_ref[x] = rows[first : first + group]


def prep(at, state):
    group = OWN * Z_RING
    degrees, channels, orders = state.shape
    padded = -(-degrees // 8) * 8
    return pl.pallas_call(
        functools.partial(prep_kernel, degrees=degrees),
        grid=(padded // 8,),
        in_specs=[
            pl.BlockSpec(memory_space=pltpu.SMEM),
            pl.BlockSpec((8, channels, orders), lambda i: (i, 0, 0)),
        ],
        out_specs=pl.BlockSpec((LAT_X, group, 8, channels), lambda i: (0, 0, i, 0)),
        out_shape=jax.ShapeDtypeStruct((LAT_X, group, padded, channels), bf16),
        scratch_shapes=[pltpu.VMEM((orders * 8, channels), f32)],
        cost_estimate=pl.CostEstimate(flops=10**6, bytes_accessed=4 * 10**6, transcendentals=0),
        name="prep",
    )(at, state)


def pack_kernel(own_ref, in_ref, a_ref, *b_refs):
    degrees, lats = in_ref.shape[1:]
    half, rows = a_ref.shape[-1], a_ref.shape[-2]
    split = rows // 2
    a_ref[...] = jnp.zeros_like(a_ref)
    for ref in b_refs:
        ref[...] = jnp.zeros_like(ref)
    for k in range(3):
        mine = in_ref[pl.ds(own_ref[k], OWN)]
        a_ref[0, k, :, :degrees, :] = mine[:, :, :half]
        b_refs[k][0, :, :degrees, : lats - half] = mine[:, :, half:]
    mine = in_ref[pl.ds(own_ref[3], OWN)]
    a_ref[0, 3, :, :split, :] = mine[:, :split, :half]
    b_refs[3][0, :, :, : lats - half] = mine[:, :split, half:]
    mine = in_ref[pl.ds(own_ref[4], OWN)]
    a_ref[0, 3, :, split:degrees, :] = mine[:, split:, :half]
    b_refs[4][0, :, : degrees - split, : lats - half] = mine[:, split:, half:]


def pack_table(own, legendre, half, rows):
    _, degrees, lats = legendre.shape
    group = OWN * Z_RING
    b_shape = lambda r: jax.ShapeDtypeStruct((LAT_X, OWN, r, half), bf16)
    b_spec = lambda r: pl.BlockSpec((1, OWN, r, half), lambda x: (x, 0, 0, 0))
    b_rows = (rows, rows, rows, rows // 2, rows // 2)
    return pl.pallas_call(
        pack_kernel,
        grid=(LAT_X,),
        in_specs=[
            pl.BlockSpec(memory_space=pltpu.SMEM),
            pl.BlockSpec(
                (pl.Element(group), pl.Element(degrees), pl.Element(lats)),
                lambda x: (OWN * first_group(x), 0, 0),
            ),
        ],
        out_specs=[pl.BlockSpec((1, 4, OWN, rows, half), lambda x: (x, 0, 0, 0, 0))]
        + [b_spec(r) for r in b_rows],
        out_shape=[jax.ShapeDtypeStruct((LAT_X, 4, OWN, rows, half), bf16)]
        + [b_shape(r) for r in b_rows],
        compiler_params=pltpu.CompilerParams(vmem_limit_bytes=16 * 2**20),
        name="pack_table",
    )(own, legendre)


def inverse_kernel(
    class_ref, a_own_ref, a_left_ref, a_right_ref, a_low_ref, a_high_ref, b_ref, coef_ref, maps_ref,
    out_ref, table_ref, sums_ref, scr_ref, *, lats, lat_local, lat_slots, width,
):
    m = pl.program_id(0)
    rows, half = b_ref.shape[-2:]
    place = LAT_X * rows
    far = jnp.concatenate([a_low_ref[...], a_high_ref[...]], axis=1)
    for k, piece in enumerate((a_own_ref[:, 0], a_left_ref[...], a_right_ref[...], far)):
        table_ref[0, k * place : (k + 1) * place, :half] = piece.reshape(place, half)
        table_ref[0, k * place : (k + 1) * place, half:] = b_ref[:, k].reshape(place, half)
    swapped = 0.0
    for v in range(maps_ref.shape[0]):
        coef = jnp.concatenate(
            [coef_ref[x * Z_LOW + class_ref[k], v] for k in range(4) for x in range(LAT_X)]
        )
        swapped += lax.dot_general(
            maps_ref[v], coef, (((1,), (1,)), ((), ())), preferred_element_type=f32
        )
    sums = dot(swapped.astype(bf16), table_ref[0]).T
    for part in range(2):
        lanes = slice(part * LANES, (part + 1) * LANES)
        for lat in range(lats):
            sums_ref[m, part, lat * lat_slots : lat * lat_slots + lat_local, :] = sums[
                lat * lat_local : (lat + 1) * lat_local, lanes
            ]
            sums_ref[m, part, lat * lat_slots + lat_local : (lat + 1) * lat_slots, :] = jnp.zeros(
                (lat_slots - lat_local, LANES), f32
            )

    @pl.when(m == OWN - 1)
    def _():
        peers = out_ref.shape[0] // 8
        slab_of = lambda part, i, m: sums_ref[m, part, pl.ds(i, peers, OWN), :]
        pack_rows(slab_of, out_ref, scr_ref, peers, width)


def inverse(classes, a_own, a_near, a_far, b_all, coef, maps, peers, lat_local, lat_slots, width):
    rows, half = b_all.shape[-2:]
    lats, levs, _, _, channels = coef.shape
    size = 4 * LAT_X * rows
    near = pl.BlockSpec((LAT_X, None, rows, half), lambda m: (0, m, 0, 0))
    far = pl.BlockSpec((LAT_X, None, rows // 2, half), lambda m: (0, m, 0, 0))
    return pl.pallas_call(
        functools.partial(
            inverse_kernel, lats=lats, lat_local=lat_local, lat_slots=lat_slots, width=width
        ),
        grid=(OWN,),
        in_specs=[
            pl.BlockSpec(memory_space=pltpu.SMEM),
            pl.BlockSpec((LAT_X, 1, None, rows, half), lambda m: (0, 0, m, 0, 0)),
            near,
            near,
            far,
            far,
            pl.BlockSpec((LAT_X, 4, None, rows, half), lambda m: (0, 0, m, 0, 0)),
            pl.BlockSpec((lats, levs, None, rows, channels), lambda m: (0, 0, m, 0, 0)),
            pl.BlockSpec(maps.shape, lambda m: (0, 0, 0)),
        ],
        out_specs=[
            pl.BlockSpec((peers * 8, 2 * LANES), lambda m: (0, 0)),
            pl.BlockSpec((1, size, 2 * half), lambda m: (m, 0, 0)),
        ],
        out_shape=[
            jax.ShapeDtypeStruct((peers * 8, 2 * LANES), bf16),
            jax.ShapeDtypeStruct((OWN, size, 2 * half), bf16),
        ],
        scratch_shapes=[
            pltpu.VMEM((OWN, 2, lats * lat_slots, LANES), f32),
            pltpu.VMEM((2, peers * 8, LANES), f32),
        ],
        compiler_params=pltpu.CompilerParams(vmem_limit_bytes=20 * 2**20),
        name="inverse",
    )(classes, a_own, *a_near, *a_far, b_all, coef, maps)


def column_kernel(
    weight_ref, in_ref, to_grid_ref, w_in_ref, bias_ref, w_hid_ref, w_out_ref,
    out_ref, fourier_ref, tendency_ref, sums_ref, scr_ref, *, x_rows, width,
):
    peers = in_ref.shape[0] // 8

    def put(part, i, m, slab):
        fourier_ref[part, m * peers : (m + 1) * peers, i * LANES : (i + 1) * LANES] = slab.astype(
            bf16
        )

    unpack_rows(in_ref, scr_ref, put, peers, width)

    def grid_rows(step, carry):
        rows = pl.ds(pl.multiple_of(step * x_rows, x_rows), x_rows)
        raw = dot(to_grid_ref[0, rows, :], fourier_ref[0]) + dot(
            to_grid_ref[1, rows, :], fourier_ref[1]
        )
        features = (transform_scale * raw).astype(bf16)
        for i in range(OWN):
            lanes = slice(i * LANES, (i + 1) * LANES)
            hidden = silu(dot(features[:, lanes], w_in_ref[...]) + bias_ref[...]).astype(bf16)
            for layer in range(w_hid_ref.shape[0]):
                update = silu(dot(hidden, w_hid_ref[layer]))
                hidden = (hidden.astype(f32) + update).astype(bf16)
            tendency_ref[rows, lanes] = dot(hidden, w_out_ref[...]).astype(bf16)
        return carry

    lax.fori_loop(0, NLON // x_rows, grid_rows, 0)

    for part in range(2):
        sums = lax.dot_general(
            tendency_ref[...],
            to_grid_ref[part],
            (((0,), (0,)), ((), ())),
            preferred_element_type=f32,
        )
        for i in range(OWN):
            weight = weight_ref[i] * transform_scale
            for m in range(OWN):
                block = sums[i * LANES : (i + 1) * LANES, m * peers : (m + 1) * peers]
                sums_ref[part, i, m] = weight * block.T

    slab_of = lambda part, i, m: sums_ref[part, i, m]
    pack_rows(slab_of, out_ref, scr_ref, peers, width)


def columns(weights, fourier, to_grid, w_in, bias, w_hid, w_out, width):
    peers = fourier.shape[0] // 8
    vmem = pl.BlockSpec(memory_space=pltpu.VMEM)
    return pl.pallas_call(
        functools.partial(column_kernel, x_rows=240, width=width),
        in_specs=[pl.BlockSpec(memory_space=pltpu.SMEM)] + [vmem] * 6,
        out_specs=vmem,
        out_shape=jax.ShapeDtypeStruct(fourier.shape, bf16),
        scratch_shapes=[
            pltpu.VMEM((2, OWN * peers, OWN * LANES), bf16),
            pltpu.VMEM((NLON, OWN * LANES), bf16),
            pltpu.VMEM((2, OWN, OWN, peers, LANES), f32),
            pltpu.VMEM((2, peers * 8, LANES), f32),
        ],
        compiler_params=pltpu.CompilerParams(vmem_limit_bytes=28 * 2**20),
        name="columns",
    )(weights, fourier, to_grid, w_in, bias, w_hid, w_out)


def forward_kernel(
    class_ref, in_ref, table_ref, maps_ref, out_ref, sums_ref, scr_ref,
    *, lats, lat_local, lat_slots, width,
):
    m = pl.program_id(0)
    peers = in_ref.shape[0] // 8

    @pl.when(m == 0)
    def _():
        def put(part, i, m, slab):
            sums_ref[m, part, pl.ds(i, peers, OWN), :] = slab

        unpack_rows(in_ref, scr_ref, put, peers, width)

    lanes = table_ref.shape[-1]
    weighted = jnp.concatenate(
        [
            jnp.concatenate(
                [
                    sums_ref[m, part, lat * lat_slots : lat * lat_slots + lat_local, :]
                    for lat in range(lats)
                ]
                + [jnp.zeros((lanes - lats * lat_local, LANES), f32)]
            )
            for part in range(2)
        ],
        axis=1,
    ).astype(bf16)
    forcing = dot(table_ref[0], weighted).astype(bf16)
    rows = out_ref.shape[2]
    for v in range(maps_ref.shape[0]):
        moved = dot(forcing, maps_ref[v]).astype(bf16)
        for k in range(4):
            for x in range(LAT_X):
                at = (k * LAT_X + x) * rows
                out_ref[x * Z_LOW + class_ref[k], v] = moved[at : at + rows]


def forward(classes, weighted, table, maps, peers, lats, rows, lat_local, lat_slots, width):
    levs, _, channels = maps.shape
    return pl.pallas_call(
        functools.partial(
            forward_kernel, lats=lats, lat_local=lat_local, lat_slots=lat_slots, width=width
        ),
        grid=(OWN,),
        in_specs=[
            pl.BlockSpec(memory_space=pltpu.SMEM),
            pl.BlockSpec(weighted.shape, lambda m: (0, 0)),
            pl.BlockSpec((1, *table.shape[1:]), lambda m: (m, 0, 0)),
            pl.BlockSpec(maps.shape, lambda m: (0, 0, 0)),
        ],
        out_specs=pl.BlockSpec((lats, levs, None, rows, channels), lambda m: (0, 0, m, 0, 0)),
        out_shape=jax.ShapeDtypeStruct((lats, levs, OWN, rows, channels), bf16),
        scratch_shapes=[
            pltpu.VMEM((OWN, 2, lats * lat_slots, LANES), f32),
            pltpu.VMEM((2, peers * 8, LANES), f32),
        ],
        compiler_params=pltpu.CompilerParams(vmem_limit_bytes=16 * 2**20),
        name="forward",
    )(classes, weighted, table, maps)


def update_kernel(at_ref, state_ref, forcing_ref, out_ref, scr_ref):
    _, channels, orders = state_ref.shape
    for x in range(LAT_X):
        skip = OWN * (first_group(x - 1) + Z_RING - first_group(x)) if x else 0
        first = (OWN * first_group(x) + skip) * 8
        mine = forcing_ref[x, skip:].astype(f32)
        scr_ref[first : first + mine.shape[0] * 8, :] = mine.reshape(-1, channels)
    order = lax.broadcasted_iota(jnp.int32, (channels, orders), 1) + at_ref[0]
    for i in range(8):
        degree = jnp.full((channels, orders), pl.program_id(0) * 8 + i + at_ref[1], jnp.int32)
        ratio = (degree * (degree + 1)).astype(f32) / ((L - 1) * L)
        damping = 1.0 / (1.0 + hyper_rate * ratio * ratio)
        forcing = scr_ref[pl.ds(i, orders, 8), :].T
        new = (state_ref[i] + time_step * forcing) * damping
        out_ref[i] = jnp.where(degree >= order, new, 0.0)


def update(at, state, forcing):
    degrees, channels, orders = state.shape
    _, group, padded, _ = forcing.shape
    block = pl.BlockSpec((8, channels, orders), lambda i: (i, 0, 0))
    return pl.pallas_call(
        update_kernel,
        grid=(padded // 8,),
        in_specs=[
            pl.BlockSpec(memory_space=pltpu.SMEM),
            block,
            pl.BlockSpec((LAT_X, group, 8, channels), lambda i: (0, 0, i, 0)),
        ],
        out_specs=block,
        out_shape=jax.ShapeDtypeStruct(state.shape, f32),
        scratch_shapes=[pltpu.VMEM((orders * 8, channels), f32)],
        name="update",
    )(at, state, forcing)


def along_z(value, step):
    pairs = []
    flat = lambda x, z: x * Z_RING + 2 * (z % Z_LOW) + z // Z_LOW
    for x in range(LAT_X):
        pairs += [(flat(x, z), flat(x, (z + step) % Z_RING)) for z in range(Z_RING)]
    return lax.ppermute(value, ("lat", "lev"), pairs)


def along_x(value):
    groups = [[x * Z_LOW + z for x in range(LAT_X)] for z in range(Z_LOW)]
    return lax.all_to_all(value, "lat", 0, 0, axis_index_groups=groups, tiled=True)


def on_device(spectral_state, legendre, quad_weight, weight_in, bias_in, weight_hidden, weight_out):
    ord_size, lat_size, lev_size = (lax.axis_size(a) for a in ("ord", "lat", "lev"))
    ord_at, lat_at, lev_at = (lax.axis_index(a) for a in ("ord", "lat", "lev"))
    order_local, degree_local = spectral_state.shape[:2]
    lat_local = quad_weight.shape[0]
    row_local = spectral_state.shape[2] * spectral_state.shape[3]
    channels = 2 * row_local
    width = lev_size * row_local
    rows = -(-degree_local // 16) * 16
    peers = ord_size * lat_size * lev_size
    lat_slots = ord_size * lev_size * OWN
    everyone = ("lat", "ord", "lev")
    at = jnp.stack([ord_at * order_local, lat_at * degree_local]).astype(jnp.int32)
    maps = lane_maps(lev_size, row_local)
    state = spectral_state.transpose(1, 2, 3, 4, 0).reshape(degree_local, channels, order_local)

    z_at = lev_at * Z_LOW + lat_at % Z_LOW
    ring = (z_at + jnp.array([0, 1, -1, 2, -2], jnp.int32)) % Z_RING
    own = OWN * (2 * (ring % Z_LOW) + ring // Z_LOW)
    a_all, b_own, *b_rest = pack_table(own, legendre, HALF, rows)
    b_left, b_right, b_low, b_high = (along_z(v, k) for v, k in zip(b_rest, (1, -1, 2, -2)))
    a_all = along_x(a_all)
    b_far = jnp.concatenate([b_low, b_high], axis=2)
    b_all = jnp.stack([b_own, b_left, b_right, b_far], axis=1)
    a_all, b_all = lax.optimization_barrier((a_all, b_all))
    a_near = [along_z(a_all[:, 1], 1), along_z(a_all[:, 2], -1)]
    a_far = [along_z(a_all[:, 3, :, : rows // 2], 2), along_z(a_all[:, 3, :, rows // 2 :], -2)]
    b_all = along_x(b_all)

    slot = lax.iota(jnp.int32, OWN * peers)
    slot_lev = slot % lev_size
    slot_ord = slot // lev_size % ord_size
    slot_lat = slot // (lev_size * ord_size) % lat_size
    slot_x, slot_w = slot_lat // Z_LOW, 2 * (slot_lat % Z_LOW) + slot_lev
    valid = (slot_x % 2 == 0) | (slot_w > 0)
    order_ids = slot_ord * order_local + OWN * (first_group(slot_x) + slot_w) + slot // peers
    to_grid = lookup_of(order_ids, valid)
    coefficients = prep(at, state)
    coefficients, a_near, a_far, b_all, to_grid = lax.optimization_barrier(
        (coefficients, a_near, a_far, b_all, to_grid)
    )

    coefficients = coefficients.reshape(lat_size * lev_size, OWN, rows, channels)
    coefficients = lax.all_to_all(coefficients, ("lat", "lev"), 0, 0, tiled=True)
    coefficients = coefficients.reshape(lat_size, lev_size, OWN, rows, channels)
    classes = (z_at + jnp.array([0, -1, 1, 2], jnp.int32)) % Z_LOW
    fourier, table = inverse(
        classes, a_all, a_near, a_far, b_all, coefficients, maps, peers, lat_local, lat_slots, width
    )

    fourier = lax.all_to_all(fourier.reshape(peers, 8, -1), everyone, 0, 0, tiled=True)
    first = (ord_at * lev_size + lev_at) * OWN
    weights = lax.dynamic_slice_in_dim(jnp.pad(quad_weight, (0, lat_slots - lat_local)), first, OWN)
    weighted = columns(
        weights,
        fourier.reshape(peers * 8, -1),
        to_grid,
        jnp.pad(weight_in, ((0, LANES - width), (0, 0))),
        bias_in[None, :],
        weight_hidden,
        jnp.pad(weight_out, ((0, 0), (0, LANES - width))),
        width,
    )

    weighted = lax.all_to_all(weighted.reshape(peers, 8, -1), everyone, 0, 0, tiled=True)
    weighted = weighted.reshape(peers * 8, -1)
    forcing = forward(
        classes, weighted, table, maps, peers, lat_size, rows, lat_local, lat_slots, width
    )
    forcing = forcing.reshape(lat_size * lev_size, OWN, rows, channels)
    forcing = lax.all_to_all(forcing, ("lat", "lev"), 0, 0, tiled=True)
    forcing = forcing.reshape(LAT_X, OWN * Z_RING, rows, channels)
    updated = update(at, state, forcing)
    updated = updated.reshape(degree_local, *spectral_state.shape[2:], order_local)
    return updated.transpose(4, 0, 1, 2, 3)


def solution(mesh):
    return jax.shard_map(
        on_device,
        mesh=mesh,
        in_specs=(
            P("ord", "lat", "lev", None, None),
            P("ord", "lat", None),
            P("lat"),
            P(),
            P(),
            P(),
            P(),
        ),
        out_specs=P("ord", "lat", "lev", None, None),
        check_vma=False,
    )
```

```python
import functools
import math

import jax
import jax.numpy as jnp
import numpy as np
from jax import lax
from jax.experimental import pallas as pl
from jax.experimental.pallas import tpu as pltpu
from jax.sharding import PartitionSpec as P

L = 720
NLON = 1440
OWN = 3
LANES = 128
LAT_X, Z_LOW, Z_RING = 4, 4, 8
HALF = 384
SPARE = 14

time_step = 1.0
hyper_rate = 2.0
transform_scale = math.sqrt(2.0 / NLON)

f32, bf16 = jnp.float32, jnp.bfloat16
dot = functools.partial(jnp.dot, preferred_element_type=jnp.float32)


def first_group(x):
    return (22 * x + 1) // 3


def lookup_of(order_ids, valid):
    phase_index = order_ids[None, :] * lax.iota(jnp.int32, NLON)[:, None] % NLON
    angles = 2.0 * math.pi / NLON * phase_index.astype(f32)
    keep = valid[None, :]
    return jnp.stack(
        [jnp.where(keep, jnp.cos(angles), 0.0), jnp.where(keep, -jnp.sin(angles), 0.0)]
    ).astype(bf16)


def silu(v):
    return 0.5 * v * (1.0 + jnp.tanh(0.5 * v))


def lane_maps(levs, row_local):
    maps = np.zeros((levs, 2 * LANES, LANES), np.float32)
    for lev in range(levs):
        for row in range(row_local):
            for part in range(2):
                maps[lev, part * LANES + lev * row_local + row, 2 * row + part] = 1.0
    return jnp.asarray(maps, bf16)


def pack_rows(slab_of, out_ref, scr_ref, peers, width):
    lane = lax.broadcasted_iota(jnp.int32, (peers, LANES), 1)
    spare = (lane >= width) & (lane < width + SPARE)
    for part in range(2):
        last = slab_of(part, 2, 2)
        for k in range(8):
            moved = pltpu.roll(last, (width - SPARE * k) % LANES, 1)
            scr_ref[part, pl.ds(k, peers, 8), :] = jnp.where(
                spare, moved, slab_of(part, k // OWN, k % OWN)
            )
        out_ref[:, part * LANES : (part + 1) * LANES] = scr_ref[part].astype(bf16)


def unpack_rows(in_ref, scr_ref, put_slab, peers, width):
    lane = lax.broadcasted_iota(jnp.int32, (peers, LANES), 1)
    for part in range(2):
        scr_ref[part] = in_ref[:, part * LANES : (part + 1) * LANES].astype(f32)
        last = jnp.zeros((peers, LANES), f32)
        for k in range(8):
            slab = scr_ref[part, pl.ds(k, peers, 8), :]
            put_slab(part, k // OWN, k % OWN, slab)
            moved = pltpu.roll(slab, (SPARE * k - width) % LANES, 1)
            last = jnp.where((lane >= SPARE * k) & (lane < SPARE * (k + 1)), moved, last)
        put_slab(part, 2, 2, last)


def spare_lanes(shape, width):
    lane = lax.broadcasted_iota(jnp.int32, shape, len(shape) - 1)
    return (lane >= width) & (lane < width + SPARE)


def scatter_last(row, t, width):
    return pltpu.roll(row, (width - SPARE * t) % LANES, 1)


def gather_last(last, slab, t, width):
    lane = lax.broadcasted_iota(jnp.int32, slab.shape, 1)
    moved = pltpu.roll(slab, (SPARE * t - width) % LANES, 1)
    return jnp.where((lane >= SPARE * t) & (lane < SPARE * (t + 1)), moved, last)


def wide(value):
    return jnp.pad(value, ((0, 0), (0, LANES - value.shape[1])))


def prep_kernel(at_ref, state_ref, last_ref, out_ref, scr_ref):
    _, channels, orders = state_ref.shape
    group, rows = out_ref.shape[1], 8 * pl.num_programs(0)
    b = pl.program_id(0)
    order = lax.broadcasted_iota(jnp.int32, (channels, orders), 1) + at_ref[0]
    masked = lambda value, degree: wide(jnp.where(degree + at_ref[1] >= order, value, 0.0).T)
    last = masked(last_ref[b], rows + b)
    spare = spare_lanes(last.shape, channels)
    for t in range(8):
        scr_ref[pl.ds(t, orders, 8), :] = jnp.where(
            spare, scatter_last(last, t, channels), masked(state_ref[t], 8 * b + t)
        )
    packed = scr_ref[...].astype(bf16).reshape(orders, 8, LANES)
    for x in range(LAT_X):
        first = OWN * first_group(x)
        out_ref[x] = packed[first : first + group]


def prep(at, state, rows):
    group = OWN * Z_RING
    _, channels, orders = state.shape
    steps = rows // 8
    return pl.pallas_call(
        prep_kernel,
        grid=(steps,),
        in_specs=[
            pl.BlockSpec(memory_space=pltpu.SMEM),
            pl.BlockSpec((8, channels, orders), lambda i: (i, 0, 0)),
            pl.BlockSpec((8, channels, orders), lambda i: (steps, 0, 0)),
        ],
        out_specs=pl.BlockSpec((LAT_X, group, 8, LANES), lambda i: (0, 0, i, 0)),
        out_shape=jax.ShapeDtypeStruct((LAT_X, group, rows, LANES), bf16),
        scratch_shapes=[pltpu.VMEM((orders * 8, LANES), f32)],
        cost_estimate=pl.CostEstimate(flops=10**6, bytes_accessed=4 * 10**6, transcendentals=0),
        name="prep",
    )(at, state, state)


def pack_kernel(own_ref, in_ref, a_ref, *b_refs):
    degrees, lats = in_ref.shape[1:]
    half, rows = a_ref.shape[-1], a_ref.shape[-2]
    split = rows // 2
    a_ref[...] = jnp.zeros_like(a_ref)
    for ref in b_refs:
        ref[...] = jnp.zeros_like(ref)
    for k in range(3):
        mine = in_ref[pl.ds(own_ref[k], OWN)]
        a_ref[0, k, :, :degrees, :] = mine[:, :, :half]
        b_refs[k][0, :, :degrees, : lats - half] = mine[:, :, half:]
    mine = in_ref[pl.ds(own_ref[3], OWN)]
    a_ref[0, 3, :, :split, :] = mine[:, :split, :half]
    b_refs[3][0, :, :, : lats - half] = mine[:, :split, half:]
    mine = in_ref[pl.ds(own_ref[4], OWN)]
    a_ref[0, 3, :, split:degrees, :] = mine[:, split:, :half]
    b_refs[4][0, :, : degrees - split, : lats - half] = mine[:, split:, half:]


def pack_table(own, legendre, half, rows):
    _, degrees, lats = legendre.shape
    group = OWN * Z_RING
    b_shape = lambda r: jax.ShapeDtypeStruct((LAT_X, OWN, r, half), bf16)
    b_spec = lambda r: pl.BlockSpec((1, OWN, r, half), lambda x: (x, 0, 0, 0))
    b_rows = (rows, rows, rows, rows // 2, rows // 2)
    return pl.pallas_call(
        pack_kernel,
        grid=(LAT_X,),
        in_specs=[
            pl.BlockSpec(memory_space=pltpu.SMEM),
            pl.BlockSpec(
                (pl.Element(group), pl.Element(degrees), pl.Element(lats)),
                lambda x: (OWN * first_group(x), 0, 0),
            ),
        ],
        out_specs=[pl.BlockSpec((1, 4, OWN, rows, half), lambda x: (x, 0, 0, 0, 0))]
        + [b_spec(r) for r in b_rows],
        out_shape=[jax.ShapeDtypeStruct((LAT_X, 4, OWN, rows, half), bf16)]
        + [b_shape(r) for r in b_rows],
        compiler_params=pltpu.CompilerParams(vmem_limit_bytes=16 * 2**20),
        name="pack_table",
    )(own, legendre)


def assemble_kernel(a_own_ref, a_left_ref, a_right_ref, a_low_ref, a_high_ref, b_ref, out_ref):
    rows, half = b_ref.shape[-2:]
    place = LAT_X * rows
    far = jnp.concatenate([a_low_ref[...], a_high_ref[...]], axis=1)
    for k, piece in enumerate((a_own_ref[:, 0], a_left_ref[...], a_right_ref[...], far)):
        out_ref[0, k * place : (k + 1) * place, :half] = piece.reshape(place, half)
        out_ref[0, k * place : (k + 1) * place, half:] = b_ref[:, k].reshape(place, half)


def assemble(a_own, a_near, a_far, b_all):
    rows, half = b_all.shape[-2:]
    size = 4 * LAT_X * rows
    near = pl.BlockSpec((LAT_X, None, rows, half), lambda m: (0, m, 0, 0))
    far = pl.BlockSpec((LAT_X, None, rows // 2, half), lambda m: (0, m, 0, 0))
    return pl.pallas_call(
        assemble_kernel,
        grid=(OWN,),
        in_specs=[
            pl.BlockSpec((LAT_X, 1, None, rows, half), lambda m: (0, 0, m, 0, 0)),
            near,
            near,
            far,
            far,
            pl.BlockSpec((LAT_X, 4, None, rows, half), lambda m: (0, 0, m, 0, 0)),
        ],
        out_specs=pl.BlockSpec((1, size, 2 * half), lambda m: (m, 0, 0)),
        out_shape=jax.ShapeDtypeStruct((OWN, size, 2 * half), bf16),
        cost_estimate=pl.CostEstimate(flops=10**6, bytes_accessed=8 * 10**6, transcendentals=0),
        name="assemble",
    )(a_own, *a_near, *a_far, b_all)


def inverse_kernel(
    class_ref, table_ref, coef_ref, maps_ref, out_ref, sums_ref, scr_ref, sent_ref, full_ref,
    *, lats, lat_local, lat_slots, width,
):
    m = pl.program_id(0)
    sent = coef_ref.shape[2]
    rows = full_ref.shape[0] // lats
    swapped = 0.0
    for v in range(maps_ref.shape[0]):
        for q in range(lats):
            k, x = divmod(q, LAT_X)
            piece = coef_ref[x * Z_LOW + class_ref[k], v].astype(f32)
            sent_ref[q * sent : (q + 1) * sent, :] = piece
            full_ref[q * rows : q * rows + sent, :] = piece
            full_ref[q * rows + sent : (q + 1) * rows, :] = jnp.zeros((rows - sent, LANES), f32)
        for b in range(sent // 8):
            last = jnp.zeros((lats, LANES), f32)
            for t in range(8):
                slab = sent_ref[pl.ds(8 * b + t, lats, sent), :]
                last = gather_last(last, slab, t, width)
            full_ref[pl.ds(sent + b, lats, rows), :] = last
        swapped += lax.dot_general(
            maps_ref[v],
            full_ref[...].astype(bf16),
            (((1,), (1,)), ((), ())),
            preferred_element_type=f32,
        )
    sums = dot(swapped.astype(bf16), table_ref[0]).T
    for part in range(2):
        lanes = slice(part * LANES, (part + 1) * LANES)
        for lat in range(lats):
            sums_ref[m, part, lat * lat_slots : lat * lat_slots + lat_local, :] = sums[
                lat * lat_local : (lat + 1) * lat_local, lanes
            ]
            sums_ref[m, part, lat * lat_slots + lat_local : (lat + 1) * lat_slots, :] = jnp.zeros(
                (lat_slots - lat_local, LANES), f32
            )

    @pl.when(m == OWN - 1)
    def _():
        peers = out_ref.shape[0] // 8
        slab_of = lambda part, i, m: sums_ref[m, part, pl.ds(i, peers, OWN), :]
        pack_rows(slab_of, out_ref, scr_ref, peers, width)


def inverse(classes, table, coef, maps, peers, lat_local, lat_slots, width):
    lats, levs, _, sent, lanes = coef.shape
    size = table.shape[1]
    return pl.pallas_call(
        functools.partial(
            inverse_kernel, lats=lats, lat_local=lat_local, lat_slots=lat_slots, width=width
        ),
        grid=(OWN,),
        in_specs=[
            pl.BlockSpec(memory_space=pltpu.SMEM),
            pl.BlockSpec((1, *table.shape[1:]), lambda m: (m, 0, 0)),
            pl.BlockSpec((lats, levs, None, sent, lanes), lambda m: (0, 0, m, 0, 0)),
            pl.BlockSpec(maps.shape, lambda m: (0, 0, 0)),
        ],
        out_specs=pl.BlockSpec((peers * 8, 2 * LANES), lambda m: (0, 0)),
        out_shape=jax.ShapeDtypeStruct((peers * 8, 2 * LANES), bf16),
        scratch_shapes=[
            pltpu.VMEM((OWN, 2, lats * lat_slots, LANES), f32),
            pltpu.VMEM((2, peers * 8, LANES), f32),
            pltpu.VMEM((lats * sent, LANES), f32),
            pltpu.VMEM((size, LANES), f32),
        ],
        compiler_params=pltpu.CompilerParams(vmem_limit_bytes=20 * 2**20),
        name="inverse",
    )(classes, table, coef, maps)


def column_kernel(
    weight_ref, in_ref, to_grid_ref, w_in_ref, bias_ref, w_hid_ref, w_out_ref,
    out_ref, fourier_ref, tendency_ref, sums_ref, scr_ref, *, x_rows, width,
):
    peers = in_ref.shape[0] // 8

    def put(part, i, m, slab):
        fourier_ref[part, m * peers : (m + 1) * peers, i * LANES : (i + 1) * LANES] = slab.astype(
            bf16
        )

    unpack_rows(in_ref, scr_ref, put, peers, width)

    def grid_rows(step, carry):
        rows = pl.ds(pl.multiple_of(step * x_rows, x_rows), x_rows)
        raw = dot(to_grid_ref[0, rows, :], fourier_ref[0]) + dot(
            to_grid_ref[1, rows, :], fourier_ref[1]
        )
        features = (transform_scale * raw).astype(bf16)
        for i in range(OWN):
            lanes = slice(i * LANES, (i + 1) * LANES)
            hidden = silu(dot(features[:, lanes], w_in_ref[...]) + bias_ref[...]).astype(bf16)
            for layer in range(w_hid_ref.shape[0]):
                update = silu(dot(hidden, w_hid_ref[layer]))
                hidden = (hidden.astype(f32) + update).astype(bf16)
            tendency_ref[rows, lanes] = dot(hidden, w_out_ref[...]).astype(bf16)
        return carry

    lax.fori_loop(0, NLON // x_rows, grid_rows, 0)

    for part in range(2):
        sums = lax.dot_general(
            tendency_ref[...],
            to_grid_ref[part],
            (((0,), (0,)), ((), ())),
            preferred_element_type=f32,
        )
        for i in range(OWN):
            weight = weight_ref[i] * transform_scale
            for m in range(OWN):
                block = sums[i * LANES : (i + 1) * LANES, m * peers : (m + 1) * peers]
                sums_ref[part, i, m] = weight * block.T

    slab_of = lambda part, i, m: sums_ref[part, i, m]
    pack_rows(slab_of, out_ref, scr_ref, peers, width)


def columns(weights, fourier, to_grid, w_in, bias, w_hid, w_out, width):
    peers = fourier.shape[0] // 8
    vmem = pl.BlockSpec(memory_space=pltpu.VMEM)
    return pl.pallas_call(
        functools.partial(column_kernel, x_rows=240, width=width),
        in_specs=[pl.BlockSpec(memory_space=pltpu.SMEM)] + [vmem] * 6,
        out_specs=vmem,
        out_shape=jax.ShapeDtypeStruct(fourier.shape, bf16),
        scratch_shapes=[
            pltpu.VMEM((2, OWN * peers, OWN * LANES), bf16),
            pltpu.VMEM((NLON, OWN * LANES), bf16),
            pltpu.VMEM((2, OWN, OWN, peers, LANES), f32),
            pltpu.VMEM((2, peers * 8, LANES), f32),
        ],
        compiler_params=pltpu.CompilerParams(vmem_limit_bytes=28 * 2**20),
        name="columns",
    )(weights, fourier, to_grid, w_in, bias, w_hid, w_out)


def forward_kernel(
    class_ref, in_ref, table_ref, maps_ref, out_ref, sums_ref, scr_ref, sent_ref, full_ref,
    *, lats, lat_local, lat_slots, width,
):
    m = pl.program_id(0)
    peers = in_ref.shape[0] // 8

    @pl.when(m == 0)
    def _():
        def put(part, i, m, slab):
            sums_ref[m, part, pl.ds(i, peers, OWN), :] = slab

        unpack_rows(in_ref, scr_ref, put, peers, width)

    lanes = table_ref.shape[-1]
    weighted = jnp.concatenate(
        [
            jnp.concatenate(
                [
                    sums_ref[m, part, lat * lat_slots : lat * lat_slots + lat_local, :]
                    for lat in range(lats)
                ]
                + [jnp.zeros((lanes - lats * lat_local, LANES), f32)]
            )
            for part in range(2)
        ],
        axis=1,
    ).astype(bf16)
    forcing = dot(table_ref[0], weighted).astype(bf16)
    sent = out_ref.shape[2]
    rows = full_ref.shape[0] // lats
    spare = spare_lanes((lats, LANES), width)
    for v in range(maps_ref.shape[0]):
        full_ref[...] = dot(forcing, maps_ref[v])
        for b in range(sent // 8):
            last = full_ref[pl.ds(sent + b, lats, rows), :]
            for t in range(8):
                main = full_ref[pl.ds(8 * b + t, lats, rows), :]
                sent_ref[pl.ds(8 * b + t, lats, sent), :] = jnp.where(
                    spare, scatter_last(last, t, width), main
                )
        for q in range(lats):
            k, x = divmod(q, LAT_X)
            out_ref[x * Z_LOW + class_ref[k], v] = sent_ref[q * sent : (q + 1) * sent, :].astype(
                bf16
            )


def forward(classes, weighted, table, maps, peers, lats, sent, lat_local, lat_slots, width):
    levs = maps.shape[0]
    return pl.pallas_call(
        functools.partial(
            forward_kernel, lats=lats, lat_local=lat_local, lat_slots=lat_slots, width=width
        ),
        grid=(OWN,),
        in_specs=[
            pl.BlockSpec(memory_space=pltpu.SMEM),
            pl.BlockSpec(weighted.shape, lambda m: (0, 0)),
            pl.BlockSpec((1, *table.shape[1:]), lambda m: (m, 0, 0)),
            pl.BlockSpec(maps.shape, lambda m: (0, 0, 0)),
        ],
        out_specs=pl.BlockSpec((lats, levs, None, sent, LANES), lambda m: (0, 0, m, 0, 0)),
        out_shape=jax.ShapeDtypeStruct((lats, levs, OWN, sent, LANES), bf16),
        scratch_shapes=[
            pltpu.VMEM((OWN, 2, lats * lat_slots, LANES), f32),
            pltpu.VMEM((2, peers * 8, LANES), f32),
            pltpu.VMEM((lats * sent, LANES), f32),
            pltpu.VMEM((table.shape[1], LANES), f32),
        ],
        compiler_params=pltpu.CompilerParams(vmem_limit_bytes=20 * 2**20),
        name="forward",
    )(classes, weighted, table, maps)


def update_kernel(at_ref, state_ref, forcing_ref, out_ref, scr_ref, last_ref):
    _, channels, orders = state_ref.shape
    b = pl.program_id(0)
    main = pl.num_programs(0) - 1
    order = lax.broadcasted_iota(jnp.int32, (channels, orders), 1) + at_ref[0]

    def put(i, forcing):
        degree = jnp.full((channels, orders), b * 8 + i + at_ref[1], jnp.int32)
        ratio = (degree * (degree + 1)).astype(f32) / ((L - 1) * L)
        damping = 1.0 / (1.0 + hyper_rate * ratio * ratio)
        new = (state_ref[i] + time_step * forcing[:, :channels].T) * damping
        out_ref[i] = jnp.where(degree >= order, new, 0.0)

    @pl.when(b < main)
    def _():
        for x in range(LAT_X):
            skip = OWN * (first_group(x - 1) + Z_RING - first_group(x)) if x else 0
            first = (OWN * first_group(x) + skip) * 8
            mine = forcing_ref[x, skip:].astype(f32)
            scr_ref[first : first + mine.shape[0] * 8, :] = mine.reshape(-1, LANES)
        last = jnp.zeros((orders, LANES), f32)
        for t in range(8):
            slab = scr_ref[pl.ds(t, orders, 8), :]
            put(t, slab)
            last = gather_last(last, slab, t, channels)
        last_ref[b] = last

    @pl.when(b == main)
    def _():
        for i in range(last_ref.shape[0]):
            put(i, last_ref[i])


def update(at, state, forcing):
    degrees, channels, orders = state.shape
    _, group, sent, _ = forcing.shape
    main = sent // 8
    block = pl.BlockSpec((8, channels, orders), lambda i: (i, 0, 0))
    return pl.pallas_call(
        update_kernel,
        grid=(main + 1,),
        in_specs=[
            pl.BlockSpec(memory_space=pltpu.SMEM),
            block,
            pl.BlockSpec((LAT_X, group, 8, LANES), lambda i: (0, 0, jnp.minimum(i, main - 1), 0)),
        ],
        out_specs=block,
        out_shape=jax.ShapeDtypeStruct(state.shape, f32),
        scratch_shapes=[
            pltpu.VMEM((orders * 8, LANES), f32),
            pltpu.VMEM((degrees - sent, orders, LANES), f32),
        ],
        name="update",
    )(at, state, forcing)


def along_z(value, step):
    pairs = []
    flat = lambda x, z: x * Z_RING + 2 * (z % Z_LOW) + z // Z_LOW
    for x in range(LAT_X):
        pairs += [(flat(x, z), flat(x, (z + step) % Z_RING)) for z in range(Z_RING)]
    return lax.ppermute(value, ("lat", "lev"), pairs)


def along_x(value):
    groups = [[x * Z_LOW + z for x in range(LAT_X)] for z in range(Z_LOW)]
    return lax.all_to_all(value, "lat", 0, 0, axis_index_groups=groups, tiled=True)


def on_device(spectral_state, legendre, quad_weight, weight_in, bias_in, weight_hidden, weight_out):
    ord_size, lat_size, lev_size = (lax.axis_size(a) for a in ("ord", "lat", "lev"))
    ord_at, lat_at, lev_at = (lax.axis_index(a) for a in ("ord", "lat", "lev"))
    order_local, degree_local = spectral_state.shape[:2]
    lat_local = quad_weight.shape[0]
    row_local = spectral_state.shape[2] * spectral_state.shape[3]
    channels = 2 * row_local
    width = lev_size * row_local
    rows = -(-degree_local // 16) * 16
    sent = degree_local // 8 * 8
    peers = ord_size * lat_size * lev_size
    lat_slots = ord_size * lev_size * OWN
    everyone = ("lat", "ord", "lev")
    at = jnp.stack([ord_at * order_local, lat_at * degree_local]).astype(jnp.int32)
    maps = lane_maps(lev_size, row_local)
    state = spectral_state.transpose(1, 2, 3, 4, 0).reshape(degree_local, channels, order_local)

    z_at = lev_at * Z_LOW + lat_at % Z_LOW
    ring = (z_at + jnp.array([0, 1, -1, 2, -2], jnp.int32)) % Z_RING
    own = OWN * (2 * (ring % Z_LOW) + ring // Z_LOW)
    a_all, b_own, *b_rest = pack_table(own, legendre, HALF, rows)
    b_left, b_right, b_low, b_high = (along_z(v, k) for v, k in zip(b_rest, (1, -1, 2, -2)))
    a_all = along_x(a_all)
    b_far = jnp.concatenate([b_low, b_high], axis=2)
    b_all = jnp.stack([b_own, b_left, b_right, b_far], axis=1)
    a_all, b_all = lax.optimization_barrier((a_all, b_all))
    a_near = [along_z(a_all[:, 1], 1), along_z(a_all[:, 2], -1)]
    a_far = [along_z(a_all[:, 3, :, : rows // 2], 2), along_z(a_all[:, 3, :, rows // 2 :], -2)]
    b_all = along_x(b_all)

    slot = lax.iota(jnp.int32, OWN * peers)
    slot_lev = slot % lev_size
    slot_ord = slot // lev_size % ord_size
    slot_lat = slot // (lev_size * ord_size) % lat_size
    slot_x, slot_w = slot_lat // Z_LOW, 2 * (slot_lat % Z_LOW) + slot_lev
    valid = (slot_x % 2 == 0) | (slot_w > 0)
    order_ids = slot_ord * order_local + OWN * (first_group(slot_x) + slot_w) + slot // peers
    coefficients = prep(at, state, sent)
    coefficients, a_near, a_far, b_all = lax.optimization_barrier(
        (coefficients, a_near, a_far, b_all)
    )

    coefficients = coefficients.reshape(lat_size * lev_size, OWN, sent, LANES)
    coefficients = lax.all_to_all(coefficients, ("lat", "lev"), 0, 0, tiled=True)
    coefficients = coefficients.reshape(lat_size, lev_size, OWN, sent, LANES)
    classes = (z_at + jnp.array([0, -1, 1, 2], jnp.int32)) % Z_LOW
    table = assemble(a_all, a_near, a_far, b_all)
    fourier = inverse(classes, table, coefficients, maps, peers, lat_local, lat_slots, width)
    fourier, order_ids, valid = lax.optimization_barrier((fourier, order_ids, valid))
    to_grid = lookup_of(order_ids, valid)

    fourier = lax.all_to_all(fourier.reshape(peers, 8, -1), everyone, 0, 0, tiled=True)
    first = (ord_at * lev_size + lev_at) * OWN
    weights = lax.dynamic_slice_in_dim(jnp.pad(quad_weight, (0, lat_slots - lat_local)), first, OWN)
    weighted = columns(
        weights,
        fourier.reshape(peers * 8, -1),
        to_grid,
        jnp.pad(weight_in, ((0, LANES - width), (0, 0))),
        bias_in[None, :],
        weight_hidden,
        jnp.pad(weight_out, ((0, 0), (0, LANES - width))),
        width,
    )

    weighted = lax.all_to_all(weighted.reshape(peers, 8, -1), everyone, 0, 0, tiled=True)
    weighted = weighted.reshape(peers * 8, -1)
    forcing = forward(
        classes, weighted, table, maps, peers, lat_size, sent, lat_local, lat_slots, width
    )
    forcing = forcing.reshape(lat_size * lev_size, OWN, sent, LANES)
    forcing = lax.all_to_all(forcing, ("lat", "lev"), 0, 0, tiled=True)
    forcing = forcing.reshape(LAT_X, OWN * Z_RING, sent, LANES)
    updated = update(at, state, forcing)
    updated = updated.reshape(degree_local, *spectral_state.shape[2:], order_local)
    return updated.transpose(4, 0, 1, 2, 3)


def solution(mesh):
    return jax.shard_map(
        on_device,
        mesh=mesh,
        in_specs=(
            P("ord", "lat", "lev", None, None),
            P("ord", "lat", None),
            P("lat"),
            P(),
            P(),
            P(),
            P(),
        ),
        out_specs=P("ord", "lat", "lev", None, None),
        check_vma=False,
    )
```

```python
import functools
import math

import jax
import jax.numpy as jnp
import numpy as np
from jax import lax
from jax.experimental import pallas as pl
from jax.experimental.pallas import tpu as pltpu
from jax.sharding import PartitionSpec as P

L = 720
NLON = 1440
OWN = 3
LANES = 128
LAT_X, Z_LOW, Z_RING = 4, 4, 8
HALF = 384
X_ROWS = 1440
SPARE = 14

time_step = 1.0
hyper_rate = 2.0
transform_scale = math.sqrt(2.0 / NLON)

f32, bf16 = jnp.float32, jnp.bfloat16
dot = functools.partial(jnp.dot, preferred_element_type=jnp.float32)


def first_group(x):
    return (22 * x + 1) // 3


def lookup_of(order_ids, valid):
    low = 32

    def waves(x):
        phase_index = order_ids[None, :] * x[:, None] % NLON
        angles = 2.0 * math.pi / NLON * phase_index.astype(f32)
        return jnp.cos(angles), jnp.sin(angles)

    high_cos, high_sin = waves(low * lax.iota(jnp.int32, NLON // low))
    high_cos = jnp.where(valid[None, :], high_cos, 0.0)[:, None]
    high_sin = jnp.where(valid[None, :], high_sin, 0.0)[:, None]
    low_cos, low_sin = (w[None] for w in waves(lax.iota(jnp.int32, low)))
    cosines = high_cos * low_cos - high_sin * low_sin
    sines = -(high_sin * low_cos + high_cos * low_sin)
    shape = (NLON, order_ids.shape[0])
    return cosines.astype(bf16).reshape(shape), sines.astype(bf16).reshape(shape)


def half_silu(u):
    return u + u * jnp.tanh(u)


def lane_maps(levs, row_local):
    maps = np.zeros((levs, 2 * LANES, LANES), np.float32)
    for lev in range(levs):
        for row in range(row_local):
            for part in range(2):
                maps[lev, part * LANES + lev * row_local + row, 2 * row + part] = 1.0
    return jnp.asarray(maps, bf16)


def pack_rows(slab_of, out_ref, scr_ref, peers, width):
    lane = lax.broadcasted_iota(jnp.int32, (peers, LANES), 1)
    spare = (lane >= width) & (lane < width + SPARE)
    for part in range(2):
        last = slab_of(part, 2, 2)
        for k in range(8):
            moved = pltpu.roll(last, (width - SPARE * k) % LANES, 1)
            scr_ref[part, pl.ds(k, peers, 8), :] = jnp.where(
                spare, moved, slab_of(part, k // OWN, k % OWN)
            )
        out_ref[:, part * LANES : (part + 1) * LANES] = scr_ref[part].astype(bf16)


def unpack_rows(in_ref, scr_ref, put_slab, peers, width):
    lane = lax.broadcasted_iota(jnp.int32, (peers, LANES), 1)
    for part in range(2):
        scr_ref[part] = in_ref[:, part * LANES : (part + 1) * LANES].astype(f32)
        last = jnp.zeros((peers, LANES), f32)
        for k in range(8):
            slab = scr_ref[part, pl.ds(k, peers, 8), :]
            put_slab(part, k // OWN, k % OWN, slab)
            moved = pltpu.roll(slab, (SPARE * k - width) % LANES, 1)
            last = jnp.where((lane >= SPARE * k) & (lane < SPARE * (k + 1)), moved, last)
        put_slab(part, 2, 2, last)


def spare_lanes(shape, width):
    lane = lax.broadcasted_iota(jnp.int32, shape, len(shape) - 1)
    return (lane >= width) & (lane < width + SPARE)


def scatter_last(row, t, width):
    return pltpu.roll(row, (width - SPARE * t) % LANES, 1)


def gather_last(last, slab, t, width):
    lane = lax.broadcasted_iota(jnp.int32, slab.shape, 1)
    moved = pltpu.roll(slab, (SPARE * t - width) % LANES, 1)
    return jnp.where((lane >= SPARE * t) & (lane < SPARE * (t + 1)), moved, last)


def wide(value):
    return jnp.pad(value, ((0, 0), (0, LANES - value.shape[1])))


def prep_kernel(at_ref, state_ref, last_ref, out_ref, scr_ref):
    _, channels, orders = state_ref.shape
    group, rows = out_ref.shape[1], 8 * pl.num_programs(0)
    b = pl.program_id(0)
    order = lax.broadcasted_iota(jnp.int32, (channels, orders), 1) + at_ref[0]
    masked = lambda value, degree: wide(jnp.where(degree + at_ref[1] >= order, value, 0.0).T)
    last = masked(last_ref[b], rows + b)
    spare = spare_lanes(last.shape, channels)
    for t in range(8):
        scr_ref[pl.ds(t, orders, 8), :] = jnp.where(
            spare, scatter_last(last, t, channels), masked(state_ref[t], 8 * b + t)
        )
    packed = scr_ref[...].astype(bf16).reshape(orders, 8, LANES)
    for x in range(LAT_X):
        first = OWN * first_group(x)
        out_ref[x] = packed[first : first + group]


def prep(at, state, rows):
    group = OWN * Z_RING
    _, channels, orders = state.shape
    steps = rows // 8
    return pl.pallas_call(
        prep_kernel,
        grid=(steps,),
        in_specs=[
            pl.BlockSpec(memory_space=pltpu.SMEM),
            pl.BlockSpec((8, channels, orders), lambda i: (i, 0, 0)),
            pl.BlockSpec((8, channels, orders), lambda i: (steps, 0, 0)),
        ],
        out_specs=pl.BlockSpec((LAT_X, group, 8, LANES), lambda i: (0, 0, i, 0)),
        out_shape=jax.ShapeDtypeStruct((LAT_X, group, rows, LANES), bf16),
        scratch_shapes=[pltpu.VMEM((orders * 8, LANES), f32)],
        cost_estimate=pl.CostEstimate(flops=10**6, bytes_accessed=4 * 10**6, transcendentals=0),
        name="prep",
    )(at, state, state)


def pack_kernel(own_ref, in_ref, a_ref, *b_refs):
    degrees, lats = in_ref.shape[1:]
    half, rows = a_ref.shape[-1], a_ref.shape[-2]
    split = rows // 2
    a_ref[...] = jnp.zeros_like(a_ref)
    for ref in b_refs:
        ref[...] = jnp.zeros_like(ref)
    for k in range(3):
        mine = in_ref[pl.ds(own_ref[k], OWN)]
        a_ref[0, k, :, :degrees, :] = mine[:, :, :half]
        b_refs[k][0, :, :degrees, : lats - half] = mine[:, :, half:]
    mine = in_ref[pl.ds(own_ref[3], OWN)]
    a_ref[0, 3, :, :split, :] = mine[:, :split, :half]
    b_refs[3][0, :, :, : lats - half] = mine[:, :split, half:]
    mine = in_ref[pl.ds(own_ref[4], OWN)]
    a_ref[0, 3, :, split:degrees, :] = mine[:, split:, :half]
    b_refs[4][0, :, : degrees - split, : lats - half] = mine[:, split:, half:]


def pack_table(own, legendre, half, rows):
    _, degrees, lats = legendre.shape
    group = OWN * Z_RING
    b_shape = lambda r: jax.ShapeDtypeStruct((LAT_X, OWN, r, half), bf16)
    b_spec = lambda r: pl.BlockSpec((1, OWN, r, half), lambda x: (x, 0, 0, 0))
    b_rows = (rows, rows, rows, rows // 2, rows // 2)
    return pl.pallas_call(
        pack_kernel,
        grid=(LAT_X,),
        in_specs=[
            pl.BlockSpec(memory_space=pltpu.SMEM),
            pl.BlockSpec(
                (pl.Element(group), pl.Element(degrees), pl.Element(lats)),
                lambda x: (OWN * first_group(x), 0, 0),
            ),
        ],
        out_specs=[pl.BlockSpec((1, 4, OWN, rows, half), lambda x: (x, 0, 0, 0, 0))]
        + [b_spec(r) for r in b_rows],
        out_shape=[jax.ShapeDtypeStruct((LAT_X, 4, OWN, rows, half), bf16)]
        + [b_shape(r) for r in b_rows],
        compiler_params=pltpu.CompilerParams(vmem_limit_bytes=60 * 2**20),
        name="pack_table",
    )(own, legendre)


def assemble_kernel(a_own_ref, a_left_ref, a_right_ref, a_low_ref, a_high_ref, b_ref, out_ref):
    rows, half = b_ref.shape[-2:]
    place = LAT_X * rows
    far = jnp.concatenate([a_low_ref[...], a_high_ref[...]], axis=1)
    for k, piece in enumerate((a_own_ref[:, 0], a_left_ref[...], a_right_ref[...], far)):
        out_ref[0, k * place : (k + 1) * place, :half] = piece.reshape(place, half)
        out_ref[0, k * place : (k + 1) * place, half:] = b_ref[:, k].reshape(place, half)


def assemble(a_own, a_near, a_far, b_all):
    rows, half = b_all.shape[-2:]
    size = 4 * LAT_X * rows
    near = pl.BlockSpec((LAT_X, None, rows, half), lambda m: (0, m, 0, 0))
    far = pl.BlockSpec((LAT_X, None, rows // 2, half), lambda m: (0, m, 0, 0))
    return pl.pallas_call(
        assemble_kernel,
        grid=(OWN,),
        in_specs=[
            pl.BlockSpec((LAT_X, 1, None, rows, half), lambda m: (0, 0, m, 0, 0)),
            near,
            near,
            far,
            far,
            pl.BlockSpec((LAT_X, 4, None, rows, half), lambda m: (0, 0, m, 0, 0)),
        ],
        out_specs=pl.BlockSpec((1, size, 2 * half), lambda m: (m, 0, 0)),
        out_shape=jax.ShapeDtypeStruct((OWN, size, 2 * half), bf16),
        cost_estimate=pl.CostEstimate(flops=10**6, bytes_accessed=8 * 10**6, transcendentals=0),
        name="assemble",
    )(a_own, *a_near, *a_far, b_all)


def inverse_kernel(
    class_ref, table_ref, coef_ref, maps_ref, out_ref, sums_ref, scr_ref, sent_ref, full_ref,
    *, lats, lat_local, lat_slots, width,
):
    sent = coef_ref.shape[3]
    rows = full_ref.shape[0] // lats
    for m in range(OWN):
        swapped = 0.0
        for v in range(maps_ref.shape[0]):
            for q in range(lats):
                k, x = divmod(q, LAT_X)
                piece = coef_ref[x * Z_LOW + class_ref[k], v, m].astype(f32)
                sent_ref[q * sent : (q + 1) * sent, :] = piece
                full_ref[q * rows : q * rows + sent, :] = piece
                full_ref[q * rows + sent : (q + 1) * rows, :] = jnp.zeros((rows - sent, LANES), f32)
            for b in range(sent // 8):
                last = jnp.zeros((lats, LANES), f32)
                for t in range(8):
                    slab = sent_ref[pl.ds(8 * b + t, lats, sent), :]
                    last = gather_last(last, slab, t, width)
                full_ref[pl.ds(sent + b, lats, rows), :] = last
            swapped += lax.dot_general(
                maps_ref[v],
                full_ref[...].astype(bf16),
                (((1,), (1,)), ((), ())),
                preferred_element_type=f32,
            )
        sums = dot(swapped.astype(bf16), table_ref[m]).T
        for part in range(2):
            lanes = slice(part * LANES, (part + 1) * LANES)
            for lat in range(lats):
                first = lat * lat_slots
                sums_ref[m, part, first : first + lat_local, :] = sums[
                    lat * lat_local : (lat + 1) * lat_local, lanes
                ]
                sums_ref[m, part, first + lat_local : first + lat_slots, :] = jnp.zeros(
                    (lat_slots - lat_local, LANES), f32
                )

    peers = out_ref.shape[0] // 8
    slab_of = lambda part, i, m: sums_ref[m, part, pl.ds(i, peers, OWN), :]
    pack_rows(slab_of, out_ref, scr_ref, peers, width)


def inverse(classes, table, coef, maps, peers, lat_local, lat_slots, width):
    lats, _, _, sent, _ = coef.shape
    vmem = pl.BlockSpec(memory_space=pltpu.VMEM)
    return pl.pallas_call(
        functools.partial(
            inverse_kernel, lats=lats, lat_local=lat_local, lat_slots=lat_slots, width=width
        ),
        in_specs=[pl.BlockSpec(memory_space=pltpu.SMEM), vmem, vmem, vmem],
        out_specs=vmem,
        out_shape=jax.ShapeDtypeStruct((peers * 8, 2 * LANES), bf16),
        scratch_shapes=[
            pltpu.VMEM((OWN, 2, lats * lat_slots, LANES), f32),
            pltpu.VMEM((2, peers * 8, LANES), f32),
            pltpu.VMEM((lats * sent, LANES), f32),
            pltpu.VMEM((table.shape[1], LANES), f32),
        ],
        compiler_params=pltpu.CompilerParams(vmem_limit_bytes=24 * 2**20),
        name="inverse",
    )(classes, table, coef, maps)


def column_kernel(
    weight_ref, in_ref, cos_ref, sin_ref, w_in_ref, bias_ref, w_hid_ref, w_out_ref,
    out_ref, fourier_ref, tendency_ref, sums_ref, scr_ref, *, x_rows, width,
):
    peers = in_ref.shape[0] // 8

    def put(part, i, m, slab):
        fourier_ref[part, m * peers : (m + 1) * peers, i * LANES : (i + 1) * LANES] = slab.astype(
            bf16
        )

    unpack_rows(in_ref, scr_ref, put, peers, width)

    def grid_rows(step, carry):
        rows = pl.ds(pl.multiple_of(step * x_rows, x_rows), x_rows)
        raw = dot(cos_ref[rows, :], fourier_ref[0]) + dot(sin_ref[rows, :], fourier_ref[1])
        features = (transform_scale * raw).astype(bf16)
        lanes = [slice(i * LANES, (i + 1) * LANES) for i in range(OWN)]
        hidden = [half_silu(dot(features[:, at], w_in_ref[...]) + bias_ref[...]) for at in lanes]
        hidden = [h.astype(bf16) for h in hidden]
        for layer in range(w_hid_ref.shape[0]):
            update = [half_silu(dot(h, w_hid_ref[layer])) for h in hidden]
            hidden = [(h.astype(f32) + u).astype(bf16) for h, u in zip(hidden, update)]
        for at, h in zip(lanes, hidden):
            tendency_ref[rows, at] = dot(h, w_out_ref[...]).astype(bf16)
        return carry

    lax.fori_loop(0, NLON // x_rows, grid_rows, 0)

    for part, table_ref in enumerate((cos_ref, sin_ref)):
        sums = lax.dot_general(
            tendency_ref[...],
            table_ref[...],
            (((0,), (0,)), ((), ())),
            preferred_element_type=f32,
        )
        for i in range(OWN):
            weight = weight_ref[i] * transform_scale
            for m in range(OWN):
                block = sums[i * LANES : (i + 1) * LANES, m * peers : (m + 1) * peers]
                sums_ref[part, i, m] = weight * block.T

    slab_of = lambda part, i, m: sums_ref[part, i, m]
    pack_rows(slab_of, out_ref, scr_ref, peers, width)


def columns(weights, fourier, cosines, sines, w_in, bias, w_hid, w_out, width):
    peers = fourier.shape[0] // 8
    vmem = pl.BlockSpec(memory_space=pltpu.VMEM)
    return pl.pallas_call(
        functools.partial(column_kernel, x_rows=X_ROWS, width=width),
        in_specs=[pl.BlockSpec(memory_space=pltpu.SMEM)] + [vmem] * 7,
        out_specs=vmem,
        out_shape=jax.ShapeDtypeStruct(fourier.shape, bf16),
        scratch_shapes=[
            pltpu.VMEM((2, OWN * peers, OWN * LANES), bf16),
            pltpu.VMEM((NLON, OWN * LANES), bf16),
            pltpu.VMEM((2, OWN, OWN, peers, LANES), f32),
            pltpu.VMEM((2, peers * 8, LANES), f32),
        ],
        compiler_params=pltpu.CompilerParams(vmem_limit_bytes=40 * 2**20),
        name="columns",
    )(weights, fourier, cosines, sines, w_in, bias, w_hid, w_out)


def forward_kernel(
    class_ref, in_ref, table_ref, maps_ref, out_ref, sums_ref, scr_ref, sent_ref, full_ref,
    *, lats, lat_local, lat_slots, width,
):
    peers = in_ref.shape[0] // 8

    def put(part, i, m, slab):
        sums_ref[m, part, pl.ds(i, peers, OWN), :] = slab

    unpack_rows(in_ref, scr_ref, put, peers, width)
    lanes = table_ref.shape[-1]
    sent = out_ref.shape[3]
    rows = full_ref.shape[0] // lats
    spare = spare_lanes((lats, LANES), width)
    for m in range(OWN):
        weighted = jnp.concatenate(
            [
                jnp.concatenate(
                    [
                        sums_ref[m, part, lat * lat_slots : lat * lat_slots + lat_local, :]
                        for lat in range(lats)
                    ]
                    + [jnp.zeros((lanes - lats * lat_local, LANES), f32)]
                )
                for part in range(2)
            ],
            axis=1,
        ).astype(bf16)
        forcing = dot(table_ref[m], weighted).astype(bf16)
        for v in range(maps_ref.shape[0]):
            full_ref[...] = dot(forcing, maps_ref[v])
            for b in range(sent // 8):
                last = full_ref[pl.ds(sent + b, lats, rows), :]
                for t in range(8):
                    main = full_ref[pl.ds(8 * b + t, lats, rows), :]
                    sent_ref[pl.ds(8 * b + t, lats, sent), :] = jnp.where(
                        spare, scatter_last(last, t, width), main
                    )
            for q in range(lats):
                k, x = divmod(q, LAT_X)
                piece = sent_ref[q * sent : (q + 1) * sent, :].astype(bf16)
                out_ref[x * Z_LOW + class_ref[k], v, m] = piece


def forward(classes, weighted, table, maps, peers, lats, sent, lat_local, lat_slots, width):
    levs = maps.shape[0]
    vmem = pl.BlockSpec(memory_space=pltpu.VMEM)
    return pl.pallas_call(
        functools.partial(
            forward_kernel, lats=lats, lat_local=lat_local, lat_slots=lat_slots, width=width
        ),
        in_specs=[pl.BlockSpec(memory_space=pltpu.SMEM), vmem, vmem, vmem],
        out_specs=vmem,
        out_shape=jax.ShapeDtypeStruct((lats, levs, OWN, sent, LANES), bf16),
        scratch_shapes=[
            pltpu.VMEM((OWN, 2, lats * lat_slots, LANES), f32),
            pltpu.VMEM((2, peers * 8, LANES), f32),
            pltpu.VMEM((lats * sent, LANES), f32),
            pltpu.VMEM((table.shape[1], LANES), f32),
        ],
        compiler_params=pltpu.CompilerParams(vmem_limit_bytes=24 * 2**20),
        name="forward",
    )(classes, weighted, table, maps)


def turn_maps(channels):
    maps = np.zeros((8, 2 * channels, LANES), np.float32)
    for t in range(8):
        maps[t, np.arange(channels), np.arange(channels)] = 1.0
        piece = np.arange(SPARE)
        maps[t, channels + SPARE * t + piece, channels + piece] = 1.0
    return jnp.asarray(maps, bf16)


def update_kernel(at_ref, damping_ref, state_ref, forcing_ref, maps_ref, out_ref, scr_ref):
    degrees, channels, orders = state_ref.shape
    order = lax.broadcasted_iota(jnp.int32, (channels, orders), 1) + at_ref[0]

    def put(degree, forcing):
        new = (state_ref[degree] + time_step * forcing) * damping_ref[degree]
        out_ref[degree] = jnp.where(degree + at_ref[1] >= order, new, 0.0)

    sent = forcing_ref.shape[2]
    for b in range(sent // 8):
        for x in range(LAT_X):
            skip = OWN * (first_group(x - 1) + Z_RING - first_group(x)) if x else 0
            first = (OWN * first_group(x) + skip) * 8
            mine = forcing_ref[x, skip:, 8 * b : 8 * b + 8, :].astype(f32)
            scr_ref[b, first : first + mine.shape[0] * 8, :] = mine.reshape(-1, LANES)
        last = 0.0
        for t in range(8):
            turned = lax.dot_general(
                maps_ref[t],
                scr_ref[b, pl.ds(t, orders, 8), :].astype(bf16),
                (((1,), (1,)), ((), ())),
                preferred_element_type=f32,
            )
            put(8 * b + t, turned[:channels])
            last += turned[channels:]
        put(sent + b, last)


def update(at, damping, state, forcing):
    degrees, channels, orders = state.shape
    _, _, sent, _ = forcing.shape
    smem, vmem = (pl.BlockSpec(memory_space=m) for m in (pltpu.SMEM, pltpu.VMEM))
    return pl.pallas_call(
        update_kernel,
        in_specs=[smem, smem, vmem, vmem, vmem],
        out_specs=vmem,
        out_shape=jax.ShapeDtypeStruct(state.shape, f32),
        scratch_shapes=[pltpu.VMEM((sent // 8, orders * 8, LANES), f32)],
        compiler_params=pltpu.CompilerParams(vmem_limit_bytes=24 * 2**20),
        name="update",
    )(at, damping, state, forcing, turn_maps(channels))


def along_z(value, step):
    pairs = []
    flat = lambda x, z: x * Z_RING + 2 * (z % Z_LOW) + z // Z_LOW
    for x in range(LAT_X):
        pairs += [(flat(x, z), flat(x, (z + step) % Z_RING)) for z in range(Z_RING)]
    return lax.ppermute(value, ("lat", "lev"), pairs)


def along_x(value):
    groups = [[x * Z_LOW + z for x in range(LAT_X)] for z in range(Z_LOW)]
    return lax.all_to_all(value, "lat", 0, 0, axis_index_groups=groups, tiled=True)


def on_device(spectral_state, legendre, quad_weight, weight_in, bias_in, weight_hidden, weight_out):
    ord_size, lat_size, lev_size = (lax.axis_size(a) for a in ("ord", "lat", "lev"))
    ord_at, lat_at, lev_at = (lax.axis_index(a) for a in ("ord", "lat", "lev"))
    order_local, degree_local = spectral_state.shape[:2]
    lat_local = quad_weight.shape[0]
    row_local = spectral_state.shape[2] * spectral_state.shape[3]
    channels = 2 * row_local
    width = lev_size * row_local
    rows = -(-degree_local // 16) * 16
    sent = degree_local // 8 * 8
    peers = ord_size * lat_size * lev_size
    lat_slots = ord_size * lev_size * OWN
    everyone = ("lat", "ord", "lev")
    at = jnp.stack([ord_at * order_local, lat_at * degree_local]).astype(jnp.int32)
    maps = lane_maps(lev_size, row_local)
    state = spectral_state.transpose(1, 2, 3, 4, 0).reshape(degree_local, channels, order_local)

    z_at = lev_at * Z_LOW + lat_at % Z_LOW
    ring = (z_at + jnp.array([0, 1, -1, 2, -2], jnp.int32)) % Z_RING
    own = OWN * (2 * (ring % Z_LOW) + ring // Z_LOW)
    a_all, b_own, *b_rest = pack_table(own, legendre, HALF, rows)
    b_left, b_right, b_low, b_high = (along_z(v, k) for v, k in zip(b_rest, (1, -1, 2, -2)))
    a_all = along_x(a_all)
    b_far = jnp.concatenate([b_low, b_high], axis=2)
    b_all = jnp.stack([b_own, b_left, b_right, b_far], axis=1)
    a_all, b_all = lax.optimization_barrier((a_all, b_all))
    a_near = [along_z(a_all[:, 1], 1), along_z(a_all[:, 2], -1)]
    a_far = [along_z(a_all[:, 3, :, : rows // 2], 2), along_z(a_all[:, 3, :, rows // 2 :], -2)]
    b_all = along_x(b_all)

    slot = lax.iota(jnp.int32, OWN * peers)
    slot_lev = slot % lev_size
    slot_ord = slot // lev_size % ord_size
    slot_lat = slot // (lev_size * ord_size) % lat_size
    slot_x, slot_w = slot_lat // Z_LOW, 2 * (slot_lat % Z_LOW) + slot_lev
    valid = (slot_x % 2 == 0) | (slot_w > 0)
    order_ids = slot_ord * order_local + OWN * (first_group(slot_x) + slot_w) + slot // peers
    coefficients = prep(at, state, sent)
    coefficients, a_near, a_far, b_all = lax.optimization_barrier(
        (coefficients, a_near, a_far, b_all)
    )

    coefficients = coefficients.reshape(lat_size * lev_size, OWN, sent, LANES)
    coefficients = lax.all_to_all(coefficients, ("lat", "lev"), 0, 0, tiled=True)
    coefficients = coefficients.reshape(lat_size, lev_size, OWN, sent, LANES)
    classes = (z_at + jnp.array([0, -1, 1, 2], jnp.int32)) % Z_LOW
    table = assemble(a_all, a_near, a_far, b_all)
    fourier = inverse(classes, table, coefficients, maps, peers, lat_local, lat_slots, width)
    fourier, order_ids, valid = lax.optimization_barrier((fourier, order_ids, valid))
    cosines, sines = lookup_of(order_ids, valid)

    fourier = lax.all_to_all(fourier.reshape(peers, 8, -1), everyone, 0, 0, tiled=True)
    first = (ord_at * lev_size + lev_at) * OWN
    weights = lax.dynamic_slice_in_dim(jnp.pad(quad_weight, (0, lat_slots - lat_local)), first, OWN)
    weighted = columns(
        weights,
        fourier.reshape(peers * 8, -1),
        cosines,
        sines,
        jnp.pad(0.5 * weight_in, ((0, LANES - width), (0, 0))),
        0.5 * bias_in[None, :],
        0.5 * weight_hidden,
        jnp.pad(weight_out, ((0, 0), (0, LANES - width))),
        width,
    )

    weighted = lax.all_to_all(weighted.reshape(peers, 8, -1), everyone, 0, 0, tiled=True)
    weighted = weighted.reshape(peers * 8, -1)
    forcing = forward(
        classes, weighted, table, maps, peers, lat_size, sent, lat_local, lat_slots, width
    )
    forcing = forcing.reshape(lat_size * lev_size, OWN, sent, LANES)
    forcing = lax.all_to_all(forcing, ("lat", "lev"), 0, 0, tiled=True)
    forcing = forcing.reshape(LAT_X, OWN * Z_RING, sent, LANES)
    degree_ids = lat_at * degree_local + lax.iota(jnp.int32, degree_local)
    degree_ratio = (degree_ids * (degree_ids + 1)).astype(f32) / ((L - 1) * L)
    damping = 1.0 / (1.0 + hyper_rate * degree_ratio * degree_ratio)
    updated = update(at, damping, state, forcing)
    updated = updated.reshape(degree_local, *spectral_state.shape[2:], order_local)
    return updated.transpose(4, 0, 1, 2, 3)


def solution(mesh):
    return jax.shard_map(
        on_device,
        mesh=mesh,
        in_specs=(
            P("ord", "lat", "lev", None, None),
            P("ord", "lat", None),
            P("lat"),
            P(),
            P(),
            P(),
            P(),
        ),
        out_specs=P("ord", "lat", "lev", None, None),
        check_vma=False,
    )
```

```python
import functools
import math

import jax
import jax.numpy as jnp
import numpy as np
from jax import lax
from jax.experimental import pallas as pl
from jax.experimental.pallas import tpu as pltpu
from jax.sharding import PartitionSpec as P

L = 720
NLON = 1440
OWN = 3
LANES = 128
LAT_X, Z_LOW, Z_RING = 4, 4, 8
HALF = 384
X_ROWS = 1440
SPARE = 14

time_step = 1.0
hyper_rate = 2.0
transform_scale = math.sqrt(2.0 / NLON)

f32, bf16 = jnp.float32, jnp.bfloat16
dot = functools.partial(jnp.dot, preferred_element_type=jnp.float32)


def first_group(x):
    return (22 * x + 1) // 3


def lookup_of(order_ids, valid):
    low = 32

    def waves(x):
        phase_index = order_ids[None, :] * x[:, None] % NLON
        angles = 2.0 * math.pi / NLON * phase_index.astype(f32)
        return jnp.cos(angles), jnp.sin(angles)

    high_cos, high_sin = waves(low * lax.iota(jnp.int32, NLON // low))
    high_cos = jnp.where(valid[None, :], high_cos, 0.0)[:, None]
    high_sin = jnp.where(valid[None, :], high_sin, 0.0)[:, None]
    low_cos, low_sin = (w[None] for w in waves(lax.iota(jnp.int32, low)))
    cosines = high_cos * low_cos - high_sin * low_sin
    sines = -(high_sin * low_cos + high_cos * low_sin)
    shape = (NLON, order_ids.shape[0])
    return cosines.astype(bf16).reshape(shape), sines.astype(bf16).reshape(shape)


def half_silu(u):
    return u + u * jnp.tanh(u)


def lane_maps(levs, row_local):
    maps = np.zeros((levs, 2 * LANES, LANES), np.float32)
    for lev in range(levs):
        for row in range(row_local):
            for part in range(2):
                maps[lev, part * LANES + lev * row_local + row, 2 * row + part] = 1.0
    return jnp.asarray(maps, bf16)


def pack_rows(slab_of, out_ref, scr_ref, peers, width):
    lane = lax.broadcasted_iota(jnp.int32, (peers, LANES), 1)
    spare = (lane >= width) & (lane < width + SPARE)
    for part in range(2):
        last = slab_of(part, 2, 2)
        for k in range(8):
            moved = pltpu.roll(last, (width - SPARE * k) % LANES, 1)
            scr_ref[part, pl.ds(k, peers, 8), :] = jnp.where(
                spare, moved, slab_of(part, k // OWN, k % OWN)
            )
        out_ref[:, part * LANES : (part + 1) * LANES] = scr_ref[part].astype(bf16)


def unpack_rows(in_ref, scr_ref, put_slab, peers, width):
    lane = lax.broadcasted_iota(jnp.int32, (peers, LANES), 1)
    for part in range(2):
        scr_ref[part] = in_ref[:, part * LANES : (part + 1) * LANES].astype(f32)
        last = jnp.zeros((peers, LANES), f32)
        for k in range(8):
            slab = scr_ref[part, pl.ds(k, peers, 8), :]
            put_slab(part, k // OWN, k % OWN, slab)
            moved = pltpu.roll(slab, (SPARE * k - width) % LANES, 1)
            last = jnp.where((lane >= SPARE * k) & (lane < SPARE * (k + 1)), moved, last)
        put_slab(part, 2, 2, last)


def spare_lanes(shape, width):
    lane = lax.broadcasted_iota(jnp.int32, shape, len(shape) - 1)
    return (lane >= width) & (lane < width + SPARE)


def scatter_last(row, t, width):
    return pltpu.roll(row, (width - SPARE * t) % LANES, 1)


def gather_last(last, slab, t, width):
    lane = lax.broadcasted_iota(jnp.int32, slab.shape, 1)
    moved = pltpu.roll(slab, (SPARE * t - width) % LANES, 1)
    return jnp.where((lane >= SPARE * t) & (lane < SPARE * (t + 1)), moved, last)


def wide(value):
    return jnp.pad(value, ((0, 0), (0, LANES - value.shape[1])))


def prep_kernel(at_ref, state_ref, last_ref, out_ref, scr_ref):
    _, channels, orders = state_ref.shape
    group, rows = out_ref.shape[1], 8 * pl.num_programs(0)
    b = pl.program_id(0)
    order = lax.broadcasted_iota(jnp.int32, (channels, orders), 1) + at_ref[0]
    masked = lambda value, degree: wide(jnp.where(degree + at_ref[1] >= order, value, 0.0).T)
    last = masked(last_ref[b], rows + b)
    spare = spare_lanes(last.shape, channels)
    for t in range(8):
        scr_ref[pl.ds(t, orders, 8), :] = jnp.where(
            spare, scatter_last(last, t, channels), masked(state_ref[t], 8 * b + t)
        )
    packed = scr_ref[...].astype(bf16).reshape(orders, 8, LANES)
    for x in range(LAT_X):
        first = OWN * first_group(x)
        out_ref[x] = packed[first : first + group]


def prep(at, state, rows):
    group = OWN * Z_RING
    _, channels, orders = state.shape
    steps = rows // 8
    return pl.pallas_call(
        prep_kernel,
        grid=(steps,),
        in_specs=[
            pl.BlockSpec(memory_space=pltpu.SMEM),
            pl.BlockSpec((8, channels, orders), lambda i: (i, 0, 0)),
            pl.BlockSpec((8, channels, orders), lambda i: (steps, 0, 0)),
        ],
        out_specs=pl.BlockSpec((LAT_X, group, 8, LANES), lambda i: (0, 0, i, 0)),
        out_shape=jax.ShapeDtypeStruct((LAT_X, group, rows, LANES), bf16),
        scratch_shapes=[pltpu.VMEM((orders * 8, LANES), f32)],
        cost_estimate=pl.CostEstimate(flops=10**6, bytes_accessed=4 * 10**6, transcendentals=0),
        name="prep",
    )(at, state, state)


def pack_kernel(meta_ref, in_ref, a_ref, *b_refs):
    degrees, lats = in_ref.shape[1:]
    half, rows = a_ref.shape[-1], a_ref.shape[-2]
    split = rows // 2
    a_ref[...] = jnp.zeros_like(a_ref)
    for ref in b_refs:
        ref[...] = jnp.zeros_like(ref)
    for k in range(3):
        mine = in_ref[pl.ds(meta_ref[1 + k], OWN)]
        a_ref[0, k, :, :degrees, :] = mine[:, :, :half]
        b_refs[k][0, :, :degrees, : lats - half] = mine[:, :, half:]
    mine = in_ref[pl.ds(meta_ref[4], OWN)]
    a_ref[0, 3, :, :split, :] = mine[:, :split, :half]
    b_refs[3][0, :, :, : lats - half] = mine[:, :split, half:]
    mine = in_ref[pl.ds(meta_ref[5], OWN)]
    a_ref[0, 3, :, split:degrees, :] = mine[:, split:, :half]
    b_refs[4][0, :, : degrees - split, : lats - half] = mine[:, split:, half:]


def pack_table(meta, legendre, half, rows):
    _, degrees, lats = legendre.shape
    group = OWN * Z_RING
    x_of = lambda d, meta: lax.rem(meta[0] + d, LAT_X)
    b_rows = (rows, rows, rows, rows // 2, rows // 2)
    b_specs = [pl.BlockSpec((1, OWN, r, half), lambda d, meta: (d, 0, 0, 0)) for r in b_rows]
    return pl.pallas_call(
        pack_kernel,
        grid_spec=pltpu.PrefetchScalarGridSpec(
            num_scalar_prefetch=1,
            grid=(LAT_X,),
            in_specs=[
                pl.BlockSpec(
                    (pl.Element(group), pl.Element(degrees), pl.Element(lats)),
                    lambda d, meta: (OWN * first_group(x_of(d, meta)), 0, 0),
                ),
            ],
            out_specs=[
                pl.BlockSpec((1, 4, OWN, rows, half), lambda d, meta: (x_of(d, meta), 0, 0, 0, 0))
            ]
            + b_specs,
        ),
        out_shape=[jax.ShapeDtypeStruct((LAT_X, 4, OWN, rows, half), bf16)]
        + [jax.ShapeDtypeStruct((LAT_X, OWN, r, half), bf16) for r in b_rows],
        compiler_params=pltpu.CompilerParams(vmem_limit_bytes=16 * 2**20),
        name="pack_table",
    )(meta, legendre)


def assemble_kernel(
    from_ref, a_own_ref, a_left_ref, a_right_ref, a_low_ref, a_high_ref, *refs
):
    out_ref, b_refs = refs[-1], refs[:-1]
    rows, half = a_own_ref.shape[-2:]
    place = LAT_X * rows
    far = jnp.concatenate([a_low_ref[...], a_high_ref[...]], axis=1)
    for k, piece in enumerate((a_own_ref[:, 0], a_left_ref[...], a_right_ref[...], far)):
        out_ref[0, k * place : (k + 1) * place, :half] = piece.reshape(place, half)
        for d, b_ref in enumerate(b_refs):
            first = pl.multiple_of(k * place + from_ref[d] * rows, 16)
            out_ref[0, pl.ds(first, rows), half:] = b_ref[k]


def assemble(sources, a_own, a_near, a_far, b_all):
    rows, half = a_own.shape[-2:]
    size = 4 * LAT_X * rows
    near = pl.BlockSpec((LAT_X, None, rows, half), lambda m: (0, m, 0, 0))
    far = pl.BlockSpec((LAT_X, None, rows // 2, half), lambda m: (0, m, 0, 0))
    return pl.pallas_call(
        assemble_kernel,
        grid=(OWN,),
        in_specs=[
            pl.BlockSpec(memory_space=pltpu.SMEM),
            pl.BlockSpec((LAT_X, 1, None, rows, half), lambda m: (0, 0, m, 0, 0)),
            near,
            near,
            far,
            far,
        ]
        + [pl.BlockSpec((4, None, rows, half), lambda m: (0, m, 0, 0))] * LAT_X,
        out_specs=pl.BlockSpec((1, size, 2 * half), lambda m: (m, 0, 0)),
        out_shape=jax.ShapeDtypeStruct((OWN, size, 2 * half), bf16),
        cost_estimate=pl.CostEstimate(flops=10**6, bytes_accessed=8 * 10**6, transcendentals=0),
        name="assemble",
    )(sources, a_own, *a_near, *a_far, *b_all)


def inverse_kernel(
    class_ref, table_ref, coef_ref, maps_ref, out_ref, sums_ref, scr_ref, sent_ref, full_ref,
    *, lats, lat_local, lat_slots, width,
):
    sent = coef_ref.shape[3]
    rows = full_ref.shape[0] // lats
    for m in range(OWN):
        swapped = 0.0
        for v in range(maps_ref.shape[0]):
            for q in range(lats):
                k, x = divmod(q, LAT_X)
                piece = coef_ref[x * Z_LOW + class_ref[k], v, m].astype(f32)
                sent_ref[q * sent : (q + 1) * sent, :] = piece
                full_ref[q * rows : q * rows + sent, :] = piece
                full_ref[q * rows + sent : (q + 1) * rows, :] = jnp.zeros((rows - sent, LANES), f32)
            for b in range(sent // 8):
                last = jnp.zeros((lats, LANES), f32)
                for t in range(8):
                    slab = sent_ref[pl.ds(8 * b + t, lats, sent), :]
                    last = gather_last(last, slab, t, width)
                full_ref[pl.ds(sent + b, lats, rows), :] = last
            swapped += lax.dot_general(
                maps_ref[v],
                full_ref[...].astype(bf16),
                (((1,), (1,)), ((), ())),
                preferred_element_type=f32,
            )
        sums = dot(swapped.astype(bf16), table_ref[m]).T
        for part in range(2):
            lanes = slice(part * LANES, (part + 1) * LANES)
            for lat in range(lats):
                first = lat * lat_slots
                sums_ref[m, part, first : first + lat_local, :] = sums[
                    lat * lat_local : (lat + 1) * lat_local, lanes
                ]
                sums_ref[m, part, first + lat_local : first + lat_slots, :] = jnp.zeros(
                    (lat_slots - lat_local, LANES), f32
                )

    peers = out_ref.shape[0] // 8
    slab_of = lambda part, i, m: sums_ref[m, part, pl.ds(i, peers, OWN), :]
    pack_rows(slab_of, out_ref, scr_ref, peers, width)


def inverse(classes, table, coef, maps, peers, lat_local, lat_slots, width):
    lats, _, _, sent, _ = coef.shape
    vmem = pl.BlockSpec(memory_space=pltpu.VMEM)
    return pl.pallas_call(
        functools.partial(
            inverse_kernel, lats=lats, lat_local=lat_local, lat_slots=lat_slots, width=width
        ),
        in_specs=[pl.BlockSpec(memory_space=pltpu.SMEM), vmem, vmem, vmem],
        out_specs=vmem,
        out_shape=jax.ShapeDtypeStruct((peers * 8, 2 * LANES), bf16),
        scratch_shapes=[
            pltpu.VMEM((OWN, 2, lats * lat_slots, LANES), f32),
            pltpu.VMEM((2, peers * 8, LANES), f32),
            pltpu.VMEM((lats * sent, LANES), f32),
            pltpu.VMEM((table.shape[1], LANES), f32),
        ],
        compiler_params=pltpu.CompilerParams(vmem_limit_bytes=24 * 2**20),
        name="inverse",
    )(classes, table, coef, maps)


def column_kernel(
    weight_ref, in_ref, cos_ref, sin_ref, w_in_ref, bias_ref, w_hid_ref, w_out_ref,
    out_ref, fourier_ref, tendency_ref, sums_ref, scr_ref, *, x_rows, width,
):
    peers = in_ref.shape[0] // 8

    def put(part, i, m, slab):
        fourier_ref[part, m * peers : (m + 1) * peers, i * LANES : (i + 1) * LANES] = slab.astype(
            bf16
        )

    unpack_rows(in_ref, scr_ref, put, peers, width)

    def grid_rows(step, carry):
        rows = pl.ds(pl.multiple_of(step * x_rows, x_rows), x_rows)
        raw = dot(cos_ref[rows, :], fourier_ref[0]) + dot(sin_ref[rows, :], fourier_ref[1])
        features = (transform_scale * raw).astype(bf16)
        lanes = [slice(i * LANES, (i + 1) * LANES) for i in range(OWN)]
        hidden = [half_silu(dot(features[:, at], w_in_ref[...]) + bias_ref[...]) for at in lanes]
        hidden = [h.astype(bf16) for h in hidden]
        for layer in range(w_hid_ref.shape[0]):
            update = [half_silu(dot(h, w_hid_ref[layer])) for h in hidden]
            hidden = [(h.astype(f32) + u).astype(bf16) for h, u in zip(hidden, update)]
        for at, h in zip(lanes, hidden):
            tendency_ref[rows, at] = dot(h, w_out_ref[...]).astype(bf16)
        return carry

    lax.fori_loop(0, NLON // x_rows, grid_rows, 0)

    for part, table_ref in enumerate((cos_ref, sin_ref)):
        sums = lax.dot_general(
            tendency_ref[...],
            table_ref[...],
            (((0,), (0,)), ((), ())),
            preferred_element_type=f32,
        )
        for i in range(OWN):
            weight = weight_ref[i] * transform_scale
            for m in range(OWN):
                block = sums[i * LANES : (i + 1) * LANES, m * peers : (m + 1) * peers]
                sums_ref[part, i, m] = weight * block.T

    slab_of = lambda part, i, m: sums_ref[part, i, m]
    pack_rows(slab_of, out_ref, scr_ref, peers, width)


def columns(weights, fourier, cosines, sines, w_in, bias, w_hid, w_out, width):
    peers = fourier.shape[0] // 8
    vmem = pl.BlockSpec(memory_space=pltpu.VMEM)
    return pl.pallas_call(
        functools.partial(column_kernel, x_rows=X_ROWS, width=width),
        in_specs=[pl.BlockSpec(memory_space=pltpu.SMEM)] + [vmem] * 7,
        out_specs=vmem,
        out_shape=jax.ShapeDtypeStruct(fourier.shape, bf16),
        scratch_shapes=[
            pltpu.VMEM((2, OWN * peers, OWN * LANES), bf16),
            pltpu.VMEM((NLON, OWN * LANES), bf16),
            pltpu.VMEM((2, OWN, OWN, peers, LANES), f32),
            pltpu.VMEM((2, peers * 8, LANES), f32),
        ],
        compiler_params=pltpu.CompilerParams(vmem_limit_bytes=40 * 2**20),
        name="columns",
    )(weights, fourier, cosines, sines, w_in, bias, w_hid, w_out)


def forward_kernel(
    class_ref, in_ref, table_ref, maps_ref, out_ref, sums_ref, scr_ref, sent_ref, full_ref,
    *, lats, lat_local, lat_slots, width,
):
    peers = in_ref.shape[0] // 8

    def put(part, i, m, slab):
        sums_ref[m, part, pl.ds(i, peers, OWN), :] = slab

    unpack_rows(in_ref, scr_ref, put, peers, width)
    lanes = table_ref.shape[-1]
    sent = out_ref.shape[3]
    rows = full_ref.shape[0] // lats
    spare = spare_lanes((lats, LANES), width)
    for m in range(OWN):
        weighted = jnp.concatenate(
            [
                jnp.concatenate(
                    [
                        sums_ref[m, part, lat * lat_slots : lat * lat_slots + lat_local, :]
                        for lat in range(lats)
                    ]
                    + [jnp.zeros((lanes - lats * lat_local, LANES), f32)]
                )
                for part in range(2)
            ],
            axis=1,
        ).astype(bf16)
        forcing = dot(table_ref[m], weighted).astype(bf16)
        for v in range(maps_ref.shape[0]):
            full_ref[...] = dot(forcing, maps_ref[v])
            for b in range(sent // 8):
                last = full_ref[pl.ds(sent + b, lats, rows), :]
                for t in range(8):
                    main = full_ref[pl.ds(8 * b + t, lats, rows), :]
                    sent_ref[pl.ds(8 * b + t, lats, sent), :] = jnp.where(
                        spare, scatter_last(last, t, width), main
                    )
            for q in range(lats):
                k, x = divmod(q, LAT_X)
                piece = sent_ref[q * sent : (q + 1) * sent, :].astype(bf16)
                out_ref[x * Z_LOW + class_ref[k], v, m] = piece


def forward(classes, weighted, table, maps, peers, lats, sent, lat_local, lat_slots, width):
    levs = maps.shape[0]
    vmem = pl.BlockSpec(memory_space=pltpu.VMEM)
    return pl.pallas_call(
        functools.partial(
            forward_kernel, lats=lats, lat_local=lat_local, lat_slots=lat_slots, width=width
        ),
        in_specs=[pl.BlockSpec(memory_space=pltpu.SMEM), vmem, vmem, vmem],
        out_specs=vmem,
        out_shape=jax.ShapeDtypeStruct((lats, levs, OWN, sent, LANES), bf16),
        scratch_shapes=[
            pltpu.VMEM((OWN, 2, lats * lat_slots, LANES), f32),
            pltpu.VMEM((2, peers * 8, LANES), f32),
            pltpu.VMEM((lats * sent, LANES), f32),
            pltpu.VMEM((table.shape[1], LANES), f32),
        ],
        compiler_params=pltpu.CompilerParams(vmem_limit_bytes=24 * 2**20),
        name="forward",
    )(classes, weighted, table, maps)


def turn_maps(channels):
    maps = np.zeros((8, 2 * channels, LANES), np.float32)
    for t in range(8):
        maps[t, np.arange(channels), np.arange(channels)] = 1.0
        piece = np.arange(SPARE)
        maps[t, channels + SPARE * t + piece, channels + piece] = 1.0
    return jnp.asarray(maps, bf16)


def update_kernel(at_ref, damping_ref, state_ref, forcing_ref, maps_ref, out_ref, scr_ref):
    degrees, channels, orders = state_ref.shape
    order = lax.broadcasted_iota(jnp.int32, (channels, orders), 1) + at_ref[0]

    def put(degree, forcing):
        new = (state_ref[degree] + time_step * forcing) * damping_ref[degree]
        out_ref[degree] = jnp.where(degree + at_ref[1] >= order, new, 0.0)

    sent = forcing_ref.shape[2]
    for b in range(sent // 8):
        for x in range(LAT_X):
            skip = OWN * (first_group(x - 1) + Z_RING - first_group(x)) if x else 0
            first = (OWN * first_group(x) + skip) * 8
            mine = forcing_ref[x, skip:, 8 * b : 8 * b + 8, :].astype(f32)
            scr_ref[b, first : first + mine.shape[0] * 8, :] = mine.reshape(-1, LANES)
        last = 0.0
        for t in range(8):
            turned = lax.dot_general(
                maps_ref[t],
                scr_ref[b, pl.ds(t, orders, 8), :].astype(bf16),
                (((1,), (1,)), ((), ())),
                preferred_element_type=f32,
            )
            put(8 * b + t, turned[:channels])
            last += turned[channels:]
        put(sent + b, last)


def update(at, damping, state, forcing):
    degrees, channels, orders = state.shape
    _, _, sent, _ = forcing.shape
    smem, vmem = (pl.BlockSpec(memory_space=m) for m in (pltpu.SMEM, pltpu.VMEM))
    return pl.pallas_call(
        update_kernel,
        in_specs=[smem, smem, vmem, vmem, vmem],
        out_specs=vmem,
        out_shape=jax.ShapeDtypeStruct(state.shape, f32),
        scratch_shapes=[pltpu.VMEM((sent // 8, orders * 8, LANES), f32)],
        compiler_params=pltpu.CompilerParams(vmem_limit_bytes=24 * 2**20),
        name="update",
    )(at, damping, state, forcing, turn_maps(channels))


def shifted(value, x_step, z_step):
    pairs = []
    flat = lambda x, z: x * Z_RING + 2 * (z % Z_LOW) + z // Z_LOW
    for x in range(LAT_X):
        to_x = (x + x_step) % LAT_X
        pairs += [(flat(x, z), flat(to_x, (z + z_step) % Z_RING)) for z in range(Z_RING)]
    return lax.ppermute(value, ("lat", "lev"), pairs)


def along_z(value, step):
    return shifted(value, 0, step)


def along_x(value):
    groups = [[x * Z_LOW + z for x in range(LAT_X)] for z in range(Z_LOW)]
    return lax.all_to_all(value, "lat", 0, 0, axis_index_groups=groups, tiled=True)


def on_device(spectral_state, legendre, quad_weight, weight_in, bias_in, weight_hidden, weight_out):
    ord_size, lat_size, lev_size = (lax.axis_size(a) for a in ("ord", "lat", "lev"))
    ord_at, lat_at, lev_at = (lax.axis_index(a) for a in ("ord", "lat", "lev"))
    order_local, degree_local = spectral_state.shape[:2]
    lat_local = quad_weight.shape[0]
    row_local = spectral_state.shape[2] * spectral_state.shape[3]
    channels = 2 * row_local
    width = lev_size * row_local
    rows = -(-degree_local // 16) * 16
    sent = degree_local // 8 * 8
    peers = ord_size * lat_size * lev_size
    lat_slots = ord_size * lev_size * OWN
    everyone = ("lat", "ord", "lev")
    at = jnp.stack([ord_at * order_local, lat_at * degree_local]).astype(jnp.int32)
    maps = lane_maps(lev_size, row_local)
    state = spectral_state.transpose(1, 2, 3, 4, 0).reshape(degree_local, channels, order_local)

    z_at = lev_at * Z_LOW + lat_at % Z_LOW
    x_at = lat_at // Z_LOW
    ring = (z_at + jnp.array([0, 1, -1, 2, -2], jnp.int32)) % Z_RING
    own = OWN * (2 * (ring % Z_LOW) + ring // Z_LOW)
    meta = jnp.concatenate([x_at[None], own]).astype(jnp.int32)
    a_all, b_own, *b_rest = pack_table(meta, legendre, HALF, rows)
    b_left, b_right, b_low, b_high = (along_z(v, k) for v, k in zip(b_rest, (1, -1, 2, -2)))
    a_all = along_x(a_all)
    b_far = jnp.concatenate([b_low, b_high], axis=2)
    b_all = [jnp.stack([v[d] for v in (b_own, b_left, b_right, b_far)]) for d in range(LAT_X)]
    coefficients = prep(at, state, sent)
    a_all, b_all, coefficients = lax.optimization_barrier((a_all, b_all, coefficients))
    a_near = [along_z(a_all[:, 1], 1), along_z(a_all[:, 2], -1)]
    a_far = [along_z(a_all[:, 3, :, : rows // 2], 2), along_z(a_all[:, 3, :, rows // 2 :], -2)]
    b_all = [b_all[0]] + [shifted(b_all[d], step, 0) for d, step in ((1, 1), (2, 2), (3, -1))]
    sources = (x_at - jnp.arange(LAT_X, dtype=jnp.int32)) % LAT_X

    slot = lax.iota(jnp.int32, OWN * peers)
    slot_lev = slot % lev_size
    slot_ord = slot // lev_size % ord_size
    slot_lat = slot // (lev_size * ord_size) % lat_size
    slot_x, slot_w = slot_lat // Z_LOW, 2 * (slot_lat % Z_LOW) + slot_lev
    valid = (slot_x % 2 == 0) | (slot_w > 0)
    order_ids = slot_ord * order_local + OWN * (first_group(slot_x) + slot_w) + slot // peers
    coefficients = coefficients.reshape(lat_size * lev_size, OWN, sent, LANES)
    coefficients = lax.all_to_all(coefficients, ("lat", "lev"), 0, 0, tiled=True)
    coefficients = coefficients.reshape(lat_size, lev_size, OWN, sent, LANES)
    classes = (z_at + jnp.array([0, -1, 1, 2], jnp.int32)) % Z_LOW
    table = assemble(sources, a_all, a_near, a_far, b_all)
    fourier = inverse(classes, table, coefficients, maps, peers, lat_local, lat_slots, width)
    fourier, order_ids, valid = lax.optimization_barrier((fourier, order_ids, valid))
    cosines, sines = lookup_of(order_ids, valid)

    fourier = lax.all_to_all(fourier.reshape(peers, 8, -1), everyone, 0, 0, tiled=True)
    first = (ord_at * lev_size + lev_at) * OWN
    weights = lax.dynamic_slice_in_dim(jnp.pad(quad_weight, (0, lat_slots - lat_local)), first, OWN)
    weighted = columns(
        weights,
        fourier.reshape(peers * 8, -1),
        cosines,
        sines,
        jnp.pad(0.5 * weight_in, ((0, LANES - width), (0, 0))),
        0.5 * bias_in[None, :],
        0.5 * weight_hidden,
        jnp.pad(weight_out, ((0, 0), (0, LANES - width))),
        width,
    )

    weighted = lax.all_to_all(weighted.reshape(peers, 8, -1), everyone, 0, 0, tiled=True)
    weighted = weighted.reshape(peers * 8, -1)
    forcing = forward(
        classes, weighted, table, maps, peers, lat_size, sent, lat_local, lat_slots, width
    )
    forcing = forcing.reshape(lat_size * lev_size, OWN, sent, LANES)
    forcing = lax.all_to_all(forcing, ("lat", "lev"), 0, 0, tiled=True)
    forcing = forcing.reshape(LAT_X, OWN * Z_RING, sent, LANES)
    degree_ids = lat_at * degree_local + lax.iota(jnp.int32, degree_local)
    degree_ratio = (degree_ids * (degree_ids + 1)).astype(f32) / ((L - 1) * L)
    damping = 1.0 / (1.0 + hyper_rate * degree_ratio * degree_ratio)
    updated = update(at, damping, state, forcing)
    updated = updated.reshape(degree_local, *spectral_state.shape[2:], order_local)
    return updated.transpose(4, 0, 1, 2, 3)


def solution(mesh):
    return jax.shard_map(
        on_device,
        mesh=mesh,
        in_specs=(
            P("ord", "lat", "lev", None, None),
            P("ord", "lat", None),
            P("lat"),
            P(),
            P(),
            P(),
            P(),
        ),
        out_specs=P("ord", "lat", "lev", None, None),
        check_vma=False,
    )
```

```python
import functools
import math

import jax
import jax.numpy as jnp
import numpy as np
from jax import lax
from jax.experimental import pallas as pl
from jax.experimental.pallas import tpu as pltpu
from jax.sharding import PartitionSpec as P

L = 720
NLON = 1440
OWN = 3
LANES = 128
LAT_X, Z_LOW, Z_RING = 4, 4, 8
HALF = 384
X_ROWS = 1440
SPARE = 14

time_step = 1.0
hyper_rate = 2.0
transform_scale = math.sqrt(2.0 / NLON)

f32, bf16 = jnp.float32, jnp.bfloat16
dot = functools.partial(jnp.dot, preferred_element_type=jnp.float32)


def first_group(x):
    return (22 * x + 1) // 3


def lookup_of(order_ids, valid):
    low = 32

    def waves(x):
        phase_index = order_ids[None, :] * x[:, None] % NLON
        angles = 2.0 * math.pi / NLON * phase_index.astype(f32)
        return jnp.cos(angles), jnp.sin(angles)

    high_cos, high_sin = waves(low * lax.iota(jnp.int32, NLON // low))
    high_cos = jnp.where(valid[None, :], high_cos, 0.0)[:, None]
    high_sin = jnp.where(valid[None, :], high_sin, 0.0)[:, None]
    low_cos, low_sin = (w[None] for w in waves(lax.iota(jnp.int32, low)))
    cosines = high_cos * low_cos - high_sin * low_sin
    sines = -(high_sin * low_cos + high_cos * low_sin)
    shape = (NLON, order_ids.shape[0])
    return cosines.astype(bf16).reshape(shape), sines.astype(bf16).reshape(shape)


def half_silu(u):
    return u + u * jnp.tanh(u)


def lane_maps(levs, row_local):
    maps = np.zeros((levs, 2 * LANES, LANES), np.float32)
    for lev in range(levs):
        for row in range(row_local):
            for part in range(2):
                maps[lev, part * LANES + lev * row_local + row, 2 * row + part] = 1.0
    return jnp.asarray(maps, bf16)


def pack_rows(slab_of, out_ref, scr_ref, peers, width):
    lane = lax.broadcasted_iota(jnp.int32, (peers, LANES), 1)
    spare = (lane >= width) & (lane < width + SPARE)
    for part in range(2):
        last = slab_of(part, 2, 2)
        for k in range(8):
            moved = pltpu.roll(last, (width - SPARE * k) % LANES, 1)
            scr_ref[part, pl.ds(k, peers, 8), :] = jnp.where(
                spare, moved, slab_of(part, k // OWN, k % OWN)
            )
        out_ref[:, part * LANES : (part + 1) * LANES] = scr_ref[part].astype(bf16)


def unpack_rows(in_ref, scr_ref, put_slab, peers, width):
    lane = lax.broadcasted_iota(jnp.int32, (peers, LANES), 1)
    for part in range(2):
        scr_ref[part] = in_ref[:, part * LANES : (part + 1) * LANES].astype(f32)
        last = jnp.zeros((peers, LANES), f32)
        for k in range(8):
            slab = scr_ref[part, pl.ds(k, peers, 8), :]
            put_slab(part, k // OWN, k % OWN, slab)
            moved = pltpu.roll(slab, (SPARE * k - width) % LANES, 1)
            last = jnp.where((lane >= SPARE * k) & (lane < SPARE * (k + 1)), moved, last)
        put_slab(part, 2, 2, last)


def spare_lanes(shape, width):
    lane = lax.broadcasted_iota(jnp.int32, shape, len(shape) - 1)
    return (lane >= width) & (lane < width + SPARE)


def scatter_last(row, t, width):
    return pltpu.roll(row, (width - SPARE * t) % LANES, 1)


def gather_last(last, slab, t, width):
    lane = lax.broadcasted_iota(jnp.int32, slab.shape, 1)
    moved = pltpu.roll(slab, (SPARE * t - width) % LANES, 1)
    return jnp.where((lane >= SPARE * t) & (lane < SPARE * (t + 1)), moved, last)


def wide(value):
    return jnp.pad(value, ((0, 0), (0, LANES - value.shape[1])))


def prep_kernel(at_ref, state_ref, last_ref, out_ref, scr_ref):
    _, channels, orders = state_ref.shape
    group, rows = out_ref.shape[1], 8 * pl.num_programs(0)
    b = pl.program_id(0)
    order = lax.broadcasted_iota(jnp.int32, (channels, orders), 1) + at_ref[0]
    masked = lambda value, degree: wide(jnp.where(degree + at_ref[1] >= order, value, 0.0).T)
    last = masked(last_ref[b], rows + b)
    spare = spare_lanes(last.shape, channels)
    for t in range(8):
        scr_ref[pl.ds(t, orders, 8), :] = jnp.where(
            spare, scatter_last(last, t, channels), masked(state_ref[t], 8 * b + t)
        )
    packed = scr_ref[...].astype(bf16).reshape(orders, 8, LANES)
    for x in range(LAT_X):
        first = OWN * first_group(x)
        out_ref[x] = packed[first : first + group]


def prep(at, state, rows):
    group = OWN * Z_RING
    _, channels, orders = state.shape
    steps = rows // 8
    return pl.pallas_call(
        prep_kernel,
        grid=(steps,),
        in_specs=[
            pl.BlockSpec(memory_space=pltpu.SMEM),
            pl.BlockSpec((8, channels, orders), lambda i: (i, 0, 0)),
            pl.BlockSpec((8, channels, orders), lambda i: (steps, 0, 0)),
        ],
        out_specs=pl.BlockSpec((LAT_X, group, 8, LANES), lambda i: (0, 0, i, 0)),
        out_shape=jax.ShapeDtypeStruct((LAT_X, group, rows, LANES), bf16),
        scratch_shapes=[pltpu.VMEM((orders * 8, LANES), f32)],
        cost_estimate=pl.CostEstimate(flops=10**6, bytes_accessed=4 * 10**6, transcendentals=0),
        name="prep",
    )(at, state, state)


def pack_kernel(own_ref, in_ref, a_ref, *b_refs):
    degrees, lats = in_ref.shape[1:]
    half, rows = a_ref.shape[-1], a_ref.shape[-2]
    split = rows // 2
    a_ref[...] = jnp.zeros_like(a_ref)
    for ref in b_refs:
        ref[...] = jnp.zeros_like(ref)
    for k in range(3):
        mine = in_ref[pl.ds(own_ref[k], OWN)]
        a_ref[0, k, :, :degrees, :] = mine[:, :, :half]
        b_refs[k][0, :, :degrees, : lats - half] = mine[:, :, half:]
    mine = in_ref[pl.ds(own_ref[3], OWN)]
    a_ref[0, 3, :, :split, :] = mine[:, :split, :half]
    b_refs[3][0, :, :, : lats - half] = mine[:, :split, half:]
    mine = in_ref[pl.ds(own_ref[4], OWN)]
    a_ref[0, 3, :, split:degrees, :] = mine[:, split:, :half]
    b_refs[4][0, :, : degrees - split, : lats - half] = mine[:, split:, half:]


def pack_table(own, legendre, half, rows):
    _, degrees, lats = legendre.shape
    group = OWN * Z_RING
    b_shape = lambda r: jax.ShapeDtypeStruct((LAT_X, OWN, r, half), bf16)
    b_spec = lambda r: pl.BlockSpec((1, OWN, r, half), lambda x: (x, 0, 0, 0))
    b_rows = (rows, rows, rows, rows // 2, rows // 2)
    return pl.pallas_call(
        pack_kernel,
        grid=(LAT_X,),
        in_specs=[
            pl.BlockSpec(memory_space=pltpu.SMEM),
            pl.BlockSpec(
                (pl.Element(group), pl.Element(degrees), pl.Element(lats)),
                lambda x: (OWN * first_group(x), 0, 0),
            ),
        ],
        out_specs=[pl.BlockSpec((1, 4, OWN, rows, half), lambda x: (x, 0, 0, 0, 0))]
        + [b_spec(r) for r in b_rows],
        out_shape=[jax.ShapeDtypeStruct((LAT_X, 4, OWN, rows, half), bf16)]
        + [b_shape(r) for r in b_rows],
        compiler_params=pltpu.CompilerParams(vmem_limit_bytes=60 * 2**20),
        name="pack_table",
    )(own, legendre)


def assemble_kernel(a_own_ref, a_left_ref, a_right_ref, a_low_ref, a_high_ref, b_ref, out_ref):
    rows, half = b_ref.shape[-2:]
    place = LAT_X * rows
    far = jnp.concatenate([a_low_ref[...], a_high_ref[...]], axis=1)
    for k, piece in enumerate((a_own_ref[:, 0], a_left_ref[...], a_right_ref[...], far)):
        out_ref[0, k * place : (k + 1) * place, :half] = piece.reshape(place, half)
        out_ref[0, k * place : (k + 1) * place, half:] = b_ref[:, k].reshape(place, half)


def assemble(a_own, a_near, a_far, b_all):
    rows, half = b_all.shape[-2:]
    size = 4 * LAT_X * rows
    near = pl.BlockSpec((LAT_X, None, rows, half), lambda m: (0, m, 0, 0))
    far = pl.BlockSpec((LAT_X, None, rows // 2, half), lambda m: (0, m, 0, 0))
    return pl.pallas_call(
        assemble_kernel,
        grid=(OWN,),
        in_specs=[
            pl.BlockSpec((LAT_X, 1, None, rows, half), lambda m: (0, 0, m, 0, 0)),
            near,
            near,
            far,
            far,
            pl.BlockSpec((LAT_X, 4, None, rows, half), lambda m: (0, 0, m, 0, 0)),
        ],
        out_specs=pl.BlockSpec((1, size, 2 * half), lambda m: (m, 0, 0)),
        out_shape=jax.ShapeDtypeStruct((OWN, size, 2 * half), bf16),
        cost_estimate=pl.CostEstimate(flops=10**6, bytes_accessed=8 * 10**6, transcendentals=0),
        name="assemble",
    )(a_own, *a_near, *a_far, b_all)


def inverse_kernel(
    class_ref, table_ref, coef_ref, maps_ref, out_ref, sums_ref, scr_ref, sent_ref, full_ref,
    *, lats, lat_local, lat_slots, width,
):
    sent = coef_ref.shape[3]
    rows = full_ref.shape[0] // lats
    for m in range(OWN):
        swapped = 0.0
        for v in range(maps_ref.shape[0]):
            for q in range(lats):
                k, x = divmod(q, LAT_X)
                piece = coef_ref[x * Z_LOW + class_ref[k], v, m].astype(f32)
                sent_ref[q * sent : (q + 1) * sent, :] = piece
                full_ref[q * rows : q * rows + sent, :] = piece
                full_ref[q * rows + sent : (q + 1) * rows, :] = jnp.zeros((rows - sent, LANES), f32)
            for b in range(sent // 8):
                last = jnp.zeros((lats, LANES), f32)
                for t in range(8):
                    slab = sent_ref[pl.ds(8 * b + t, lats, sent), :]
                    last = gather_last(last, slab, t, width)
                full_ref[pl.ds(sent + b, lats, rows), :] = last
            swapped += lax.dot_general(
                maps_ref[v],
                full_ref[...].astype(bf16),
                (((1,), (1,)), ((), ())),
                preferred_element_type=f32,
            )
        sums = dot(swapped.astype(bf16), table_ref[m]).T
        for part in range(2):
            lanes = slice(part * LANES, (part + 1) * LANES)
            for lat in range(lats):
                first = lat * lat_slots
                sums_ref[m, part, first : first + lat_local, :] = sums[
                    lat * lat_local : (lat + 1) * lat_local, lanes
                ]
                sums_ref[m, part, first + lat_local : first + lat_slots, :] = jnp.zeros(
                    (lat_slots - lat_local, LANES), f32
                )

    peers = out_ref.shape[0] // 8
    slab_of = lambda part, i, m: sums_ref[m, part, pl.ds(i, peers, OWN), :]
    pack_rows(slab_of, out_ref, scr_ref, peers, width)


def inverse(classes, table, coef, maps, peers, lat_local, lat_slots, width):
    lats, _, _, sent, _ = coef.shape
    vmem = pl.BlockSpec(memory_space=pltpu.VMEM)
    return pl.pallas_call(
        functools.partial(
            inverse_kernel, lats=lats, lat_local=lat_local, lat_slots=lat_slots, width=width
        ),
        in_specs=[pl.BlockSpec(memory_space=pltpu.SMEM), vmem, vmem, vmem],
        out_specs=vmem,
        out_shape=jax.ShapeDtypeStruct((peers * 8, 2 * LANES), bf16),
        scratch_shapes=[
            pltpu.VMEM((OWN, 2, lats * lat_slots, LANES), f32),
            pltpu.VMEM((2, peers * 8, LANES), f32),
            pltpu.VMEM((lats * sent, LANES), f32),
            pltpu.VMEM((table.shape[1], LANES), f32),
        ],
        compiler_params=pltpu.CompilerParams(vmem_limit_bytes=24 * 2**20),
        name="inverse",
    )(classes, table, coef, maps)


def column_kernel(
    weight_ref, in_ref, cos_ref, sin_ref, w_in_ref, bias_ref, w_hid_ref, w_out_ref,
    out_ref, fourier_ref, tendency_ref, sums_ref, scr_ref, *, x_rows, width,
):
    peers = in_ref.shape[0] // 8

    def put(part, i, m, slab):
        fourier_ref[part, m * peers : (m + 1) * peers, i * LANES : (i + 1) * LANES] = slab.astype(
            bf16
        )

    unpack_rows(in_ref, scr_ref, put, peers, width)

    half_in, half_bias = 0.5 * w_in_ref[...], 0.5 * bias_ref[...]
    half_hid = [0.5 * w_hid_ref[layer] for layer in range(w_hid_ref.shape[0])]

    def grid_rows(step, carry):
        rows = pl.ds(pl.multiple_of(step * x_rows, x_rows), x_rows)
        raw = dot(cos_ref[rows, :], fourier_ref[0]) + dot(sin_ref[rows, :], fourier_ref[1])
        features = (transform_scale * raw).astype(bf16)
        lanes = [slice(i * LANES, (i + 1) * LANES) for i in range(OWN)]
        hidden = [half_silu(dot(features[:, at], half_in) + half_bias) for at in lanes]
        hidden = [h.astype(bf16) for h in hidden]
        for weights in half_hid:
            update = [half_silu(dot(h, weights)) for h in hidden]
            hidden = [(h.astype(f32) + u).astype(bf16) for h, u in zip(hidden, update)]
        for at, h in zip(lanes, hidden):
            tendency_ref[rows, at] = dot(h, w_out_ref[...]).astype(bf16)
        return carry

    lax.fori_loop(0, NLON // x_rows, grid_rows, 0)

    for part, table_ref in enumerate((cos_ref, sin_ref)):
        sums = lax.dot_general(
            tendency_ref[...],
            table_ref[...],
            (((0,), (0,)), ((), ())),
            preferred_element_type=f32,
        )
        for i in range(OWN):
            weight = weight_ref[i] * transform_scale
            for m in range(OWN):
                block = sums[i * LANES : (i + 1) * LANES, m * peers : (m + 1) * peers]
                sums_ref[part, i, m] = weight * block.T

    slab_of = lambda part, i, m: sums_ref[part, i, m]
    pack_rows(slab_of, out_ref, scr_ref, peers, width)


def columns(weights, fourier, cosines, sines, w_in, bias, w_hid, w_out, width):
    peers = fourier.shape[0] // 8
    vmem = pl.BlockSpec(memory_space=pltpu.VMEM)
    return pl.pallas_call(
        functools.partial(column_kernel, x_rows=X_ROWS, width=width),
        in_specs=[pl.BlockSpec(memory_space=pltpu.SMEM)] + [vmem] * 7,
        out_specs=vmem,
        out_shape=jax.ShapeDtypeStruct(fourier.shape, bf16),
        scratch_shapes=[
            pltpu.VMEM((2, OWN * peers, OWN * LANES), bf16),
            pltpu.VMEM((NLON, OWN * LANES), bf16),
            pltpu.VMEM((2, OWN, OWN, peers, LANES), f32),
            pltpu.VMEM((2, peers * 8, LANES), f32),
        ],
        compiler_params=pltpu.CompilerParams(vmem_limit_bytes=26 * 2**20),
        name="columns",
    )(weights, fourier, cosines, sines, w_in, bias, w_hid, w_out)


def forward_kernel(
    class_ref, in_ref, table_ref, maps_ref, out_ref, sums_ref, scr_ref, sent_ref, full_ref,
    *, lats, lat_local, lat_slots, width,
):
    peers = in_ref.shape[0] // 8

    def put(part, i, m, slab):
        sums_ref[m, part, pl.ds(i, peers, OWN), :] = slab

    unpack_rows(in_ref, scr_ref, put, peers, width)
    lanes = table_ref.shape[-1]
    sent = out_ref.shape[3]
    rows = full_ref.shape[0] // lats
    spare = spare_lanes((lats, LANES), width)
    for m in range(OWN):
        weighted = jnp.concatenate(
            [
                jnp.concatenate(
                    [
                        sums_ref[m, part, lat * lat_slots : lat * lat_slots + lat_local, :]
                        for lat in range(lats)
                    ]
                    + [jnp.zeros((lanes - lats * lat_local, LANES), f32)]
                )
                for part in range(2)
            ],
            axis=1,
        ).astype(bf16)
        forcing = dot(table_ref[m], weighted).astype(bf16)
        for v in range(maps_ref.shape[0]):
            full_ref[...] = dot(forcing, maps_ref[v])
            for b in range(sent // 8):
                last = full_ref[pl.ds(sent + b, lats, rows), :]
                for t in range(8):
                    main = full_ref[pl.ds(8 * b + t, lats, rows), :]
                    sent_ref[pl.ds(8 * b + t, lats, sent), :] = jnp.where(
                        spare, scatter_last(last, t, width), main
                    )
            for q in range(lats):
                k, x = divmod(q, LAT_X)
                piece = sent_ref[q * sent : (q + 1) * sent, :].astype(bf16)
                out_ref[x * Z_LOW + class_ref[k], v, m] = piece


def forward(classes, weighted, table, maps, peers, lats, sent, lat_local, lat_slots, width):
    levs = maps.shape[0]
    vmem = pl.BlockSpec(memory_space=pltpu.VMEM)
    return pl.pallas_call(
        functools.partial(
            forward_kernel, lats=lats, lat_local=lat_local, lat_slots=lat_slots, width=width
        ),
        in_specs=[pl.BlockSpec(memory_space=pltpu.SMEM), vmem, vmem, vmem],
        out_specs=vmem,
        out_shape=jax.ShapeDtypeStruct((lats, levs, OWN, sent, LANES), bf16),
        scratch_shapes=[
            pltpu.VMEM((OWN, 2, lats * lat_slots, LANES), f32),
            pltpu.VMEM((2, peers * 8, LANES), f32),
            pltpu.VMEM((lats * sent, LANES), f32),
            pltpu.VMEM((table.shape[1], LANES), f32),
        ],
        compiler_params=pltpu.CompilerParams(vmem_limit_bytes=24 * 2**20),
        name="forward",
    )(classes, weighted, table, maps)


def turn_maps(channels):
    maps = np.zeros((8, 2 * channels, LANES), np.float32)
    for t in range(8):
        maps[t, np.arange(channels), np.arange(channels)] = 1.0
        piece = np.arange(SPARE)
        maps[t, channels + SPARE * t + piece, channels + piece] = 1.0
    return jnp.asarray(maps, bf16)


def update_kernel(at_ref, damping_ref, state_ref, forcing_ref, maps_ref, out_ref, scr_ref):
    degrees, channels, orders = state_ref.shape
    order = lax.broadcasted_iota(jnp.int32, (channels, orders), 1) + at_ref[0]

    def put(degree, forcing):
        new = (state_ref[degree] + time_step * forcing) * damping_ref[degree]
        out_ref[degree] = jnp.where(degree + at_ref[1] >= order, new, 0.0)

    sent = forcing_ref.shape[2]
    for b in range(sent // 8):
        for x in range(LAT_X):
            skip = OWN * (first_group(x - 1) + Z_RING - first_group(x)) if x else 0
            first = (OWN * first_group(x) + skip) * 8
            mine = forcing_ref[x, skip:, 8 * b : 8 * b + 8, :].astype(f32)
            scr_ref[b, first : first + mine.shape[0] * 8, :] = mine.reshape(-1, LANES)
        last = 0.0
        for t in range(8):
            turned = lax.dot_general(
                maps_ref[t],
                scr_ref[b, pl.ds(t, orders, 8), :].astype(bf16),
                (((1,), (1,)), ((), ())),
                preferred_element_type=f32,
            )
            put(8 * b + t, turned[:channels])
            last += turned[channels:]
        put(sent + b, last)


def update(at, damping, state, forcing):
    degrees, channels, orders = state.shape
    _, _, sent, _ = forcing.shape
    smem, vmem = (pl.BlockSpec(memory_space=m) for m in (pltpu.SMEM, pltpu.VMEM))
    return pl.pallas_call(
        update_kernel,
        in_specs=[smem, smem, vmem, vmem, vmem],
        out_specs=vmem,
        out_shape=jax.ShapeDtypeStruct(state.shape, f32),
        scratch_shapes=[pltpu.VMEM((sent // 8, orders * 8, LANES), f32)],
        compiler_params=pltpu.CompilerParams(vmem_limit_bytes=24 * 2**20),
        name="update",
    )(at, damping, state, forcing, turn_maps(channels))


def along_z(value, step):
    pairs = []
    flat = lambda x, z: x * Z_RING + 2 * (z % Z_LOW) + z // Z_LOW
    for x in range(LAT_X):
        pairs += [(flat(x, z), flat(x, (z + step) % Z_RING)) for z in range(Z_RING)]
    return lax.ppermute(value, ("lat", "lev"), pairs)


def along_x(value):
    groups = [[x * Z_LOW + z for x in range(LAT_X)] for z in range(Z_LOW)]
    return lax.all_to_all(value, "lat", 0, 0, axis_index_groups=groups, tiled=True)


def on_device(spectral_state, legendre, quad_weight, weight_in, bias_in, weight_hidden, weight_out):
    ord_size, lat_size, lev_size = (lax.axis_size(a) for a in ("ord", "lat", "lev"))
    ord_at, lat_at, lev_at = (lax.axis_index(a) for a in ("ord", "lat", "lev"))
    order_local, degree_local = spectral_state.shape[:2]
    lat_local = quad_weight.shape[0]
    row_local = spectral_state.shape[2] * spectral_state.shape[3]
    channels = 2 * row_local
    width = lev_size * row_local
    rows = -(-degree_local // 16) * 16
    sent = degree_local // 8 * 8
    peers = ord_size * lat_size * lev_size
    lat_slots = ord_size * lev_size * OWN
    everyone = ("lat", "ord", "lev")
    at = jnp.stack([ord_at * order_local, lat_at * degree_local]).astype(jnp.int32)
    maps = lane_maps(lev_size, row_local)
    state = spectral_state.transpose(1, 2, 3, 4, 0).reshape(degree_local, channels, order_local)

    z_at = lev_at * Z_LOW + lat_at % Z_LOW
    ring = (z_at + jnp.array([0, 1, -1, 2, -2], jnp.int32)) % Z_RING
    own = OWN * (2 * (ring % Z_LOW) + ring // Z_LOW)
    a_all, b_own, *b_rest = pack_table(own, legendre, HALF, rows)
    b_left, b_right, b_low, b_high = (along_z(v, k) for v, k in zip(b_rest, (1, -1, 2, -2)))
    a_all = along_x(a_all)
    b_far = jnp.concatenate([b_low, b_high], axis=2)
    b_all = jnp.stack([b_own, b_left, b_right, b_far], axis=1)
    a_all, b_all = lax.optimization_barrier((a_all, b_all))
    a_cut = [a_all[:, 1], a_all[:, 2], a_all[:, 3, :, : rows // 2], a_all[:, 3, :, rows // 2 :]]
    a_cut, b_all = lax.optimization_barrier((a_cut, b_all))
    a_near = [along_z(a_cut[0], 1), along_z(a_cut[1], -1)]
    a_far = [along_z(a_cut[2], 2), along_z(a_cut[3], -2)]
    b_all = along_x(b_all)

    slot = lax.iota(jnp.int32, OWN * peers)
    slot_lev = slot % lev_size
    slot_ord = slot // lev_size % ord_size
    slot_lat = slot // (lev_size * ord_size) % lat_size
    slot_x, slot_w = slot_lat // Z_LOW, 2 * (slot_lat % Z_LOW) + slot_lev
    valid = (slot_x % 2 == 0) | (slot_w > 0)
    order_ids = slot_ord * order_local + OWN * (first_group(slot_x) + slot_w) + slot // peers
    coefficients = prep(at, state, sent)
    coefficients, a_near, a_far, b_all, order_ids, valid = lax.optimization_barrier(
        (coefficients, a_near, a_far, b_all, order_ids, valid)
    )

    coefficients = coefficients.reshape(lat_size * lev_size, OWN, sent, LANES)
    coefficients = lax.all_to_all(coefficients, ("lat", "lev"), 0, 0, tiled=True)
    coefficients = coefficients.reshape(lat_size, lev_size, OWN, sent, LANES)
    classes = (z_at + jnp.array([0, -1, 1, 2], jnp.int32)) % Z_LOW
    table = assemble(a_all, a_near, a_far, b_all)

    first = (ord_at * lev_size + lev_at) * OWN
    weights = lax.dynamic_slice_in_dim(jnp.pad(quad_weight, (0, lat_slots - lat_local)), first, OWN)
    w_in = jnp.pad(weight_in, ((0, LANES - width), (0, 0)))
    w_out = jnp.pad(weight_out, ((0, 0), (0, LANES - width)))
    degree_ids = lat_at * degree_local + lax.iota(jnp.int32, degree_local)
    degree_ratio = (degree_ids * (degree_ids + 1)).astype(f32) / ((L - 1) * L)
    damping = 1.0 / (1.0 + hyper_rate * degree_ratio * degree_ratio)
    cosines, sines = lookup_of(order_ids, valid)
    table, coefficients, cosines, sines, weights, w_in, w_out, damping = lax.optimization_barrier(
        (table, coefficients, cosines, sines, weights, w_in, w_out, damping)
    )
    fourier = inverse(classes, table, coefficients, maps, peers, lat_local, lat_slots, width)

    fourier = lax.all_to_all(fourier.reshape(peers, 8, -1), everyone, 0, 0, tiled=True)
    weighted = columns(
        weights,
        fourier.reshape(peers * 8, -1),
        cosines,
        sines,
        w_in,
        bias_in[None, :],
        weight_hidden,
        w_out,
        width,
    )

    weighted = lax.all_to_all(weighted.reshape(peers, 8, -1), everyone, 0, 0, tiled=True)
    weighted = weighted.reshape(peers * 8, -1)
    forcing = forward(
        classes, weighted, table, maps, peers, lat_size, sent, lat_local, lat_slots, width
    )
    forcing = forcing.reshape(lat_size * lev_size, OWN, sent, LANES)
    forcing = lax.all_to_all(forcing, ("lat", "lev"), 0, 0, tiled=True)
    forcing = forcing.reshape(LAT_X, OWN * Z_RING, sent, LANES)
    updated = update(at, damping, state, forcing)
    updated = updated.reshape(degree_local, *spectral_state.shape[2:], order_local)
    return updated.transpose(4, 0, 1, 2, 3)


def solution(mesh):
    return jax.shard_map(
        on_device,
        mesh=mesh,
        in_specs=(
            P("ord", "lat", "lev", None, None),
            P("ord", "lat", None),
            P("lat"),
            P(),
            P(),
            P(),
            P(),
        ),
        out_specs=P("ord", "lat", "lev", None, None),
        check_vma=False,
    )
```

```python
import functools
import math

import jax
import jax.numpy as jnp
import numpy as np
from jax import lax
from jax.experimental import pallas as pl
from jax.experimental.pallas import tpu as pltpu
from jax.sharding import PartitionSpec as P

L = 720
NLON = 1440
OWN = 3
LANES = 128
LAT_X, Z_LOW, Z_RING = 4, 4, 8
HALF = 384
X_ROWS = 1440
SPARE = 14

time_step = 1.0
hyper_rate = 2.0
transform_scale = math.sqrt(2.0 / NLON)

f32, bf16 = jnp.float32, jnp.bfloat16
dot = functools.partial(jnp.dot, preferred_element_type=jnp.float32)


def first_group(x):
    return (22 * x + 1) // 3


def lookup_of(order_ids, valid):
    low = 32

    def waves(x):
        phase_index = order_ids[None, :] * x[:, None] % NLON
        angles = 2.0 * math.pi / NLON * phase_index.astype(f32)
        return jnp.cos(angles), jnp.sin(angles)

    high_cos, high_sin = waves(low * lax.iota(jnp.int32, NLON // low))
    high_cos = jnp.where(valid[None, :], high_cos, 0.0)[:, None]
    high_sin = jnp.where(valid[None, :], high_sin, 0.0)[:, None]
    low_cos, low_sin = (w[None] for w in waves(lax.iota(jnp.int32, low)))
    cosines = high_cos * low_cos - high_sin * low_sin
    sines = -(high_sin * low_cos + high_cos * low_sin)
    shape = (NLON, order_ids.shape[0])
    return cosines.astype(bf16).reshape(shape), sines.astype(bf16).reshape(shape)


def half_silu(u):
    return u + u * jnp.tanh(u)


def lane_map(lev, row_local):
    wide_lane = lax.broadcasted_iota(jnp.int32, (2 * LANES, LANES), 0)
    lane = lax.broadcasted_iota(jnp.int32, (2 * LANES, LANES), 1)
    part = (wide_lane >= LANES).astype(jnp.int32)
    row = wide_lane - LANES * part - lev * row_local
    hit = (row >= 0) & (row < row_local) & (lane == 2 * row + part)
    return jnp.where(hit, 1.0, 0.0).astype(bf16)


def pack_rows(slab_of, out_ref, scr_ref, peers, width):
    lane = lax.broadcasted_iota(jnp.int32, (peers, LANES), 1)
    spare = (lane >= width) & (lane < width + SPARE)
    for part in range(2):
        last = slab_of(part, 2, 2)
        for k in range(8):
            moved = pltpu.roll(last, (width - SPARE * k) % LANES, 1)
            scr_ref[part, pl.ds(k, peers, 8), :] = jnp.where(
                spare, moved, slab_of(part, k // OWN, k % OWN)
            )
        out_ref[:, part * LANES : (part + 1) * LANES] = scr_ref[part].astype(bf16)


def unpack_rows(in_ref, scr_ref, put_slab, peers, width):
    lane = lax.broadcasted_iota(jnp.int32, (peers, LANES), 1)
    for part in range(2):
        scr_ref[part] = in_ref[:, part * LANES : (part + 1) * LANES].astype(f32)
        last = jnp.zeros((peers, LANES), f32)
        for k in range(8):
            slab = scr_ref[part, pl.ds(k, peers, 8), :]
            put_slab(part, k // OWN, k % OWN, slab)
            moved = pltpu.roll(slab, (SPARE * k - width) % LANES, 1)
            last = jnp.where((lane >= SPARE * k) & (lane < SPARE * (k + 1)), moved, last)
        put_slab(part, 2, 2, last)


def spare_lanes(shape, width):
    lane = lax.broadcasted_iota(jnp.int32, shape, len(shape) - 1)
    return (lane >= width) & (lane < width + SPARE)


def scatter_last(row, t, width):
    return pltpu.roll(row, (width - SPARE * t) % LANES, 1)


def gather_last(last, slab, t, width):
    lane = lax.broadcasted_iota(jnp.int32, slab.shape, 1)
    moved = pltpu.roll(slab, (SPARE * t - width) % LANES, 1)
    return jnp.where((lane >= SPARE * t) & (lane < SPARE * (t + 1)), moved, last)


def wide(value):
    return jnp.pad(value, ((0, 0), (0, LANES - value.shape[1])))


def prep_kernel(at_ref, state_ref, last_ref, out_ref, scr_ref):
    _, channels, orders = state_ref.shape
    group, rows = out_ref.shape[1], 8 * pl.num_programs(0)
    b = pl.program_id(0)
    order = lax.broadcasted_iota(jnp.int32, (channels, orders), 1) + at_ref[0]
    masked = lambda value, degree: wide(jnp.where(degree + at_ref[1] >= order, value, 0.0).T)
    last = masked(last_ref[b], rows + b)
    spare = spare_lanes(last.shape, channels)
    for t in range(8):
        scr_ref[pl.ds(t, orders, 8), :] = jnp.where(
            spare, scatter_last(last, t, channels), masked(state_ref[t], 8 * b + t)
        )
    packed = scr_ref[...].astype(bf16).reshape(orders, 8, LANES)
    for x in range(LAT_X):
        first = OWN * first_group(x)
        out_ref[x] = packed[first : first + group]


def prep(at, state, rows):
    group = OWN * Z_RING
    _, channels, orders = state.shape
    steps = rows // 8
    return pl.pallas_call(
        prep_kernel,
        grid=(steps,),
        in_specs=[
            pl.BlockSpec(memory_space=pltpu.SMEM),
            pl.BlockSpec((8, channels, orders), lambda i: (i, 0, 0)),
            pl.BlockSpec((8, channels, orders), lambda i: (steps, 0, 0)),
        ],
        out_specs=pl.BlockSpec((LAT_X, group, 8, LANES), lambda i: (0, 0, i, 0)),
        out_shape=jax.ShapeDtypeStruct((LAT_X, group, rows, LANES), bf16),
        scratch_shapes=[pltpu.VMEM((orders * 8, LANES), f32)],
        cost_estimate=pl.CostEstimate(flops=10**6, bytes_accessed=4 * 10**6, transcendentals=0),
        name="prep",
    )(at, state, state)


def pack_kernel(own_ref, in_ref, a_ref, *b_refs):
    degrees, lats = in_ref.shape[1:]
    half, rows = a_ref.shape[-1], a_ref.shape[-2]
    split = rows // 2
    a_ref[...] = jnp.zeros_like(a_ref)
    for ref in b_refs:
        ref[...] = jnp.zeros_like(ref)
    for k in range(3):
        mine = in_ref[pl.ds(own_ref[k], OWN)]
        a_ref[0, k, :, :degrees, :] = mine[:, :, :half]
        b_refs[k][0, :, :degrees, : lats - half] = mine[:, :, half:]
    mine = in_ref[pl.ds(own_ref[3], OWN)]
    a_ref[0, 3, :, :split, :] = mine[:, :split, :half]
    b_refs[3][0, :, :, : lats - half] = mine[:, :split, half:]
    mine = in_ref[pl.ds(own_ref[4], OWN)]
    a_ref[0, 3, :, split:degrees, :] = mine[:, split:, :half]
    b_refs[4][0, :, : degrees - split, : lats - half] = mine[:, split:, half:]


def pack_table(own, legendre, half, rows):
    _, degrees, lats = legendre.shape
    group = OWN * Z_RING
    b_shape = lambda r: jax.ShapeDtypeStruct((LAT_X, OWN, r, half), bf16)
    b_spec = lambda r: pl.BlockSpec((1, OWN, r, half), lambda x: (x, 0, 0, 0))
    b_rows = (rows, rows, rows, rows // 2, rows // 2)
    return pl.pallas_call(
        pack_kernel,
        grid=(LAT_X,),
        in_specs=[
            pl.BlockSpec(memory_space=pltpu.SMEM),
            pl.BlockSpec(
                (pl.Element(group), pl.Element(degrees), pl.Element(lats)),
                lambda x: (OWN * first_group(x), 0, 0),
            ),
        ],
        out_specs=[pl.BlockSpec((1, 4, OWN, rows, half), lambda x: (x, 0, 0, 0, 0))]
        + [b_spec(r) for r in b_rows],
        out_shape=[jax.ShapeDtypeStruct((LAT_X, 4, OWN, rows, half), bf16)]
        + [b_shape(r) for r in b_rows],
        compiler_params=pltpu.CompilerParams(vmem_limit_bytes=60 * 2**20),
        name="pack_table",
    )(own, legendre)


def assemble_kernel(a_own_ref, a_left_ref, a_right_ref, a_low_ref, a_high_ref, b_ref, out_ref):
    rows, half = b_ref.shape[-2:]
    place = LAT_X * rows
    far = jnp.concatenate([a_low_ref[...], a_high_ref[...]], axis=1)
    for k, piece in enumerate((a_own_ref[:, 0], a_left_ref[...], a_right_ref[...], far)):
        out_ref[0, k * place : (k + 1) * place, :half] = piece.reshape(place, half)
        out_ref[0, k * place : (k + 1) * place, half:] = b_ref[:, k].reshape(place, half)


def assemble(a_own, a_near, a_far, b_all):
    rows, half = b_all.shape[-2:]
    size = 4 * LAT_X * rows
    near = pl.BlockSpec((LAT_X, None, rows, half), lambda m: (0, m, 0, 0))
    far = pl.BlockSpec((LAT_X, None, rows // 2, half), lambda m: (0, m, 0, 0))
    return pl.pallas_call(
        assemble_kernel,
        grid=(OWN,),
        in_specs=[
            pl.BlockSpec((LAT_X, 1, None, rows, half), lambda m: (0, 0, m, 0, 0)),
            near,
            near,
            far,
            far,
            pl.BlockSpec((LAT_X, 4, None, rows, half), lambda m: (0, 0, m, 0, 0)),
        ],
        out_specs=pl.BlockSpec((1, size, 2 * half), lambda m: (m, 0, 0)),
        out_shape=jax.ShapeDtypeStruct((OWN, size, 2 * half), bf16),
        cost_estimate=pl.CostEstimate(flops=10**6, bytes_accessed=8 * 10**6, transcendentals=0),
        name="assemble",
    )(a_own, *a_near, *a_far, b_all)


def inverse_kernel(
    class_ref, table_ref, coef_ref, out_ref, sums_ref, scr_ref, sent_ref, full_ref,
    *, lats, lat_local, lat_slots, width,
):
    levs, _, sent, _ = coef_ref.shape[1:]
    rows = full_ref.shape[0] // lats
    maps = [lane_map(v, width // levs) for v in range(levs)]
    for m in range(OWN):
        swapped = 0.0
        for v in range(levs):
            for q in range(lats):
                k, x = divmod(q, LAT_X)
                piece = coef_ref[x * Z_LOW + class_ref[k], v, m].astype(f32)
                sent_ref[q * sent : (q + 1) * sent, :] = piece
                full_ref[q * rows : q * rows + sent, :] = piece
                full_ref[q * rows + sent : (q + 1) * rows, :] = jnp.zeros((rows - sent, LANES), f32)
            for b in range(sent // 8):
                last = jnp.zeros((lats, LANES), f32)
                for t in range(8):
                    slab = sent_ref[pl.ds(8 * b + t, lats, sent), :]
                    last = gather_last(last, slab, t, width)
                full_ref[pl.ds(sent + b, lats, rows), :] = last
            swapped += lax.dot_general(
                maps[v],
                full_ref[...].astype(bf16),
                (((1,), (1,)), ((), ())),
                preferred_element_type=f32,
            )
        sums = dot(swapped.astype(bf16), table_ref[m]).T
        for part in range(2):
            lanes = slice(part * LANES, (part + 1) * LANES)
            for lat in range(lats):
                first = lat * lat_slots
                sums_ref[m, part, first : first + lat_local, :] = sums[
                    lat * lat_local : (lat + 1) * lat_local, lanes
                ]
                sums_ref[m, part, first + lat_local : first + lat_slots, :] = jnp.zeros(
                    (lat_slots - lat_local, LANES), f32
                )

    peers = out_ref.shape[0] // 8
    slab_of = lambda part, i, m: sums_ref[m, part, pl.ds(i, peers, OWN), :]
    pack_rows(slab_of, out_ref, scr_ref, peers, width)


def inverse(classes, table, coef, peers, lat_local, lat_slots, width):
    lats, _, _, sent, _ = coef.shape
    vmem = pl.BlockSpec(memory_space=pltpu.VMEM)
    return pl.pallas_call(
        functools.partial(
            inverse_kernel, lats=lats, lat_local=lat_local, lat_slots=lat_slots, width=width
        ),
        in_specs=[pl.BlockSpec(memory_space=pltpu.SMEM), vmem, vmem],
        out_specs=vmem,
        out_shape=jax.ShapeDtypeStruct((peers * 8, 2 * LANES), bf16),
        scratch_shapes=[
            pltpu.VMEM((OWN, 2, lats * lat_slots, LANES), f32),
            pltpu.VMEM((2, peers * 8, LANES), f32),
            pltpu.VMEM((lats * sent, LANES), f32),
            pltpu.VMEM((table.shape[1], LANES), f32),
        ],
        compiler_params=pltpu.CompilerParams(vmem_limit_bytes=24 * 2**20),
        name="inverse",
    )(classes, table, coef)


def column_kernel(
    weight_ref, in_ref, cos_ref, sin_ref, w_in_ref, bias_ref, w_hid_ref, w_out_ref,
    out_ref, fourier_ref, tendency_ref, sums_ref, scr_ref, *, x_rows, width,
):
    peers = in_ref.shape[0] // 8

    def put(part, i, m, slab):
        fourier_ref[part, m * peers : (m + 1) * peers, i * LANES : (i + 1) * LANES] = slab.astype(
            bf16
        )

    unpack_rows(in_ref, scr_ref, put, peers, width)

    half_in, half_bias = 0.5 * w_in_ref[...], 0.5 * bias_ref[...]
    half_hid = [0.5 * w_hid_ref[layer] for layer in range(w_hid_ref.shape[0])]

    def grid_rows(step, carry):
        rows = pl.ds(pl.multiple_of(step * x_rows, x_rows), x_rows)
        raw = dot(cos_ref[rows, :], fourier_ref[0]) + dot(sin_ref[rows, :], fourier_ref[1])
        features = (transform_scale * raw).astype(bf16)
        lanes = [slice(i * LANES, (i + 1) * LANES) for i in range(OWN)]
        hidden = [half_silu(dot(features[:, at], half_in) + half_bias) for at in lanes]
        hidden = [h.astype(bf16) for h in hidden]
        for weights in half_hid:
            update = [half_silu(dot(h, weights)) for h in hidden]
            hidden = [(h.astype(f32) + u).astype(bf16) for h, u in zip(hidden, update)]
        for at, h in zip(lanes, hidden):
            tendency_ref[rows, at] = dot(h, w_out_ref[...]).astype(bf16)
        return carry

    lax.fori_loop(0, NLON // x_rows, grid_rows, 0)

    for part, table_ref in enumerate((cos_ref, sin_ref)):
        sums = lax.dot_general(
            tendency_ref[...],
            table_ref[...],
            (((0,), (0,)), ((), ())),
            preferred_element_type=f32,
        )
        for i in range(OWN):
            weight = weight_ref[i] * transform_scale
            for m in range(OWN):
                block = sums[i * LANES : (i + 1) * LANES, m * peers : (m + 1) * peers]
                sums_ref[part, i, m] = weight * block.T

    slab_of = lambda part, i, m: sums_ref[part, i, m]
    pack_rows(slab_of, out_ref, scr_ref, peers, width)


def columns(weights, fourier, cosines, sines, w_in, bias, w_hid, w_out, width):
    peers = fourier.shape[0] // 8
    vmem = pl.BlockSpec(memory_space=pltpu.VMEM)
    return pl.pallas_call(
        functools.partial(column_kernel, x_rows=X_ROWS, width=width),
        in_specs=[pl.BlockSpec(memory_space=pltpu.SMEM)] + [vmem] * 7,
        out_specs=vmem,
        out_shape=jax.ShapeDtypeStruct(fourier.shape, bf16),
        scratch_shapes=[
            pltpu.VMEM((2, OWN * peers, OWN * LANES), bf16),
            pltpu.VMEM((NLON, OWN * LANES), bf16),
            pltpu.VMEM((2, OWN, OWN, peers, LANES), f32),
            pltpu.VMEM((2, peers * 8, LANES), f32),
        ],
        compiler_params=pltpu.CompilerParams(vmem_limit_bytes=26 * 2**20),
        name="columns",
    )(weights, fourier, cosines, sines, w_in, bias, w_hid, w_out)


def forward_kernel(
    class_ref, in_ref, table_ref, out_ref, sums_ref, scr_ref, sent_ref, full_ref,
    *, lats, lat_local, lat_slots, width,
):
    peers = in_ref.shape[0] // 8

    def put(part, i, m, slab):
        sums_ref[m, part, pl.ds(i, peers, OWN), :] = slab

    unpack_rows(in_ref, scr_ref, put, peers, width)
    lanes = table_ref.shape[-1]
    levs, _, sent, _ = out_ref.shape[1:]
    rows = full_ref.shape[0] // lats
    maps = [lane_map(v, width // levs) for v in range(levs)]
    spare = spare_lanes((lats, LANES), width)
    for m in range(OWN):
        weighted = jnp.concatenate(
            [
                jnp.concatenate(
                    [
                        sums_ref[m, part, lat * lat_slots : lat * lat_slots + lat_local, :]
                        for lat in range(lats)
                    ]
                    + [jnp.zeros((lanes - lats * lat_local, LANES), f32)]
                )
                for part in range(2)
            ],
            axis=1,
        ).astype(bf16)
        forcing = dot(table_ref[m], weighted).astype(bf16)
        for v in range(levs):
            full_ref[...] = dot(forcing, maps[v])
            for b in range(sent // 8):
                last = full_ref[pl.ds(sent + b, lats, rows), :]
                for t in range(8):
                    main = full_ref[pl.ds(8 * b + t, lats, rows), :]
                    sent_ref[pl.ds(8 * b + t, lats, sent), :] = jnp.where(
                        spare, scatter_last(last, t, width), main
                    )
            for q in range(lats):
                k, x = divmod(q, LAT_X)
                piece = sent_ref[q * sent : (q + 1) * sent, :].astype(bf16)
                out_ref[x * Z_LOW + class_ref[k], v, m] = piece


def forward(classes, weighted, table, peers, lats, levs, sent, lat_local, lat_slots, width):
    vmem = pl.BlockSpec(memory_space=pltpu.VMEM)
    return pl.pallas_call(
        functools.partial(
            forward_kernel, lats=lats, lat_local=lat_local, lat_slots=lat_slots, width=width
        ),
        in_specs=[pl.BlockSpec(memory_space=pltpu.SMEM), vmem, vmem],
        out_specs=vmem,
        out_shape=jax.ShapeDtypeStruct((lats, levs, OWN, sent, LANES), bf16),
        scratch_shapes=[
            pltpu.VMEM((OWN, 2, lats * lat_slots, LANES), f32),
            pltpu.VMEM((2, peers * 8, LANES), f32),
            pltpu.VMEM((lats * sent, LANES), f32),
            pltpu.VMEM((table.shape[1], LANES), f32),
        ],
        compiler_params=pltpu.CompilerParams(vmem_limit_bytes=24 * 2**20),
        name="forward",
    )(classes, weighted, table)


def turn_maps(channels):
    maps = np.zeros((8, 2 * channels, LANES), np.float32)
    for t in range(8):
        maps[t, np.arange(channels), np.arange(channels)] = 1.0
        piece = np.arange(SPARE)
        maps[t, channels + SPARE * t + piece, channels + piece] = 1.0
    return jnp.asarray(maps, bf16)


def update_kernel(at_ref, damping_ref, state_ref, forcing_ref, maps_ref, out_ref, scr_ref):
    degrees, channels, orders = state_ref.shape
    order = lax.broadcasted_iota(jnp.int32, (channels, orders), 1) + at_ref[0]

    def put(degree, forcing):
        new = (state_ref[degree] + time_step * forcing) * damping_ref[degree]
        out_ref[degree] = jnp.where(degree + at_ref[1] >= order, new, 0.0)

    sent = forcing_ref.shape[2]
    for b in range(sent // 8):
        for x in range(LAT_X):
            skip = OWN * (first_group(x - 1) + Z_RING - first_group(x)) if x else 0
            first = (OWN * first_group(x) + skip) * 8
            mine = forcing_ref[x, skip:, 8 * b : 8 * b + 8, :].astype(f32)
            scr_ref[b, first : first + mine.shape[0] * 8, :] = mine.reshape(-1, LANES)
        last = 0.0
        for t in range(8):
            turned = lax.dot_general(
                maps_ref[t],
                scr_ref[b, pl.ds(t, orders, 8), :].astype(bf16),
                (((1,), (1,)), ((), ())),
                preferred_element_type=f32,
            )
            put(8 * b + t, turned[:channels])
            last += turned[channels:]
        put(sent + b, last)


def update(at, damping, state, forcing):
    degrees, channels, orders = state.shape
    _, _, sent, _ = forcing.shape
    smem, vmem = (pl.BlockSpec(memory_space=m) for m in (pltpu.SMEM, pltpu.VMEM))
    return pl.pallas_call(
        update_kernel,
        in_specs=[smem, smem, vmem, vmem, vmem],
        out_specs=vmem,
        out_shape=jax.ShapeDtypeStruct(state.shape, f32),
        scratch_shapes=[pltpu.VMEM((sent // 8, orders * 8, LANES), f32)],
        compiler_params=pltpu.CompilerParams(vmem_limit_bytes=24 * 2**20),
        name="update",
    )(at, damping, state, forcing, turn_maps(channels))


def along_z(value, step):
    pairs = []
    flat = lambda x, z: x * Z_RING + 2 * (z % Z_LOW) + z // Z_LOW
    for x in range(LAT_X):
        pairs += [(flat(x, z), flat(x, (z + step) % Z_RING)) for z in range(Z_RING)]
    return lax.ppermute(value, ("lat", "lev"), pairs)


def along_x(value):
    groups = [[x * Z_LOW + z for x in range(LAT_X)] for z in range(Z_LOW)]
    return lax.all_to_all(value, "lat", 0, 0, axis_index_groups=groups, tiled=True)


def on_device(spectral_state, legendre, quad_weight, weight_in, bias_in, weight_hidden, weight_out):
    ord_size, lat_size, lev_size = (lax.axis_size(a) for a in ("ord", "lat", "lev"))
    ord_at, lat_at, lev_at = (lax.axis_index(a) for a in ("ord", "lat", "lev"))
    order_local, degree_local = spectral_state.shape[:2]
    lat_local = quad_weight.shape[0]
    row_local = spectral_state.shape[2] * spectral_state.shape[3]
    channels = 2 * row_local
    width = lev_size * row_local
    rows = -(-degree_local // 16) * 16
    sent = degree_local // 8 * 8
    peers = ord_size * lat_size * lev_size
    lat_slots = ord_size * lev_size * OWN
    everyone = ("lat", "ord", "lev")
    at = jnp.stack([ord_at * order_local, lat_at * degree_local]).astype(jnp.int32)
    state = spectral_state.transpose(1, 2, 3, 4, 0).reshape(degree_local, channels, order_local)

    z_at = lev_at * Z_LOW + lat_at % Z_LOW
    ring = (z_at + jnp.array([0, 1, -1, 2, -2], jnp.int32)) % Z_RING
    own = OWN * (2 * (ring % Z_LOW) + ring // Z_LOW)
    a_all, b_own, *b_rest = pack_table(own, legendre, HALF, rows)
    b_left, b_right, b_low, b_high = (along_z(v, k) for v, k in zip(b_rest, (1, -1, 2, -2)))
    a_all = along_x(a_all)
    b_far = jnp.concatenate([b_low, b_high], axis=2)
    b_all = jnp.stack([b_own, b_left, b_right, b_far], axis=1)
    a_cut = [a_all[:, 1], a_all[:, 2], a_all[:, 3, :, : rows // 2], a_all[:, 3, :, rows // 2 :]]
    coefficients = prep(at, state, sent)
    a_cut, b_all, coefficients = lax.optimization_barrier((a_cut, b_all, coefficients))
    a_near = [along_z(a_cut[0], 1), along_z(a_cut[1], -1)]
    a_far = [along_z(a_cut[2], 2), along_z(a_cut[3], -2)]
    b_all = along_x(b_all)

    slot = lax.iota(jnp.int32, OWN * peers)
    slot_lev = slot % lev_size
    slot_ord = slot // lev_size % ord_size
    slot_lat = slot // (lev_size * ord_size) % lat_size
    slot_x, slot_w = slot_lat // Z_LOW, 2 * (slot_lat % Z_LOW) + slot_lev
    valid = (slot_x % 2 == 0) | (slot_w > 0)
    order_ids = slot_ord * order_local + OWN * (first_group(slot_x) + slot_w) + slot // peers
    coefficients, a_near, a_far, b_all, order_ids, valid = lax.optimization_barrier(
        (coefficients, a_near, a_far, b_all, order_ids, valid)
    )

    coefficients = coefficients.reshape(lat_size * lev_size, OWN, sent, LANES)
    coefficients = lax.all_to_all(coefficients, ("lat", "lev"), 0, 0, tiled=True)
    coefficients = coefficients.reshape(lat_size, lev_size, OWN, sent, LANES)
    classes = (z_at + jnp.array([0, -1, 1, 2], jnp.int32)) % Z_LOW
    table = assemble(a_all, a_near, a_far, b_all)

    first = (ord_at * lev_size + lev_at) * OWN
    weights = lax.dynamic_slice_in_dim(jnp.pad(quad_weight, (0, lat_slots - lat_local)), first, OWN)
    w_in = jnp.pad(weight_in, ((0, LANES - width), (0, 0)))
    w_out = jnp.pad(weight_out, ((0, 0), (0, LANES - width)))
    degree_ids = lat_at * degree_local + lax.iota(jnp.int32, degree_local)
    degree_ratio = (degree_ids * (degree_ids + 1)).astype(f32) / ((L - 1) * L)
    damping = 1.0 / (1.0 + hyper_rate * degree_ratio * degree_ratio)
    cosines, sines = lookup_of(order_ids, valid)
    table, coefficients, cosines, sines, weights, w_in, w_out, damping = lax.optimization_barrier(
        (table, coefficients, cosines, sines, weights, w_in, w_out, damping)
    )
    fourier = inverse(classes, table, coefficients, peers, lat_local, lat_slots, width)

    fourier = lax.all_to_all(fourier.reshape(peers, 8, -1), everyone, 0, 0, tiled=True)
    weighted = columns(
        weights,
        fourier.reshape(peers * 8, -1),
        cosines,
        sines,
        w_in,
        bias_in[None, :],
        weight_hidden,
        w_out,
        width,
    )

    weighted = lax.all_to_all(weighted.reshape(peers, 8, -1), everyone, 0, 0, tiled=True)
    weighted = weighted.reshape(peers * 8, -1)
    forcing = forward(
        classes, weighted, table, peers, lat_size, lev_size, sent, lat_local, lat_slots, width
    )
    forcing = forcing.reshape(lat_size * lev_size, OWN, sent, LANES)
    forcing = lax.all_to_all(forcing, ("lat", "lev"), 0, 0, tiled=True)
    forcing = forcing.reshape(LAT_X, OWN * Z_RING, sent, LANES)
    updated = update(at, damping, state, forcing)
    updated = updated.reshape(degree_local, *spectral_state.shape[2:], order_local)
    return updated.transpose(4, 0, 1, 2, 3)


def solution(mesh):
    return jax.shard_map(
        on_device,
        mesh=mesh,
        in_specs=(
            P("ord", "lat", "lev", None, None),
            P("ord", "lat", None),
            P("lat"),
            P(),
            P(),
            P(),
            P(),
        ),
        out_specs=P("ord", "lat", "lev", None, None),
        check_vma=False,
    )
```

```python
import functools
import math

import jax
import jax.numpy as jnp
import numpy as np
from jax import lax
from jax.experimental import pallas as pl
from jax.experimental.pallas import tpu as pltpu
from jax.sharding import PartitionSpec as P

L = 720
NLON = 1440
OWN = 3
LANES = 128
LAT_X, Z_LOW, Z_RING = 4, 4, 8
HALF = 384
X_ROWS = 1440
SPARE = 14

time_step = 1.0
hyper_rate = 2.0
transform_scale = math.sqrt(2.0 / NLON)

f32, bf16 = jnp.float32, jnp.bfloat16
dot = functools.partial(jnp.dot, preferred_element_type=jnp.float32)


def first_group(x):
    return (22 * x + 1) // 3


def lookup_of(order_ids, valid):
    low = 32

    def waves(x):
        phase_index = order_ids[None, :] * x[:, None] % NLON
        angles = 2.0 * math.pi / NLON * phase_index.astype(f32)
        return jnp.cos(angles), jnp.sin(angles)

    high_cos, high_sin = waves(low * lax.iota(jnp.int32, NLON // low))
    high_cos = jnp.where(valid[None, :], high_cos, 0.0)[:, None]
    high_sin = jnp.where(valid[None, :], high_sin, 0.0)[:, None]
    low_cos, low_sin = (w[None] for w in waves(lax.iota(jnp.int32, low)))
    cosines = high_cos * low_cos - high_sin * low_sin
    sines = -(high_sin * low_cos + high_cos * low_sin)
    shape = (NLON, order_ids.shape[0])
    return cosines.astype(bf16).reshape(shape), sines.astype(bf16).reshape(shape)


def half_silu(u):
    return u + u * jnp.tanh(u)


def lane_map(lev, row_local):
    wide_lane = lax.broadcasted_iota(jnp.int32, (2 * LANES, LANES), 0)
    lane = lax.broadcasted_iota(jnp.int32, (2 * LANES, LANES), 1)
    part = (wide_lane >= LANES).astype(jnp.int32)
    row = wide_lane - LANES * part - lev * row_local
    hit = (row >= 0) & (row < row_local) & (lane == 2 * row + part)
    return jnp.where(hit, 1.0, 0.0).astype(bf16)


def pack_rows(slab_of, out_ref, scr_ref, peers, width):
    lane = lax.broadcasted_iota(jnp.int32, (peers, LANES), 1)
    spare = (lane >= width) & (lane < width + SPARE)
    for part in range(2):
        last = slab_of(part, 2, 2)
        for k in range(8):
            moved = pltpu.roll(last, (width - SPARE * k) % LANES, 1)
            scr_ref[part, pl.ds(k, peers, 8), :] = jnp.where(
                spare, moved, slab_of(part, k // OWN, k % OWN)
            )
        out_ref[:, part * LANES : (part + 1) * LANES] = scr_ref[part].astype(bf16)


def unpack_rows(in_ref, scr_ref, put_slab, peers, width):
    lane = lax.broadcasted_iota(jnp.int32, (peers, LANES), 1)
    for part in range(2):
        scr_ref[part] = in_ref[:, part * LANES : (part + 1) * LANES].astype(f32)
        last = jnp.zeros((peers, LANES), f32)
        for k in range(8):
            slab = scr_ref[part, pl.ds(k, peers, 8), :]
            put_slab(part, k // OWN, k % OWN, slab)
            moved = pltpu.roll(slab, (SPARE * k - width) % LANES, 1)
            last = jnp.where((lane >= SPARE * k) & (lane < SPARE * (k + 1)), moved, last)
        put_slab(part, 2, 2, last)


def spare_lanes(shape, width):
    lane = lax.broadcasted_iota(jnp.int32, shape, len(shape) - 1)
    return (lane >= width) & (lane < width + SPARE)


def scatter_last(row, t, width):
    return pltpu.roll(row, (width - SPARE * t) % LANES, 1)


def gather_last(last, slab, t, width):
    lane = lax.broadcasted_iota(jnp.int32, slab.shape, 1)
    moved = pltpu.roll(slab, (SPARE * t - width) % LANES, 1)
    return jnp.where((lane >= SPARE * t) & (lane < SPARE * (t + 1)), moved, last)


def wide(value):
    return jnp.pad(value, ((0, 0), (0, LANES - value.shape[1])))


def prep_kernel(at_ref, state_ref, last_ref, out_ref, scr_ref):
    _, channels, orders = state_ref.shape
    group, rows = out_ref.shape[1], 8 * pl.num_programs(0)
    b = pl.program_id(0)
    order = lax.broadcasted_iota(jnp.int32, (channels, orders), 1) + at_ref[0]
    masked = lambda value, degree: wide(jnp.where(degree + at_ref[1] >= order, value, 0.0).T)
    last = masked(last_ref[b], rows + b)
    spare = spare_lanes(last.shape, channels)
    for t in range(8):
        scr_ref[pl.ds(t, orders, 8), :] = jnp.where(
            spare, scatter_last(last, t, channels), masked(state_ref[t], 8 * b + t)
        )
    packed = scr_ref[...].astype(bf16).reshape(orders, 8, LANES)
    for x in range(LAT_X):
        first = OWN * first_group(x)
        out_ref[x] = packed[first : first + group]


def prep(at, state, rows):
    group = OWN * Z_RING
    _, channels, orders = state.shape
    steps = rows // 8
    return pl.pallas_call(
        prep_kernel,
        grid=(steps,),
        in_specs=[
            pl.BlockSpec(memory_space=pltpu.SMEM),
            pl.BlockSpec((8, channels, orders), lambda i: (i, 0, 0)),
            pl.BlockSpec((8, channels, orders), lambda i: (steps, 0, 0)),
        ],
        out_specs=pl.BlockSpec((LAT_X, group, 8, LANES), lambda i: (0, 0, i, 0)),
        out_shape=jax.ShapeDtypeStruct((LAT_X, group, rows, LANES), bf16),
        scratch_shapes=[pltpu.VMEM((orders * 8, LANES), f32)],
        cost_estimate=pl.CostEstimate(flops=10**6, bytes_accessed=4 * 10**6, transcendentals=0),
        name="prep",
    )(at, state, state)


def pack_kernel(z_ref, in_ref, a_ref, *b_refs):
    degrees, lats = in_ref.shape[1:]
    half, rows = a_ref.shape[-1], a_ref.shape[-2]
    split = rows // 2
    ring = [lax.rem(z_ref[0] + (Z_RING + step), Z_RING) for step in (0, 1, -1, 2, -2)]
    own = [OWN * (2 * lax.rem(z, Z_LOW) + lax.div(z, Z_LOW)) for z in ring]
    a_ref[...] = jnp.zeros_like(a_ref)
    for ref in b_refs:
        ref[...] = jnp.zeros_like(ref)
    for k in range(3):
        mine = in_ref[pl.ds(own[k], OWN)]
        a_ref[0, k, :, :degrees, :] = mine[:, :, :half]
        b_refs[k][0, :, :degrees, : lats - half] = mine[:, :, half:]
    mine = in_ref[pl.ds(own[3], OWN)]
    a_ref[0, 3, :, :split, :] = mine[:, :split, :half]
    b_refs[3][0, :, :, : lats - half] = mine[:, :split, half:]
    mine = in_ref[pl.ds(own[4], OWN)]
    a_ref[0, 3, :, split:degrees, :] = mine[:, split:, :half]
    b_refs[4][0, :, : degrees - split, : lats - half] = mine[:, split:, half:]


def pack_table(z_at, legendre, half, rows):
    _, degrees, lats = legendre.shape
    group = OWN * Z_RING
    b_shape = lambda r: jax.ShapeDtypeStruct((LAT_X, OWN, r, half), bf16)
    b_spec = lambda r: pl.BlockSpec((1, OWN, r, half), lambda x: (x, 0, 0, 0))
    b_rows = (rows, rows, rows, rows // 2, rows // 2)
    return pl.pallas_call(
        pack_kernel,
        grid=(LAT_X,),
        in_specs=[
            pl.BlockSpec(memory_space=pltpu.SMEM),
            pl.BlockSpec(
                (pl.Element(group), pl.Element(degrees), pl.Element(lats)),
                lambda x: (OWN * first_group(x), 0, 0),
            ),
        ],
        out_specs=[pl.BlockSpec((1, 4, OWN, rows, half), lambda x: (x, 0, 0, 0, 0))]
        + [b_spec(r) for r in b_rows],
        out_shape=[jax.ShapeDtypeStruct((LAT_X, 4, OWN, rows, half), bf16)]
        + [b_shape(r) for r in b_rows],
        compiler_params=pltpu.CompilerParams(vmem_limit_bytes=60 * 2**20),
        name="pack_table",
    )(z_at, legendre)


def assemble_kernel(a_own_ref, a_left_ref, a_right_ref, a_low_ref, a_high_ref, b_ref, out_ref):
    rows, half = b_ref.shape[-2:]
    place = LAT_X * rows
    far = jnp.concatenate([a_low_ref[...], a_high_ref[...]], axis=1)
    for k, piece in enumerate((a_own_ref[:, 0], a_left_ref[...], a_right_ref[...], far)):
        out_ref[0, k * place : (k + 1) * place, :half] = piece.reshape(place, half)
        out_ref[0, k * place : (k + 1) * place, half:] = b_ref[:, k].reshape(place, half)


def assemble(a_own, a_near, a_far, b_all):
    rows, half = b_all.shape[-2:]
    size = 4 * LAT_X * rows
    near = pl.BlockSpec((LAT_X, None, rows, half), lambda m: (0, m, 0, 0))
    far = pl.BlockSpec((LAT_X, None, rows // 2, half), lambda m: (0, m, 0, 0))
    return pl.pallas_call(
        assemble_kernel,
        grid=(OWN,),
        in_specs=[
            pl.BlockSpec((LAT_X, 1, None, rows, half), lambda m: (0, 0, m, 0, 0)),
            near,
            near,
            far,
            far,
            pl.BlockSpec((LAT_X, 4, None, rows, half), lambda m: (0, 0, m, 0, 0)),
        ],
        out_specs=pl.BlockSpec((1, size, 2 * half), lambda m: (m, 0, 0)),
        out_shape=jax.ShapeDtypeStruct((OWN, size, 2 * half), bf16),
        cost_estimate=pl.CostEstimate(flops=10**6, bytes_accessed=8 * 10**6, transcendentals=0),
        name="assemble",
    )(a_own, *a_near, *a_far, b_all)


def inverse_kernel(
    class_ref, table_ref, coef_ref, out_ref, sums_ref, scr_ref, sent_ref, full_ref,
    *, lats, lat_local, lat_slots, width,
):
    levs, _, sent, _ = coef_ref.shape[1:]
    rows = full_ref.shape[0] // lats
    maps = [lane_map(v, width // levs) for v in range(levs)]
    for m in range(OWN):
        swapped = 0.0
        for v in range(levs):
            for q in range(lats):
                k, x = divmod(q, LAT_X)
                piece = coef_ref[x * Z_LOW + class_ref[k], v, m].astype(f32)
                sent_ref[q * sent : (q + 1) * sent, :] = piece
                full_ref[q * rows : q * rows + sent, :] = piece
                full_ref[q * rows + sent : (q + 1) * rows, :] = jnp.zeros((rows - sent, LANES), f32)
            for b in range(sent // 8):
                last = jnp.zeros((lats, LANES), f32)
                for t in range(8):
                    slab = sent_ref[pl.ds(8 * b + t, lats, sent), :]
                    last = gather_last(last, slab, t, width)
                full_ref[pl.ds(sent + b, lats, rows), :] = last
            swapped += lax.dot_general(
                maps[v],
                full_ref[...].astype(bf16),
                (((1,), (1,)), ((), ())),
                preferred_element_type=f32,
            )
        sums = dot(swapped.astype(bf16), table_ref[m]).T
        for part in range(2):
            lanes = slice(part * LANES, (part + 1) * LANES)
            for lat in range(lats):
                first = lat * lat_slots
                sums_ref[m, part, first : first + lat_local, :] = sums[
                    lat * lat_local : (lat + 1) * lat_local, lanes
                ]
                sums_ref[m, part, first + lat_local : first + lat_slots, :] = jnp.zeros(
                    (lat_slots - lat_local, LANES), f32
                )

    peers = out_ref.shape[0] // 8
    slab_of = lambda part, i, m: sums_ref[m, part, pl.ds(i, peers, OWN), :]
    pack_rows(slab_of, out_ref, scr_ref, peers, width)


def inverse(classes, table, coef, peers, lat_local, lat_slots, width):
    lats, _, _, sent, _ = coef.shape
    vmem = pl.BlockSpec(memory_space=pltpu.VMEM)
    return pl.pallas_call(
        functools.partial(
            inverse_kernel, lats=lats, lat_local=lat_local, lat_slots=lat_slots, width=width
        ),
        in_specs=[pl.BlockSpec(memory_space=pltpu.SMEM), vmem, vmem],
        out_specs=vmem,
        out_shape=jax.ShapeDtypeStruct((peers * 8, 2 * LANES), bf16),
        scratch_shapes=[
            pltpu.VMEM((OWN, 2, lats * lat_slots, LANES), f32),
            pltpu.VMEM((2, peers * 8, LANES), f32),
            pltpu.VMEM((lats * sent, LANES), f32),
            pltpu.VMEM((table.shape[1], LANES), f32),
        ],
        compiler_params=pltpu.CompilerParams(vmem_limit_bytes=24 * 2**20),
        name="inverse",
    )(classes, table, coef)


def column_kernel(
    weight_ref, in_ref, cos_ref, sin_ref, w_in_ref, bias_ref, w_hid_ref, w_out_ref,
    out_ref, fourier_ref, tendency_ref, sums_ref, scr_ref, *, x_rows, width,
):
    peers = in_ref.shape[0] // 8

    def put(part, i, m, slab):
        fourier_ref[part, m * peers : (m + 1) * peers, i * LANES : (i + 1) * LANES] = slab.astype(
            bf16
        )

    unpack_rows(in_ref, scr_ref, put, peers, width)

    half_in, half_bias = 0.5 * w_in_ref[...], 0.5 * bias_ref[...]
    half_hid = [0.5 * w_hid_ref[layer] for layer in range(w_hid_ref.shape[0])]

    def grid_rows(step, carry):
        rows = pl.ds(pl.multiple_of(step * x_rows, x_rows), x_rows)
        raw = dot(cos_ref[rows, :], fourier_ref[0]) + dot(sin_ref[rows, :], fourier_ref[1])
        features = (transform_scale * raw).astype(bf16)
        lanes = [slice(i * LANES, (i + 1) * LANES) for i in range(OWN)]
        hidden = [half_silu(dot(features[:, at], half_in) + half_bias) for at in lanes]
        hidden = [h.astype(bf16) for h in hidden]
        for weights in half_hid:
            update = [half_silu(dot(h, weights)) for h in hidden]
            hidden = [(h.astype(f32) + u).astype(bf16) for h, u in zip(hidden, update)]
        for at, h in zip(lanes, hidden):
            tendency_ref[rows, at] = dot(h, w_out_ref[...]).astype(bf16)
        return carry

    lax.fori_loop(0, NLON // x_rows, grid_rows, 0)

    for part, table_ref in enumerate((cos_ref, sin_ref)):
        sums = lax.dot_general(
            tendency_ref[...],
            table_ref[...],
            (((0,), (0,)), ((), ())),
            preferred_element_type=f32,
        )
        for i in range(OWN):
            weight = weight_ref[i] * transform_scale
            for m in range(OWN):
                block = sums[i * LANES : (i + 1) * LANES, m * peers : (m + 1) * peers]
                sums_ref[part, i, m] = weight * block.T

    slab_of = lambda part, i, m: sums_ref[part, i, m]
    pack_rows(slab_of, out_ref, scr_ref, peers, width)


def columns(weights, fourier, cosines, sines, w_in, bias, w_hid, w_out, width):
    peers = fourier.shape[0] // 8
    vmem = pl.BlockSpec(memory_space=pltpu.VMEM)
    return pl.pallas_call(
        functools.partial(column_kernel, x_rows=X_ROWS, width=width),
        in_specs=[pl.BlockSpec(memory_space=pltpu.SMEM)] + [vmem] * 7,
        out_specs=vmem,
        out_shape=jax.ShapeDtypeStruct(fourier.shape, bf16),
        scratch_shapes=[
            pltpu.VMEM((2, OWN * peers, OWN * LANES), bf16),
            pltpu.VMEM((NLON, OWN * LANES), bf16),
            pltpu.VMEM((2, OWN, OWN, peers, LANES), f32),
            pltpu.VMEM((2, peers * 8, LANES), f32),
        ],
        compiler_params=pltpu.CompilerParams(vmem_limit_bytes=26 * 2**20),
        name="columns",
    )(weights, fourier, cosines, sines, w_in, bias, w_hid, w_out)


def forward_kernel(
    class_ref, in_ref, table_ref, out_ref, sums_ref, scr_ref, sent_ref, full_ref,
    *, lats, lat_local, lat_slots, width,
):
    peers = in_ref.shape[0] // 8

    def put(part, i, m, slab):
        sums_ref[m, part, pl.ds(i, peers, OWN), :] = slab

    unpack_rows(in_ref, scr_ref, put, peers, width)
    lanes = table_ref.shape[-1]
    levs, _, sent, _ = out_ref.shape[1:]
    rows = full_ref.shape[0] // lats
    maps = [lane_map(v, width // levs) for v in range(levs)]
    spare = spare_lanes((lats, LANES), width)
    for m in range(OWN):
        weighted = jnp.concatenate(
            [
                jnp.concatenate(
                    [
                        sums_ref[m, part, lat * lat_slots : lat * lat_slots + lat_local, :]
                        for lat in range(lats)
                    ]
                    + [jnp.zeros((lanes - lats * lat_local, LANES), f32)]
                )
                for part in range(2)
            ],
            axis=1,
        ).astype(bf16)
        forcing = dot(table_ref[m], weighted).astype(bf16)
        for v in range(levs):
            full_ref[...] = dot(forcing, maps[v])
            for b in range(sent // 8):
                last = full_ref[pl.ds(sent + b, lats, rows), :]
                for t in range(8):
                    main = full_ref[pl.ds(8 * b + t, lats, rows), :]
                    sent_ref[pl.ds(8 * b + t, lats, sent), :] = jnp.where(
                        spare, scatter_last(last, t, width), main
                    )
            for q in range(lats):
                k, x = divmod(q, LAT_X)
                piece = sent_ref[q * sent : (q + 1) * sent, :].astype(bf16)
                out_ref[x * Z_LOW + class_ref[k], v, m] = piece


def forward(classes, weighted, table, peers, lats, levs, sent, lat_local, lat_slots, width):
    vmem = pl.BlockSpec(memory_space=pltpu.VMEM)
    return pl.pallas_call(
        functools.partial(
            forward_kernel, lats=lats, lat_local=lat_local, lat_slots=lat_slots, width=width
        ),
        in_specs=[pl.BlockSpec(memory_space=pltpu.SMEM), vmem, vmem],
        out_specs=vmem,
        out_shape=jax.ShapeDtypeStruct((lats, levs, OWN, sent, LANES), bf16),
        scratch_shapes=[
            pltpu.VMEM((OWN, 2, lats * lat_slots, LANES), f32),
            pltpu.VMEM((2, peers * 8, LANES), f32),
            pltpu.VMEM((lats * sent, LANES), f32),
            pltpu.VMEM((table.shape[1], LANES), f32),
        ],
        compiler_params=pltpu.CompilerParams(vmem_limit_bytes=24 * 2**20),
        name="forward",
    )(classes, weighted, table)


def turn_maps(channels):
    maps = np.zeros((8, 2 * channels, LANES), np.float32)
    for t in range(8):
        maps[t, np.arange(channels), np.arange(channels)] = 1.0
        piece = np.arange(SPARE)
        maps[t, channels + SPARE * t + piece, channels + piece] = 1.0
    return jnp.asarray(maps, bf16)


def update_kernel(at_ref, damping_ref, state_ref, forcing_ref, maps_ref, out_ref, scr_ref):
    degrees, channels, orders = state_ref.shape
    order = lax.broadcasted_iota(jnp.int32, (channels, orders), 1) + at_ref[0]

    def put(degree, forcing):
        new = (state_ref[degree] + time_step * forcing) * damping_ref[degree]
        out_ref[degree] = jnp.where(degree + at_ref[1] >= order, new, 0.0)

    sent = forcing_ref.shape[2]
    for b in range(sent // 8):
        for x in range(LAT_X):
            skip = OWN * (first_group(x - 1) + Z_RING - first_group(x)) if x else 0
            first = (OWN * first_group(x) + skip) * 8
            mine = forcing_ref[x, skip:, 8 * b : 8 * b + 8, :].astype(f32)
            scr_ref[b, first : first + mine.shape[0] * 8, :] = mine.reshape(-1, LANES)
        last = 0.0
        for t in range(8):
            turned = lax.dot_general(
                maps_ref[t],
                scr_ref[b, pl.ds(t, orders, 8), :].astype(bf16),
                (((1,), (1,)), ((), ())),
                preferred_element_type=f32,
            )
            put(8 * b + t, turned[:channels])
            last += turned[channels:]
        put(sent + b, last)


def update(at, damping, state, forcing):
    degrees, channels, orders = state.shape
    _, _, sent, _ = forcing.shape
    smem, vmem = (pl.BlockSpec(memory_space=m) for m in (pltpu.SMEM, pltpu.VMEM))
    return pl.pallas_call(
        update_kernel,
        in_specs=[smem, smem, vmem, vmem, vmem],
        out_specs=vmem,
        out_shape=jax.ShapeDtypeStruct(state.shape, f32),
        scratch_shapes=[pltpu.VMEM((sent // 8, orders * 8, LANES), f32)],
        compiler_params=pltpu.CompilerParams(vmem_limit_bytes=24 * 2**20),
        name="update",
    )(at, damping, state, forcing, turn_maps(channels))


def along_z(value, step):
    pairs = []
    flat = lambda x, z: x * Z_RING + 2 * (z % Z_LOW) + z // Z_LOW
    for x in range(LAT_X):
        pairs += [(flat(x, z), flat(x, (z + step) % Z_RING)) for z in range(Z_RING)]
    return lax.ppermute(value, ("lat", "lev"), pairs)


def along_x(value):
    groups = [[x * Z_LOW + z for x in range(LAT_X)] for z in range(Z_LOW)]
    return lax.all_to_all(value, "lat", 0, 0, axis_index_groups=groups, tiled=True)


def on_device(spectral_state, legendre, quad_weight, weight_in, bias_in, weight_hidden, weight_out):
    ord_size, lat_size, lev_size = (lax.axis_size(a) for a in ("ord", "lat", "lev"))
    ord_at, lat_at, lev_at = (lax.axis_index(a) for a in ("ord", "lat", "lev"))
    order_local, degree_local = spectral_state.shape[:2]
    lat_local = quad_weight.shape[0]
    row_local = spectral_state.shape[2] * spectral_state.shape[3]
    channels = 2 * row_local
    width = lev_size * row_local
    rows = -(-degree_local // 16) * 16
    sent = degree_local // 8 * 8
    peers = ord_size * lat_size * lev_size
    lat_slots = ord_size * lev_size * OWN
    everyone = ("lat", "ord", "lev")
    at = jnp.stack([ord_at * order_local, lat_at * degree_local]).astype(jnp.int32)
    state = spectral_state.transpose(1, 2, 3, 4, 0).reshape(degree_local, channels, order_local)

    z_at = lev_at * Z_LOW + lat_at % Z_LOW
    a_all, b_own, *b_rest = pack_table(z_at[None], legendre, HALF, rows)
    b_left, b_right, b_low, b_high = (along_z(v, k) for v, k in zip(b_rest, (1, -1, 2, -2)))
    a_all = along_x(a_all)
    a_cut = [a_all[:, 1], a_all[:, 2], a_all[:, 3, :, : rows // 2], a_all[:, 3, :, rows // 2 :]]
    a_cut, b_left, b_right, b_low, b_high = lax.optimization_barrier(
        (a_cut, b_left, b_right, b_low, b_high)
    )
    b_far = jnp.concatenate([b_low, b_high], axis=2)
    b_all = jnp.stack([b_own, b_left, b_right, b_far], axis=1)
    coefficients = prep(at, state, sent)
    a_cut, b_all, coefficients = lax.optimization_barrier((a_cut, b_all, coefficients))
    a_near = [along_z(a_cut[0], 1), along_z(a_cut[1], -1)]
    a_far = [along_z(a_cut[2], 2), along_z(a_cut[3], -2)]
    b_all = along_x(b_all)

    slot = lax.iota(jnp.int32, OWN * peers)
    slot_lev = slot % lev_size
    slot_ord = slot // lev_size % ord_size
    slot_lat = slot // (lev_size * ord_size) % lat_size
    slot_x, slot_w = slot_lat // Z_LOW, 2 * (slot_lat % Z_LOW) + slot_lev
    valid = (slot_x % 2 == 0) | (slot_w > 0)
    order_ids = slot_ord * order_local + OWN * (first_group(slot_x) + slot_w) + slot // peers
    coefficients, a_near, a_far, b_all, order_ids, valid = lax.optimization_barrier(
        (coefficients, a_near, a_far, b_all, order_ids, valid)
    )

    coefficients = coefficients.reshape(lat_size * lev_size, OWN, sent, LANES)
    coefficients = lax.all_to_all(coefficients, ("lat", "lev"), 0, 0, tiled=True)
    coefficients = coefficients.reshape(lat_size, lev_size, OWN, sent, LANES)
    classes = (z_at + jnp.array([0, -1, 1, 2], jnp.int32)) % Z_LOW
    table = assemble(a_all, a_near, a_far, b_all)

    first = (ord_at * lev_size + lev_at) * OWN
    weights = lax.dynamic_slice_in_dim(jnp.pad(quad_weight, (0, lat_slots - lat_local)), first, OWN)
    w_in = jnp.pad(weight_in, ((0, LANES - width), (0, 0)))
    w_out = jnp.pad(weight_out, ((0, 0), (0, LANES - width)))
    degree_ids = lat_at * degree_local + lax.iota(jnp.int32, degree_local)
    degree_ratio = (degree_ids * (degree_ids + 1)).astype(f32) / ((L - 1) * L)
    damping = 1.0 / (1.0 + hyper_rate * degree_ratio * degree_ratio)
    cosines, sines = lookup_of(order_ids, valid)
    table, coefficients, cosines, sines, weights, w_in, w_out, damping = lax.optimization_barrier(
        (table, coefficients, cosines, sines, weights, w_in, w_out, damping)
    )
    fourier = inverse(classes, table, coefficients, peers, lat_local, lat_slots, width)

    fourier = lax.all_to_all(fourier.reshape(peers, 8, -1), everyone, 0, 0, tiled=True)
    weighted = columns(
        weights,
        fourier.reshape(peers * 8, -1),
        cosines,
        sines,
        w_in,
        bias_in[None, :],
        weight_hidden,
        w_out,
        width,
    )

    weighted = lax.all_to_all(weighted.reshape(peers, 8, -1), everyone, 0, 0, tiled=True)
    weighted = weighted.reshape(peers * 8, -1)
    forcing = forward(
        classes, weighted, table, peers, lat_size, lev_size, sent, lat_local, lat_slots, width
    )
    forcing = forcing.reshape(lat_size * lev_size, OWN, sent, LANES)
    forcing = lax.all_to_all(forcing, ("lat", "lev"), 0, 0, tiled=True)
    forcing = forcing.reshape(LAT_X, OWN * Z_RING, sent, LANES)
    updated = update(at, damping, state, forcing)
    updated = updated.reshape(degree_local, *spectral_state.shape[2:], order_local)
    return updated.transpose(4, 0, 1, 2, 3)


def solution(mesh):
    return jax.shard_map(
        on_device,
        mesh=mesh,
        in_specs=(
            P("ord", "lat", "lev", None, None),
            P("ord", "lat", None),
            P("lat"),
            P(),
            P(),
            P(),
            P(),
        ),
        out_specs=P("ord", "lat", "lev", None, None),
        check_vma=False,
    )
```

```python
import functools
import math

import jax
import jax.numpy as jnp
import numpy as np
from jax import lax
from jax.experimental import pallas as pl
from jax.experimental.pallas import tpu as pltpu
from jax.sharding import PartitionSpec as P

L = 720
NLON = 1440
OWN = 3
LANES = 128
LAT_X, Z_LOW, Z_RING = 4, 4, 8
HALF = 384
X_ROWS = 1440
SPARE = 14

time_step = 1.0
hyper_rate = 2.0
transform_scale = math.sqrt(2.0 / NLON)

f32, bf16 = jnp.float32, jnp.bfloat16
dot = functools.partial(jnp.dot, preferred_element_type=jnp.float32)


def first_group(x):
    return (22 * x + 1) // 3


def lookup_of(order_ids, valid):
    low = 32

    def waves(x):
        phase_index = order_ids[None, :] * x[:, None] % NLON
        angles = 2.0 * math.pi / NLON * phase_index.astype(f32)
        return jnp.cos(angles), jnp.sin(angles)

    high_cos, high_sin = waves(low * lax.iota(jnp.int32, NLON // low))
    high_cos = jnp.where(valid[None, :], high_cos, 0.0)[:, None]
    high_sin = jnp.where(valid[None, :], high_sin, 0.0)[:, None]
    low_cos, low_sin = (w[None] for w in waves(lax.iota(jnp.int32, low)))
    cosines = high_cos * low_cos - high_sin * low_sin
    sines = -(high_sin * low_cos + high_cos * low_sin)
    shape = (NLON, order_ids.shape[0])
    return cosines.astype(bf16).reshape(shape), sines.astype(bf16).reshape(shape)


def half_silu(u):
    return u + u * jnp.tanh(u)


def lane_map(lev, row_local):
    wide_lane = lax.broadcasted_iota(jnp.int32, (2 * LANES, LANES), 0)
    lane = lax.broadcasted_iota(jnp.int32, (2 * LANES, LANES), 1)
    part = (wide_lane >= LANES).astype(jnp.int32)
    row = wide_lane - LANES * part - lev * row_local
    hit = (row >= 0) & (row < row_local) & (lane == 2 * row + part)
    return jnp.where(hit, 1.0, 0.0).astype(bf16)


def pack_rows(slab_of, out_ref, scr_ref, peers, width):
    lane = lax.broadcasted_iota(jnp.int32, (peers, LANES), 1)
    spare = (lane >= width) & (lane < width + SPARE)
    for part in range(2):
        last = slab_of(part, 2, 2)
        for k in range(8):
            moved = pltpu.roll(last, (width - SPARE * k) % LANES, 1)
            scr_ref[part, pl.ds(k, peers, 8), :] = jnp.where(
                spare, moved, slab_of(part, k // OWN, k % OWN)
            )
        out_ref[:, part * LANES : (part + 1) * LANES] = scr_ref[part].astype(bf16)


def unpack_rows(in_ref, scr_ref, put_slab, peers, width):
    lane = lax.broadcasted_iota(jnp.int32, (peers, LANES), 1)
    for part in range(2):
        scr_ref[part] = in_ref[:, part * LANES : (part + 1) * LANES].astype(f32)
        last = jnp.zeros((peers, LANES), f32)
        for k in range(8):
            slab = scr_ref[part, pl.ds(k, peers, 8), :]
            put_slab(part, k // OWN, k % OWN, slab)
            moved = pltpu.roll(slab, (SPARE * k - width) % LANES, 1)
            last = jnp.where((lane >= SPARE * k) & (lane < SPARE * (k + 1)), moved, last)
        put_slab(part, 2, 2, last)


def spare_lanes(shape, width):
    lane = lax.broadcasted_iota(jnp.int32, shape, len(shape) - 1)
    return (lane >= width) & (lane < width + SPARE)


def scatter_last(row, t, width):
    return pltpu.roll(row, (width - SPARE * t) % LANES, 1)


def gather_last(last, slab, t, width):
    lane = lax.broadcasted_iota(jnp.int32, slab.shape, 1)
    moved = pltpu.roll(slab, (SPARE * t - width) % LANES, 1)
    return jnp.where((lane >= SPARE * t) & (lane < SPARE * (t + 1)), moved, last)


def wide(value):
    return jnp.pad(value, ((0, 0), (0, LANES - value.shape[1])))


def prep_kernel(at_ref, state_ref, last_ref, out_ref, scr_ref):
    _, channels, orders = state_ref.shape
    group, rows = out_ref.shape[1], 8 * pl.num_programs(0)
    b = pl.program_id(0)
    order = lax.broadcasted_iota(jnp.int32, (channels, orders), 1) + at_ref[0]
    masked = lambda value, degree: wide(jnp.where(degree + at_ref[1] >= order, value, 0.0).T)
    last = masked(last_ref[b], rows + b)
    spare = spare_lanes(last.shape, channels)
    for t in range(8):
        scr_ref[pl.ds(t, orders, 8), :] = jnp.where(
            spare, scatter_last(last, t, channels), masked(state_ref[t], 8 * b + t)
        )
    packed = scr_ref[...].astype(bf16).reshape(orders, 8, LANES)
    for x in range(LAT_X):
        first = OWN * first_group(x)
        out_ref[x] = packed[first : first + group]


def prep(at, state, rows):
    group = OWN * Z_RING
    _, channels, orders = state.shape
    steps = rows // 8
    return pl.pallas_call(
        prep_kernel,
        grid=(steps,),
        in_specs=[
            pl.BlockSpec(memory_space=pltpu.SMEM),
            pl.BlockSpec((8, channels, orders), lambda i: (i, 0, 0)),
            pl.BlockSpec((8, channels, orders), lambda i: (steps, 0, 0)),
        ],
        out_specs=pl.BlockSpec((LAT_X, group, 8, LANES), lambda i: (0, 0, i, 0)),
        out_shape=jax.ShapeDtypeStruct((LAT_X, group, rows, LANES), bf16),
        scratch_shapes=[pltpu.VMEM((orders * 8, LANES), f32)],
        cost_estimate=pl.CostEstimate(flops=10**6, bytes_accessed=4 * 10**6, transcendentals=0),
        name="prep",
    )(at, state, state)


def pack_kernel(z_ref, in_ref, a_ref, *b_refs):
    degrees, lats = in_ref.shape[1:]
    half, rows = a_ref.shape[-1], a_ref.shape[-2]
    split = rows // 2
    ring = [lax.rem(z_ref[0] + (Z_RING + step), Z_RING) for step in (0, 1, -1, 2, -2)]
    own = [OWN * (2 * lax.rem(z, Z_LOW) + lax.div(z, Z_LOW)) for z in ring]
    a_ref[...] = jnp.zeros_like(a_ref)
    for ref in b_refs:
        ref[...] = jnp.zeros_like(ref)
    for k in range(3):
        mine = in_ref[pl.ds(own[k], OWN)]
        a_ref[0, k, :, :degrees, :] = mine[:, :, :half]
        b_refs[k][0, :, :degrees, : lats - half] = mine[:, :, half:]
    mine = in_ref[pl.ds(own[3], OWN)]
    a_ref[0, 3, :, :split, :] = mine[:, :split, :half]
    b_refs[3][0, :, :, : lats - half] = mine[:, :split, half:]
    mine = in_ref[pl.ds(own[4], OWN)]
    a_ref[0, 3, :, split:degrees, :] = mine[:, split:, :half]
    b_refs[4][0, :, : degrees - split, : lats - half] = mine[:, split:, half:]


def pack_table(z_at, legendre, half, rows):
    _, degrees, lats = legendre.shape
    group = OWN * Z_RING
    b_shape = lambda r: jax.ShapeDtypeStruct((LAT_X, OWN, r, half), bf16)
    b_spec = lambda r: pl.BlockSpec((1, OWN, r, half), lambda x: (x, 0, 0, 0))
    b_rows = (rows, rows, rows, rows // 2, rows // 2)
    return pl.pallas_call(
        pack_kernel,
        grid=(LAT_X,),
        in_specs=[
            pl.BlockSpec(memory_space=pltpu.SMEM),
            pl.BlockSpec(
                (pl.Element(group), pl.Element(degrees), pl.Element(lats)),
                lambda x: (OWN * first_group(x), 0, 0),
            ),
        ],
        out_specs=[pl.BlockSpec((1, 4, OWN, rows, half), lambda x: (x, 0, 0, 0, 0))]
        + [b_spec(r) for r in b_rows],
        out_shape=[jax.ShapeDtypeStruct((LAT_X, 4, OWN, rows, half), bf16)]
        + [b_shape(r) for r in b_rows],
        compiler_params=pltpu.CompilerParams(vmem_limit_bytes=60 * 2**20),
        name="pack_table",
    )(z_at, legendre)


def assemble_kernel(a_own_ref, a_left_ref, a_right_ref, a_low_ref, a_high_ref, b_ref, out_ref):
    rows, half = b_ref.shape[-2:]
    place = LAT_X * rows
    far = jnp.concatenate([a_low_ref[...], a_high_ref[...]], axis=1)
    for k, piece in enumerate((a_own_ref[:, 0], a_left_ref[...], a_right_ref[...], far)):
        out_ref[0, k * place : (k + 1) * place, :half] = piece.reshape(place, half)
        out_ref[0, k * place : (k + 1) * place, half:] = b_ref[:, k].reshape(place, half)


def assemble(a_own, a_near, a_far, b_all):
    rows, half = b_all.shape[-2:]
    size = 4 * LAT_X * rows
    near = pl.BlockSpec((LAT_X, None, rows, half), lambda m: (0, m, 0, 0))
    far = pl.BlockSpec((LAT_X, None, rows // 2, half), lambda m: (0, m, 0, 0))
    return pl.pallas_call(
        assemble_kernel,
        grid=(OWN,),
        in_specs=[
            pl.BlockSpec((LAT_X, 1, None, rows, half), lambda m: (0, 0, m, 0, 0)),
            near,
            near,
            far,
            far,
            pl.BlockSpec((LAT_X, 4, None, rows, half), lambda m: (0, 0, m, 0, 0)),
        ],
        out_specs=pl.BlockSpec((1, size, 2 * half), lambda m: (m, 0, 0)),
        out_shape=jax.ShapeDtypeStruct((OWN, size, 2 * half), bf16),
        cost_estimate=pl.CostEstimate(flops=10**6, bytes_accessed=8 * 10**6, transcendentals=0),
        name="assemble",
    )(a_own, *a_near, *a_far, b_all)


def inverse_kernel(
    class_ref, table_ref, coef_ref, out_ref, sums_ref, scr_ref, sent_ref, full_ref,
    *, lats, lat_local, lat_slots, width,
):
    levs, _, sent, _ = coef_ref.shape[1:]
    rows = full_ref.shape[0] // lats
    maps = [lane_map(v, width // levs) for v in range(levs)]
    for m in range(OWN):
        swapped = 0.0
        for v in range(levs):
            for q in range(lats):
                k, x = divmod(q, LAT_X)
                piece = coef_ref[x * Z_LOW + class_ref[k], v, m].astype(f32)
                sent_ref[q * sent : (q + 1) * sent, :] = piece
                full_ref[q * rows : q * rows + sent, :] = piece
                full_ref[q * rows + sent : (q + 1) * rows, :] = jnp.zeros((rows - sent, LANES), f32)
            for b in range(sent // 8):
                last = jnp.zeros((lats, LANES), f32)
                for t in range(8):
                    slab = sent_ref[pl.ds(8 * b + t, lats, sent), :]
                    last = gather_last(last, slab, t, width)
                full_ref[pl.ds(sent + b, lats, rows), :] = last
            swapped += lax.dot_general(
                maps[v],
                full_ref[...].astype(bf16),
                (((1,), (1,)), ((), ())),
                preferred_element_type=f32,
            )
        sums = dot(swapped.astype(bf16), table_ref[m]).T
        for part in range(2):
            lanes = slice(part * LANES, (part + 1) * LANES)
            for lat in range(lats):
                first = lat * lat_slots
                sums_ref[m, part, first : first + lat_local, :] = sums[
                    lat * lat_local : (lat + 1) * lat_local, lanes
                ]
                sums_ref[m, part, first + lat_local : first + lat_slots, :] = jnp.zeros(
                    (lat_slots - lat_local, LANES), f32
                )

    peers = out_ref.shape[0] // 8
    slab_of = lambda part, i, m: sums_ref[m, part, pl.ds(i, peers, OWN), :]
    pack_rows(slab_of, out_ref, scr_ref, peers, width)


def inverse(classes, table, coef, peers, lat_local, lat_slots, width):
    lats, _, _, sent, _ = coef.shape
    vmem = pl.BlockSpec(memory_space=pltpu.VMEM)
    return pl.pallas_call(
        functools.partial(
            inverse_kernel, lats=lats, lat_local=lat_local, lat_slots=lat_slots, width=width
        ),
        in_specs=[pl.BlockSpec(memory_space=pltpu.SMEM), vmem, vmem],
        out_specs=vmem,
        out_shape=jax.ShapeDtypeStruct((peers * 8, 2 * LANES), bf16),
        scratch_shapes=[
            pltpu.VMEM((OWN, 2, lats * lat_slots, LANES), f32),
            pltpu.VMEM((2, peers * 8, LANES), f32),
            pltpu.VMEM((lats * sent, LANES), f32),
            pltpu.VMEM((table.shape[1], LANES), f32),
        ],
        compiler_params=pltpu.CompilerParams(vmem_limit_bytes=24 * 2**20),
        name="inverse",
    )(classes, table, coef)


def column_kernel(
    weight_ref, in_ref, cos_ref, sin_ref, w_in_ref, bias_ref, w_hid_ref, w_out_ref,
    out_ref, fourier_ref, tendency_ref, sums_ref, scr_ref, *, x_rows, width,
):
    peers = in_ref.shape[0] // 8

    def put(part, i, m, slab):
        fourier_ref[part, m * peers : (m + 1) * peers, i * LANES : (i + 1) * LANES] = slab.astype(
            bf16
        )

    unpack_rows(in_ref, scr_ref, put, peers, width)

    half_in, half_bias = 0.5 * w_in_ref[...], 0.5 * bias_ref[...]
    half_hid = [0.5 * w_hid_ref[layer] for layer in range(w_hid_ref.shape[0])]

    def grid_rows(step, carry):
        rows = pl.ds(pl.multiple_of(step * x_rows, x_rows), x_rows)
        raw = dot(cos_ref[rows, :], fourier_ref[0]) + dot(sin_ref[rows, :], fourier_ref[1])
        features = (transform_scale * raw).astype(bf16)
        lanes = [slice(i * LANES, (i + 1) * LANES) for i in range(OWN)]
        hidden = [half_silu(dot(features[:, at], half_in) + half_bias) for at in lanes]
        hidden = [h.astype(bf16) for h in hidden]
        for weights in half_hid:
            update = [half_silu(dot(h, weights)) for h in hidden]
            hidden = [(h.astype(f32) + u).astype(bf16) for h, u in zip(hidden, update)]
        for at, h in zip(lanes, hidden):
            tendency_ref[rows, at] = dot(h, w_out_ref[...]).astype(bf16)
        return carry

    lax.fori_loop(0, NLON // x_rows, grid_rows, 0)

    for part, table_ref in enumerate((cos_ref, sin_ref)):
        sums = lax.dot_general(
            tendency_ref[...],
            table_ref[...],
            (((0,), (0,)), ((), ())),
            preferred_element_type=f32,
        )
        for i in range(OWN):
            weight = weight_ref[i] * transform_scale
            for m in range(OWN):
                block = sums[i * LANES : (i + 1) * LANES, m * peers : (m + 1) * peers]
                sums_ref[part, i, m] = weight * block.T

    slab_of = lambda part, i, m: sums_ref[part, i, m]
    pack_rows(slab_of, out_ref, scr_ref, peers, width)


def columns(weights, fourier, cosines, sines, w_in, bias, w_hid, w_out, width):
    peers = fourier.shape[0] // 8
    vmem = pl.BlockSpec(memory_space=pltpu.VMEM)
    return pl.pallas_call(
        functools.partial(column_kernel, x_rows=X_ROWS, width=width),
        in_specs=[pl.BlockSpec(memory_space=pltpu.SMEM)] + [vmem] * 7,
        out_specs=vmem,
        out_shape=jax.ShapeDtypeStruct(fourier.shape, bf16),
        scratch_shapes=[
            pltpu.VMEM((2, OWN * peers, OWN * LANES), bf16),
            pltpu.VMEM((NLON, OWN * LANES), bf16),
            pltpu.VMEM((2, OWN, OWN, peers, LANES), f32),
            pltpu.VMEM((2, peers * 8, LANES), f32),
        ],
        compiler_params=pltpu.CompilerParams(vmem_limit_bytes=26 * 2**20),
        name="columns",
    )(weights, fourier, cosines, sines, w_in, bias, w_hid, w_out)


def forward_kernel(
    class_ref, in_ref, table_ref, out_ref, sums_ref, scr_ref, sent_ref, full_ref,
    *, lats, lat_local, lat_slots, width,
):
    peers = in_ref.shape[0] // 8

    def put(part, i, m, slab):
        sums_ref[m, part, pl.ds(i, peers, OWN), :] = slab

    unpack_rows(in_ref, scr_ref, put, peers, width)
    lanes = table_ref.shape[-1]
    levs, _, sent, _ = out_ref.shape[1:]
    rows = full_ref.shape[0] // lats
    maps = [lane_map(v, width // levs) for v in range(levs)]
    spare = spare_lanes((lats, LANES), width)
    for m in range(OWN):
        weighted = jnp.concatenate(
            [
                jnp.concatenate(
                    [
                        sums_ref[m, part, lat * lat_slots : lat * lat_slots + lat_local, :]
                        for lat in range(lats)
                    ]
                    + [jnp.zeros((lanes - lats * lat_local, LANES), f32)]
                )
                for part in range(2)
            ],
            axis=1,
        ).astype(bf16)
        forcing = dot(table_ref[m], weighted).astype(bf16)
        for v in range(levs):
            full_ref[...] = dot(forcing, maps[v])
            for b in range(sent // 8):
                last = full_ref[pl.ds(sent + b, lats, rows), :]
                for t in range(8):
                    main = full_ref[pl.ds(8 * b + t, lats, rows), :]
                    sent_ref[pl.ds(8 * b + t, lats, sent), :] = jnp.where(
                        spare, scatter_last(last, t, width), main
                    )
            for q in range(lats):
                k, x = divmod(q, LAT_X)
                piece = sent_ref[q * sent : (q + 1) * sent, :].astype(bf16)
                out_ref[x * Z_LOW + class_ref[k], v, m] = piece


def forward(classes, weighted, table, peers, lats, levs, sent, lat_local, lat_slots, width):
    vmem = pl.BlockSpec(memory_space=pltpu.VMEM)
    return pl.pallas_call(
        functools.partial(
            forward_kernel, lats=lats, lat_local=lat_local, lat_slots=lat_slots, width=width
        ),
        in_specs=[pl.BlockSpec(memory_space=pltpu.SMEM), vmem, vmem],
        out_specs=vmem,
        out_shape=jax.ShapeDtypeStruct((lats, levs, OWN, sent, LANES), bf16),
        scratch_shapes=[
            pltpu.VMEM((OWN, 2, lats * lat_slots, LANES), f32),
            pltpu.VMEM((2, peers * 8, LANES), f32),
            pltpu.VMEM((lats * sent, LANES), f32),
            pltpu.VMEM((table.shape[1], LANES), f32),
        ],
        compiler_params=pltpu.CompilerParams(vmem_limit_bytes=24 * 2**20),
        name="forward",
    )(classes, weighted, table)


def turn_maps(channels):
    maps = np.zeros((8, 2 * channels, LANES), np.float32)
    for t in range(8):
        maps[t, np.arange(channels), np.arange(channels)] = 1.0
        piece = np.arange(SPARE)
        maps[t, channels + SPARE * t + piece, channels + piece] = 1.0
    return jnp.asarray(maps, bf16)


def update_kernel(at_ref, damping_ref, state_ref, forcing_ref, maps_ref, out_ref, scr_ref):
    degrees, channels, orders = state_ref.shape
    order = lax.broadcasted_iota(jnp.int32, (channels, orders), 1) + at_ref[0]

    def put(degree, forcing):
        new = (state_ref[degree] + time_step * forcing) * damping_ref[degree]
        out_ref[degree] = jnp.where(degree + at_ref[1] >= order, new, 0.0)

    sent = forcing_ref.shape[2]
    for b in range(sent // 8):
        for x in range(LAT_X):
            skip = OWN * (first_group(x - 1) + Z_RING - first_group(x)) if x else 0
            first = (OWN * first_group(x) + skip) * 8
            mine = forcing_ref[x, skip:, 8 * b : 8 * b + 8, :].astype(f32)
            scr_ref[b, first : first + mine.shape[0] * 8, :] = mine.reshape(-1, LANES)
        last = 0.0
        for t in range(8):
            turned = lax.dot_general(
                maps_ref[t],
                scr_ref[b, pl.ds(t, orders, 8), :].astype(bf16),
                (((1,), (1,)), ((), ())),
                preferred_element_type=f32,
            )
            put(8 * b + t, turned[:channels])
            last += turned[channels:]
        put(sent + b, last)


def update(at, damping, state, forcing):
    degrees, channels, orders = state.shape
    _, _, sent, _ = forcing.shape
    smem, vmem = (pl.BlockSpec(memory_space=m) for m in (pltpu.SMEM, pltpu.VMEM))
    return pl.pallas_call(
        update_kernel,
        in_specs=[smem, smem, vmem, vmem, vmem],
        out_specs=vmem,
        out_shape=jax.ShapeDtypeStruct(state.shape, f32),
        scratch_shapes=[pltpu.VMEM((sent // 8, orders * 8, LANES), f32)],
        compiler_params=pltpu.CompilerParams(vmem_limit_bytes=24 * 2**20),
        name="update",
    )(at, damping, state, forcing, turn_maps(channels))


def along_z(value, step):
    pairs = []
    flat = lambda x, z: x * Z_RING + 2 * (z % Z_LOW) + z // Z_LOW
    for x in range(LAT_X):
        pairs += [(flat(x, z), flat(x, (z + step) % Z_RING)) for z in range(Z_RING)]
    return lax.ppermute(value, ("lat", "lev"), pairs)


def along_x(value):
    groups = [[x * Z_LOW + z for x in range(LAT_X)] for z in range(Z_LOW)]
    return lax.all_to_all(value, "lat", 0, 0, axis_index_groups=groups, tiled=True)


def on_device(spectral_state, legendre, quad_weight, weight_in, bias_in, weight_hidden, weight_out):
    ord_size, lat_size, lev_size = (lax.axis_size(a) for a in ("ord", "lat", "lev"))
    ord_at, lat_at, lev_at = (lax.axis_index(a) for a in ("ord", "lat", "lev"))
    order_local, degree_local = spectral_state.shape[:2]
    lat_local = quad_weight.shape[0]
    row_local = spectral_state.shape[2] * spectral_state.shape[3]
    channels = 2 * row_local
    width = lev_size * row_local
    rows = -(-degree_local // 16) * 16
    sent = degree_local // 8 * 8
    peers = ord_size * lat_size * lev_size
    lat_slots = ord_size * lev_size * OWN
    everyone = ("lat", "ord", "lev")
    at = jnp.stack([ord_at * order_local, lat_at * degree_local]).astype(jnp.int32)
    state = spectral_state.transpose(1, 2, 3, 4, 0).reshape(degree_local, channels, order_local)

    z_at = lev_at * Z_LOW + lat_at % Z_LOW
    a_all, b_own, *b_rest = pack_table(z_at[None], legendre, HALF, rows)
    b_left, b_right, b_low, b_high = (along_z(v, k) for v, k in zip(b_rest, (1, -1, 2, -2)))
    a_all = along_x(a_all)
    b_far = jnp.concatenate([b_low, b_high], axis=2)
    b_all = jnp.stack([b_own, b_left, b_right, b_far], axis=1)
    a_cut = [a_all[:, 1], a_all[:, 2], a_all[:, 3, :, : rows // 2], a_all[:, 3, :, rows // 2 :]]
    coefficients = prep(at, state, sent)
    a_cut, b_all, coefficients = lax.optimization_barrier((a_cut, b_all, coefficients))
    a_near = [along_z(a_cut[0], 1), along_z(a_cut[1], -1)]
    a_far = [along_z(a_cut[2], 2), along_z(a_cut[3], -2)]
    b_all = along_x(b_all)

    slot = lax.iota(jnp.int32, OWN * peers)
    slot_lev = slot % lev_size
    slot_ord = slot // lev_size % ord_size
    slot_lat = slot // (lev_size * ord_size) % lat_size
    slot_x, slot_w = slot_lat // Z_LOW, 2 * (slot_lat % Z_LOW) + slot_lev
    valid = (slot_x % 2 == 0) | (slot_w > 0)
    order_ids = slot_ord * order_local + OWN * (first_group(slot_x) + slot_w) + slot // peers
    coefficients, a_near, a_far, b_all, order_ids, valid = lax.optimization_barrier(
        (coefficients, a_near, a_far, b_all, order_ids, valid)
    )

    coefficients = coefficients.reshape(lat_size * lev_size, OWN, sent, LANES)
    coefficients = lax.all_to_all(coefficients, ("lat", "lev"), 0, 0, tiled=True)
    coefficients = coefficients.reshape(lat_size, lev_size, OWN, sent, LANES)
    classes = (z_at + jnp.array([0, -1, 1, 2], jnp.int32)) % Z_LOW
    table = assemble(a_all, a_near, a_far, b_all)

    first = (ord_at * lev_size + lev_at) * OWN
    weights = lax.dynamic_slice_in_dim(jnp.pad(quad_weight, (0, lat_slots - lat_local)), first, OWN)
    w_in = jnp.pad(weight_in, ((0, LANES - width), (0, 0)))
    w_out = jnp.pad(weight_out, ((0, 0), (0, LANES - width)))
    degree_ids = lat_at * degree_local + lax.iota(jnp.int32, degree_local)
    degree_ratio = (degree_ids * (degree_ids + 1)).astype(f32) / ((L - 1) * L)
    damping = 1.0 / (1.0 + hyper_rate * degree_ratio * degree_ratio)
    cosines, sines = lookup_of(order_ids, valid)
    table, coefficients, cosines, sines, weights, w_in, w_out, damping = lax.optimization_barrier(
        (table, coefficients, cosines, sines, weights, w_in, w_out, damping)
    )
    fourier = inverse(classes, table, coefficients, peers, lat_local, lat_slots, width)

    fourier = lax.all_to_all(fourier.reshape(peers, 8, -1), everyone, 0, 0, tiled=True)
    weighted = columns(
        weights,
        fourier.reshape(peers * 8, -1),
        cosines,
        sines,
        w_in,
        bias_in[None, :],
        weight_hidden,
        w_out,
        width,
    )

    weighted = lax.all_to_all(weighted.reshape(peers, 8, -1), everyone, 0, 0, tiled=True)
    weighted = weighted.reshape(peers * 8, -1)
    forcing = forward(
        classes, weighted, table, peers, lat_size, lev_size, sent, lat_local, lat_slots, width
    )
    forcing = forcing.reshape(lat_size * lev_size, OWN, sent, LANES)
    forcing = lax.all_to_all(forcing, ("lat", "lev"), 0, 0, tiled=True)
    forcing = forcing.reshape(LAT_X, OWN * Z_RING, sent, LANES)
    updated = update(at, damping, state, forcing)
    updated = updated.reshape(degree_local, *spectral_state.shape[2:], order_local)
    return updated.transpose(4, 0, 1, 2, 3)


def solution(mesh):
    return jax.shard_map(
        on_device,
        mesh=mesh,
        in_specs=(
            P("ord", "lat", "lev", None, None),
            P("ord", "lat", None),
            P("lat"),
            P(),
            P(),
            P(),
            P(),
        ),
        out_specs=P("ord", "lat", "lev", None, None),
        check_vma=False,
    )
```
